32 devices in a mesh: dp: 2 (over x), row: 4 (over y, core), col: 4 (over z).
Axes of the slice: x: 2, y: 2, z: 4, core: 2. Of those that a mesh axis runs over, the one named last changes fastest.
Arguments:
- inputs: bfloat16 [2, 512, 4096], P('dp', 'col', 'row'), may hold values from -6 to 6
- weights: bfloat16 [4096, 3, 4096], P('row', None, 'col'), may hold values from -0.09375 to 0.09375
- feature_taps: float32 [3, 3, 4096], P(None, None, 'col'), may hold values from -2.5 to 2.5
- inner_taps: float32 [7, 4096], P(None, 'col'), may hold values from -2.5 to 2.5
- grad_out: bfloat16 [2, 512, 4096], P('dp', 'row', 'col'), may hold values from -6 to 6
Outputs:
- grad_in: bfloat16 [2, 512, 4096], P('dp', 'col', 'row')
- grad_weights: float32 [4096, 3, 4096], P('row', None, 'col')
The draws below stay inside these ranges and needn't reach their ends.
All inputs are finite; a program needn't handle non-finite values.
Results may differ from the reference program's by a relative error of at most 0.033.
Values may be sent and summed in bfloat16 or wider, within the bound.
No kernel may reach another device: no remote copies, remote signals or barrier semaphores. Data moves between devices by JAX's collectives and lax.ppermute only.
A program may use at most 128 MiB of HBM per device.

```python
import jax
import jax.numpy as jnp
from jax import lax

D = 4096
FEAT_TAPS = 3
TAPS = 7
TOKENS = 512
GROUPS = 2
N_ROW = 4
N_COL = 4


def block_scale(stream_key, extent, cuts, smallest, high):
    def one(axis_at, blocks):
        draws = jax.random.uniform(jax.random.fold_in(jax.random.fold_in(stream_key, 6), axis_at), (blocks,), jnp.float32, smallest / len(cuts), high / len(cuts))
        return jnp.repeat(jnp.exp(draws), extent[axis_at] // blocks).reshape((-1,) + (1,) * (len(extent) - axis_at - 1))

    loudness = one(*cuts[0])
    for cut in cuts[1:]:
        loudness = loudness * one(*cut)
    return loudness


def scatter_about(own_key, extent, deviation, limit, shards=(), kind=jnp.bfloat16):
    gain = block_scale(own_key, extent, shards, -0.22, 0.18) if shards else 1.0
    drawn = jax.random.normal(own_key, extent, jnp.float32) * deviation * gain
    return jnp.minimum(jnp.maximum(drawn, -limit), limit).astype(kind)


def setup_inputs(seed: int = 0) -> dict:
    key_list = jax.random.split(jax.random.key(seed), 6)
    inputs = scatter_about(key_list[0], (GROUPS, TOKENS, D), 1.0, 6.0, ((0, 2), (1, 4), (2, 4)))
    weights = scatter_about(key_list[1], (D, 3, D), D ** -0.5, 0.09375, ((0, 4), (2, 4)))
    feature_taps = scatter_about(key_list[2], (FEAT_TAPS, 3, D), 0.5, 2.5, ((2, 4),), jnp.float32)
    inner_taps = scatter_about(key_list[3], (TAPS, D), 0.35, 2.5, ((1, 4),), jnp.float32)
    grad_out = scatter_about(key_list[4], (GROUPS, TOKENS, D), 1.0, 6.0, ((0, 2), (1, 4), (2, 4)))
    return {"inputs": inputs, "weights": weights, "feature_taps": feature_taps, "inner_taps": inner_taps, "grad_out": grad_out}


def causal(seq, taps):
    total = taps[0] * seq
    for lag in range(1, taps.shape[0]):
        pad = jnp.zeros((lag,) + seq.shape[1:], jnp.float32)
        total = total + taps[lag] * jnp.concatenate([pad, seq[:-lag]], axis=0)
    return total


def anticausal(seq, taps):
    total = taps[0] * seq
    for lag in range(1, taps.shape[0]):
        pad = jnp.zeros((lag,) + seq.shape[1:], jnp.float32)
        total = total + taps[lag] * jnp.concatenate([seq[lag:], pad], axis=0)
    return total


def rounded(value):
    return lax.optimization_barrier(value.astype(jnp.bfloat16)).astype(jnp.float32)


def one_group(tokens, cotangent, weights, feature_taps, inner_taps):
    width_row = D // N_ROW
    width_col = D // N_COL
    flat_w = weights.reshape(D, 3 * D)

    def add_rows(total, index):
        block = lax.dynamic_slice_in_dim(tokens, index * width_row, width_row, 1)
        rows_w = lax.dynamic_slice_in_dim(flat_w, index * width_row, width_row, 0)
        return total + rounded(jnp.dot(block, rows_w, preferred_element_type=jnp.float32)), None

    proj_sum, unused = lax.scan(add_rows, jnp.zeros((TOKENS, 3 * D), jnp.float32), jnp.arange(N_ROW, dtype=jnp.int32))
    proj = rounded(proj_sum).reshape(TOKENS, 3, D)
    mixed = causal(proj, feature_taps)
    query = mixed[:, 0]
    key = mixed[:, 1]
    value = mixed[:, 2]
    product = rounded(key * value)
    inner = causal(product, inner_taps)
    upstream = cotangent.astype(jnp.float32)
    grad_query = upstream * inner
    grad_inner = upstream * query
    grad_product = anticausal(grad_inner, inner_taps)
    grad_mixed = jnp.stack([grad_query, grad_product * value, grad_product * key], axis=1)
    grad_proj = anticausal(grad_mixed, feature_taps).astype(jnp.bfloat16)

    def add_cols(total, index):
        block = lax.dynamic_slice_in_dim(grad_proj, index * width_col, width_col, 2).reshape(TOKENS, 3 * width_col)
        cols_w = lax.dynamic_slice_in_dim(weights, index * width_col, width_col, 2).reshape(D, 3 * width_col)
        part = lax.dot_general(block, cols_w, (((1,), (1,)), ((), ())), preferred_element_type=jnp.float32)
        return total + rounded(part), None

    grad_sum, unused = lax.scan(add_cols, jnp.zeros((TOKENS, D), jnp.float32), jnp.arange(N_COL, dtype=jnp.int32))
    grad_in = grad_sum.astype(jnp.bfloat16)
    grad_w = lax.dot_general(tokens, grad_proj.reshape(TOKENS, 3 * D), (((0,), (0,)), ((), ())), preferred_element_type=jnp.float32)
    return grad_in, grad_w


def reference(inputs, weights, feature_taps, inner_taps, grad_out):
    def step(total, pair):
        grad_in, grad_w = one_group(pair[0], pair[1], weights, feature_taps, inner_taps)
        return total + grad_w, grad_in

    total, grad_in = lax.scan(step, jnp.zeros((D, 3 * D), jnp.float32), (inputs, grad_out))
    return grad_in, total.reshape(D, 3, D)
```

```python
import functools

import jax
import jax.numpy as jnp
from jax import lax
from jax.experimental import pallas as pl
from jax.experimental.pallas import tpu as pltpu
from jax.sharding import PartitionSpec as P

LANES = 128
PAD = 8
CORES = 2


def shifted(shard, axis, by):
    length = lax.axis_size(axis)
    pairs = [(i, i + by) for i in range(length) if 0 <= i + by < length]
    return lax.ppermute(shard, axis, pairs)


def with_halo(cells, axis, width):
    head = shifted(cells[:width], axis, -1)
    tail = shifted(cells[-width:], axis, 1)
    return jnp.concatenate([tail, cells, head], axis=0)


def causal(seq, taps):
    total = taps[0] * seq
    for lag in range(1, taps.shape[0]):
        pad = jnp.zeros((lag,) + seq.shape[1:], jnp.float32)
        total = total + taps[lag] * jnp.concatenate([pad, seq[:-lag]], axis=0)
    return total


def anticausal(seq, taps):
    total = taps[0] * seq
    for lag in range(1, taps.shape[0]):
        pad = jnp.zeros((lag,) + seq.shape[1:], jnp.float32)
        total = total + taps[lag] * jnp.concatenate([seq[lag:], pad], axis=0)
    return total


def rounded(value):
    return lax.optimization_barrier(value.astype(jnp.bfloat16)).astype(jnp.float32)


def by_tokens(inputs, weights, feature_taps, inner_taps, grad_out):
    tile = inputs[0]
    upstream_tile = grad_out[0]
    rows_dev = upstream_tile.shape[0]
    width_row = weights.shape[0]
    width_col = weights.shape[2]
    margin = feature_taps.shape[0] - 1 + (inner_taps.shape[0] - 1)
    flat_w = weights.reshape(width_row, 3 * width_col)
    columns = lax.all_gather(tile, "col", axis=0, tiled=True)
    proj = lax.psum_scatter(
        jnp.dot(columns, flat_w, preferred_element_type=jnp.float32).astype(jnp.bfloat16),
        "row",
        scatter_dimension=0,
        tiled=True,
    )
    length = rows_dev + 2 * margin
    window = with_halo(proj, "row", margin).astype(jnp.float32).reshape(length, 3, width_col)
    after = shifted(upstream_tile[:margin], "row", -1)
    upstream = jnp.concatenate(
        [
            jnp.zeros((margin, width_col), jnp.float32),
            upstream_tile.astype(jnp.float32),
            after.astype(jnp.float32),
        ],
        axis=0,
    )
    mixed = causal(window, feature_taps)
    query = mixed[:, 0]
    key = mixed[:, 1]
    value = mixed[:, 2]
    product = rounded(key * value)
    inner = causal(product, inner_taps)
    grad_query = upstream * inner
    grad_product = anticausal(upstream * query, inner_taps)
    grad_mixed = jnp.stack([grad_query, grad_product * value, grad_product * key], axis=1)
    grad_proj = anticausal(grad_mixed, feature_taps)[margin : margin + rows_dev].astype(
        jnp.bfloat16
    )
    gathered = lax.all_gather(grad_proj.reshape(rows_dev, 3 * width_col), "row", axis=0, tiled=True)
    grad_x = lax.psum_scatter(
        lax.dot_general(
            gathered, flat_w, (((1,), (1,)), ((), ())), preferred_element_type=jnp.float32
        ).astype(jnp.bfloat16),
        "col",
        scatter_dimension=0,
        tiled=True,
    )
    local = lax.dot_general(
        columns, gathered, (((0,), (0,)), ((), ())), preferred_element_type=jnp.float32
    )
    grad_w = lax.psum(local.astype(jnp.bfloat16), "dp").astype(jnp.float32)
    return (grad_x[None], grad_w.reshape(width_row, 3, width_col))


def ring_order(count):
    return list(range(0, count, 2)) + list(range(1, count, 2))[::-1]


def swap(value, axis, step):
    size = lax.axis_size(axis)
    return lax.ppermute(value, axis, [(i, i ^ step) for i in range(size)])


def params(mib, grid=1):
    return pltpu.CompilerParams(
        dimension_semantics=("arbitrary",) * grid, vmem_limit_bytes=mib * 2**20
    )


def cost(flops, *arrays):
    total = sum(a.size * a.dtype.itemsize for a in arrays)
    return pl.CostEstimate(flops=flops, bytes_accessed=total, transcendentals=0)


def project(xs, w, cols):
    parts, depth, width = w.shape
    count = cols.shape[0]
    block = width // (lax.axis_size("row"))
    rows = [x.shape[0] for x in xs]
    tall = sum(rows)

    def body(cols_ref, *refs):
        x_refs, w_ref, out_ref = refs[: len(xs)], refs[-2], refs[-1]
        at = 0
        for x_ref, height in zip(x_refs, rows):
            out_ref[0, 0, at : at + height, :] = jnp.dot(
                x_ref[...], w_ref[0], preferred_element_type=jnp.float32
            ).astype(jnp.bfloat16)
            at += height

    out = jax.ShapeDtypeStruct((count, parts, tall, block), jnp.bfloat16)
    return pl.pallas_call(
        body,
        out_shape=out,
        grid_spec=pltpu.PrefetchScalarGridSpec(
            num_scalar_prefetch=1,
            grid=(count, parts),
            in_specs=[pl.BlockSpec((h, depth), lambda i, c, s: (0, 0)) for h in rows]
            + [pl.BlockSpec((1, depth, block), lambda i, c, s: (c, 0, s[i]))],
            out_specs=pl.BlockSpec((1, 1, tall, block), lambda i, c, s: (i, c, 0, 0)),
        ),
        compiler_params=params(16, 2),
        cost_estimate=cost(2 * tall * depth * parts * block * count, out, *xs, w),
    )(cols, *xs, w)


def gate(places, groups, ups, feature_taps, inner_taps, tokens, cuts):
    parts = feature_taps.shape[1]
    lags, long_lags = feature_taps.shape[0], inner_taps.shape[0]
    block = groups[0][2].shape[-1]
    shards = lax.axis_size("col")
    high = tokens // shards
    window = high + 2 * PAD
    n_in = 3 * len(groups)
    n_up = len(ups)

    def body(places_ref, *refs):
        ins, up_refs = refs[:n_in], refs[n_in : n_in + n_up]
        taps_ref, long_ref = refs[n_in + n_up : n_in + n_up + 2]
        outs = refs[n_in + n_up + 2 : -2]
        seq, cot = refs[-2:]
        seq[:, :PAD, :] = jnp.zeros((parts, PAD, LANES), jnp.float32)
        seq[:, PAD + tokens :, :] = jnp.zeros((parts, PAD, LANES), jnp.float32)
        cot[:PAD, :] = jnp.zeros((PAD, LANES), jnp.float32)
        cot[PAD + tokens :, :] = jnp.zeros((PAD, LANES), jnp.float32)
        shard = 0
        for g in range(len(groups)):
            keep, near, far = ins[3 * g : 3 * g + 3]
            for at in range(0, far.shape[1], high):
                to = pl.multiple_of(places_ref[shard] * high + PAD, PAD)
                shard += 1
                for c in range(parts):
                    total = (
                        keep[0, c, at : at + high, :].astype(jnp.float32)
                        + near[0, c, at : at + high, :].astype(jnp.float32)
                        + far[c, at : at + high, :].astype(jnp.float32)
                    )
                    seq[c, pl.ds(to, high), :] = total.astype(jnp.bfloat16).astype(jnp.float32)
        up_at = 2 * shards
        for up in up_refs:
            tall = up.shape[1]
            for i in range(up.shape[0]):
                to = pl.multiple_of(places_ref[up_at] * tall + PAD, PAD)
                up_at += 1
                cot[pl.ds(to, tall), :] = up[i].astype(jnp.float32)

        def back(value, lag):
            return pltpu.roll(value, lag, 0) if lag else value

        def ahead(value, lag):
            return pltpu.roll(value, window - lag, 0) if lag else value

        taps = [[taps_ref[s, c][None, :] for c in range(parts)] for s in range(lags)]
        long_taps = [long_ref[s][None, :] for s in range(long_lags)]
        shard = 0
        for out in outs:
            for at in range(0, out.shape[1], high):
                start = pl.multiple_of(places_ref[shards + shard] * high, PAD)
                shard += 1
                mixed = []
                for c in range(parts):
                    proj = seq[c, pl.ds(start, window), :]
                    total = taps[0][c] * proj
                    for s in range(1, lags):
                        total = total + taps[s][c] * back(proj, s)
                    mixed.append(total)
                query, key, value = mixed
                upstream = cot[pl.ds(start, window), :]
                product = (key * value).astype(jnp.bfloat16).astype(jnp.float32)
                inner = long_taps[0] * product
                for s in range(1, long_lags):
                    inner = inner + long_taps[s] * back(product, s)
                grad_inner = upstream * query
                grad_product = long_taps[0] * grad_inner
                for s in range(1, long_lags):
                    grad_product = grad_product + long_taps[s] * ahead(grad_inner, s)
                grads = (upstream * inner, grad_product * value, grad_product * key)
                for c, grad in enumerate(grads):
                    total = taps[0][c] * grad
                    for s in range(1, lags):
                        total = total + taps[s][c] * ahead(grad, s)
                    out[c, at : at + high, :] = total[PAD : PAD + high].astype(jnp.bfloat16)

    in_specs = []
    operands = []
    for keep, near, far in groups:
        tall = far.shape[1]
        in_specs += [
            pl.BlockSpec((1, parts, tall, LANES), lambda l, s: (0, 0, 0, l)),
            pl.BlockSpec((1, parts, tall, LANES), lambda l, s: (0, 0, 0, l)),
            pl.BlockSpec((parts, tall, LANES), lambda l, s: (0, 0, l)),
        ]
        operands += [keep, near, far]
    for up in ups:
        in_specs.append(pl.BlockSpec(up.shape[:2] + (LANES,), lambda l, s: (0, 0, l)))
        operands.append(up)
    per = block // LANES
    last = places.shape[0] - 1
    in_specs += [
        pl.BlockSpec((lags, parts, LANES), lambda l, s: (0, 0, s[last] * per + l)),
        pl.BlockSpec((long_lags, LANES), lambda l, s: (0, s[last] * per + l)),
    ]
    outs = [jax.ShapeDtypeStruct((parts, cut * high, block), jnp.bfloat16) for cut in cuts]
    return pl.pallas_call(
        body,
        out_shape=outs,
        grid_spec=pltpu.PrefetchScalarGridSpec(
            num_scalar_prefetch=1,
            grid=(block // LANES,),
            in_specs=in_specs,
            out_specs=[
                pl.BlockSpec((parts, cut * high, LANES), lambda l, s: (0, 0, l)) for cut in cuts
            ],
            scratch_shapes=[
                pltpu.VMEM((parts, tokens + 2 * PAD, LANES), jnp.float32),
                pltpu.VMEM((tokens + 2 * PAD, LANES), jnp.float32),
            ],
        ),
        compiler_params=params(16),
        cost_estimate=cost(100 * tokens * block * 8, *operands, *outs),
    )(places, *operands, feature_taps, inner_taps)


def input_grads(pieces, w, cols, high):
    parts, depth, width = w.shape
    tall, block = pieces[0].shape[1:]
    outs = [jax.ShapeDtypeStruct((high, depth), jnp.bfloat16) for _ in range(tall // high)]

    def body(cols_ref, *refs):
        gs, w_ref = refs[: len(pieces)], refs[len(pieces)]
        out_refs, total = refs[len(pieces) + 1 : -1], refs[-1]
        c = pl.program_id(0)
        part = None
        for i, g in enumerate(gs):
            at = pl.multiple_of(cols_ref[i] * block, LANES)
            term = lax.dot_general(
                g[0],
                w_ref[0, :, pl.ds(at, block)],
                (((1,), (1,)), ((), ())),
                preferred_element_type=jnp.float32,
            )
            part = term if part is None else part + term

        @pl.when(c == 0)
        def _():
            total[...] = part

        @pl.when((c > 0) & (c < parts - 1))
        def _():
            total[...] += part

        @pl.when(c == parts - 1)
        def _():
            full = total[...] + part
            for i, out in enumerate(out_refs):
                out[...] = full[i * high : (i + 1) * high].astype(jnp.bfloat16)

    return pl.pallas_call(
        body,
        out_shape=outs,
        grid_spec=pltpu.PrefetchScalarGridSpec(
            num_scalar_prefetch=1,
            grid=(parts,),
            in_specs=[pl.BlockSpec((1, tall, block), lambda c, s: (c, 0, 0)) for _ in pieces]
            + [pl.BlockSpec((1, depth, width), lambda c, s: (c, 0, 0))],
            out_specs=[pl.BlockSpec((high, depth), lambda c, s: (0, 0)) for _ in outs],
            scratch_shapes=[pltpu.VMEM((tall, depth), jnp.float32)],
        ),
        compiler_params=params(24),
        cost_estimate=cost(2 * tall * depth * parts * width, *pieces, w, *outs),
    )(cols, *pieces, w)


def weight_grads(done, xts, grads, col, width):
    depth = xts[0].shape[0]
    parts, _, block = grads[0][0].shape
    flat = [g for group in grads for g in group]

    def body(col_ref, *refs):
        x_refs, g_refs, out = refs[:2], refs[2 : 2 + len(flat)], refs[-1]
        total = None
        i = 0
        for x, group in zip(x_refs, grads):
            at = 0
            for g in group:
                tall = g.shape[1]
                term = jnp.dot(
                    x[:, at : at + tall], g_refs[i][0], preferred_element_type=jnp.float32
                )
                total = term if total is None else total + term
                at += tall
                i += 1
        out[0] = total

    shape = jax.ShapeDtypeStruct((parts, depth, width), jnp.float32)
    in_specs = [pl.BlockSpec(x.shape, lambda c, s: (0, 0)) for x in xts] + [
        pl.BlockSpec((1,) + g.shape[1:], lambda c, s: (c, 0, 0)) for g in flat
    ]
    operands = list(xts) + flat
    aliases = {}
    if done is not None:
        in_specs.append(pl.BlockSpec(memory_space=pl.ANY))
        aliases = {1 + len(operands): 0}
        operands.append(done)
    tokens = sum(g.shape[1] for g in flat)
    return pl.pallas_call(
        body,
        out_shape=shape,
        grid_spec=pltpu.PrefetchScalarGridSpec(
            num_scalar_prefetch=1,
            grid=(parts,),
            in_specs=in_specs,
            out_specs=pl.BlockSpec((1, depth, block), lambda c, s: (c, 0, s[0])),
        ),
        input_output_aliases=aliases,
        compiler_params=params(24),
        cost_estimate=pl.CostEstimate(
            flops=2 * tokens * depth * parts * block,
            bytes_accessed=4 * depth * parts * block + 2 * tokens * (depth + parts * block),
            transcendentals=0,
        ),
    )(col, *operands)


def by_channels(inputs, weights, feature_taps, inner_taps, grad_out):
    x_own = inputs[0]
    high = x_own.shape[0]
    n_row, n_col = lax.axis_size("row"), lax.axis_size("col")
    chips = n_row // CORES
    tokens = high * n_col
    w = jnp.transpose(weights, (1, 0, 2))
    parts, depth, width = w.shape
    block = width // n_row
    row, col = lax.axis_index("row"), lax.axis_index("col")
    chip, core = row // CORES, row % CORES

    order = ring_order(n_col)
    ring = [(order[i], order[(i + 1) % n_col]) for i in range(n_col)]
    spot = jnp.array([order.index(i) for i in range(n_col)], jnp.int32)[col]
    arrive = [jnp.array(order, jnp.int32)[(spot - j) % n_col] for j in range(n_col)]
    leave = [arrive[(j + 1) % n_col] for j in range(n_col)]

    there = [((chip + j) % chips) * CORES + (1 - core) for j in range(chips)]
    here = [((chip + j) % chips) * CORES + core for j in range(chips)]

    up = grad_out[0]
    cut = lambda i: lax.dynamic_slice_in_dim(up, i * block, block, 1)
    near = swap(jnp.stack([cut(i) for i in there]), "row", 1)
    far = swap(jnp.stack([cut(here[1]), near[1]]), "row", CORES)
    ups = [jnp.stack([cut(here[0]), near[0]]), far]
    up_places = [row, there[0], here[1], there[1]]

    xs = [x_own]
    for _ in range(n_col - 1):
        xs.append(lax.ppermute(xs[-1], "col", ring))
    groups = []
    for members in (tuple(range(n_col)),):
        mine = [xs[j] for j in members]
        send = project(mine, w, jnp.stack(there).astype(jnp.int32))
        got = swap(send, "row", 1)
        keep = project(mine, w, jnp.stack(here).astype(jnp.int32))
        both = (keep[1].astype(jnp.float32) + got[1].astype(jnp.float32)).astype(jnp.bfloat16)
        groups.append((keep, got, swap(both, "row", CORES)))

    xt = jnp.concatenate([xs[(j + 1) % n_col] for j in range(n_col)], axis=0).T
    xt_other = swap(xt, "dp", 1)

    places = jnp.stack(arrive + leave + up_places + [row]).astype(jnp.int32)
    grads = gate(places, groups, ups, feature_taps, inner_taps, tokens, (n_col,))

    own, y, x, xy = [], [], [], []
    for g in grads:
        gy = swap(g, "row", CORES)
        gx = swap(g, "dp", 1)
        own.append((g, swap(g, "row", 1)))
        y.append((gy, swap(gy, "row", 1)))
        x.append((gx, swap(gx, "row", 1)))
        gxy = swap(gx, "row", CORES)
        xy.append((gxy, swap(gxy, "row", 1)))
    spots = jnp.stack([here[0], here[1], there[0], there[1]]).astype(jnp.int32)
    shares = []
    for a, b in zip(own, y):
        shares += input_grads([a[0], b[0], a[1], b[1]], w, spots, high)

    passed = shares[0]
    for share in shares[1:]:
        got = lax.ppermute(passed, "col", ring)
        passed = (got.astype(jnp.float32) + share.astype(jnp.float32)).astype(jnp.bfloat16)

    grad_w = None
    for side in range(CORES):
        for mine, theirs, at in ((own, x, 0), (y, xy, 1)):
            pair = ([g[side] for g in mine], [g[side] for g in theirs])
            spot_at = spots[2 * side + at][None]
            grad_w = weight_grads(grad_w, (xt, xt_other), pair, spot_at, width)
    return (passed[None], jnp.transpose(grad_w, (1, 0, 2)))


def solution(mesh):
    placed = (
        P("dp", "col", "row"),
        P("row", None, "col"),
        P(None, None, "col"),
        P(None, "col"),
        P("dp", "row", "col"),
    )

    def on_device(inputs, weights, feature_taps, inner_taps, grad_out):
        n_row = mesh.shape["row"]
        fits = weights.shape[2] % (n_row * LANES) == 0 and inputs.shape[1] % LANES == 0
        small = n_row == 2 * CORES and mesh.shape["dp"] == 2
        plan = by_channels if fits and small else by_tokens
        return plan(inputs, weights, feature_taps, inner_taps, grad_out)

    return jax.shard_map(
        on_device,
        mesh=mesh,
        in_specs=placed,
        out_specs=(P("dp", "col", "row"), P("row", None, "col")),
        check_vma=False,
    )
```

```python
import math

import jax
import jax.numpy as jnp
from jax import lax
from jax.experimental import pallas as pl
from jax.experimental.pallas import tpu as pltpu
from jax.sharding import PartitionSpec as P

LANES = 128
PAD = 8
CORES = 2


def shifted(shard, axis, by):
    length = lax.axis_size(axis)
    pairs = [(i, i + by) for i in range(length) if 0 <= i + by < length]
    return lax.ppermute(shard, axis, pairs)


def with_halo(cells, axis, width):
    head = shifted(cells[:width], axis, -1)
    tail = shifted(cells[-width:], axis, 1)
    return jnp.concatenate([tail, cells, head], axis=0)


def causal(seq, taps):
    total = taps[0] * seq
    for lag in range(1, taps.shape[0]):
        pad = jnp.zeros((lag,) + seq.shape[1:], jnp.float32)
        total = total + taps[lag] * jnp.concatenate([pad, seq[:-lag]], axis=0)
    return total


def anticausal(seq, taps):
    total = taps[0] * seq
    for lag in range(1, taps.shape[0]):
        pad = jnp.zeros((lag,) + seq.shape[1:], jnp.float32)
        total = total + taps[lag] * jnp.concatenate([seq[lag:], pad], axis=0)
    return total


def rounded(value):
    return lax.optimization_barrier(value.astype(jnp.bfloat16)).astype(jnp.float32)


def by_tokens(inputs, weights, feature_taps, inner_taps, grad_out):
    tile = inputs[0]
    upstream_tile = grad_out[0]
    rows_dev = upstream_tile.shape[0]
    width_row = weights.shape[0]
    width_col = weights.shape[2]
    margin = feature_taps.shape[0] - 1 + (inner_taps.shape[0] - 1)
    flat_w = weights.reshape(width_row, 3 * width_col)
    columns = lax.all_gather(tile, "col", axis=0, tiled=True)
    proj = lax.psum_scatter(
        jnp.dot(columns, flat_w, preferred_element_type=jnp.float32).astype(jnp.bfloat16),
        "row",
        scatter_dimension=0,
        tiled=True,
    )
    length = rows_dev + 2 * margin
    window = with_halo(proj, "row", margin).astype(jnp.float32).reshape(length, 3, width_col)
    after = shifted(upstream_tile[:margin], "row", -1)
    upstream = jnp.concatenate(
        [
            jnp.zeros((margin, width_col), jnp.float32),
            upstream_tile.astype(jnp.float32),
            after.astype(jnp.float32),
        ],
        axis=0,
    )
    mixed = causal(window, feature_taps)
    query = mixed[:, 0]
    key = mixed[:, 1]
    value = mixed[:, 2]
    product = rounded(key * value)
    inner = causal(product, inner_taps)
    grad_query = upstream * inner
    grad_product = anticausal(upstream * query, inner_taps)
    grad_mixed = jnp.stack([grad_query, grad_product * value, grad_product * key], axis=1)
    grad_proj = anticausal(grad_mixed, feature_taps)[margin : margin + rows_dev].astype(
        jnp.bfloat16
    )
    gathered = lax.all_gather(grad_proj.reshape(rows_dev, 3 * width_col), "row", axis=0, tiled=True)
    grad_x = lax.psum_scatter(
        lax.dot_general(
            gathered, flat_w, (((1,), (1,)), ((), ())), preferred_element_type=jnp.float32
        ).astype(jnp.bfloat16),
        "col",
        scatter_dimension=0,
        tiled=True,
    )
    local = lax.dot_general(
        columns, gathered, (((0,), (0,)), ((), ())), preferred_element_type=jnp.float32
    )
    grad_w = lax.psum(local.astype(jnp.bfloat16), "dp").astype(jnp.float32)
    return (grad_x[None], grad_w.reshape(width_row, 3, width_col))


def swap(value, axis, step):
    size = lax.axis_size(axis)
    return lax.ppermute(value, axis, [(i, i ^ step) for i in range(size)])


def after(value, *others):
    return lax.optimization_barrier((value,) + others)[0]


VMEM = pl.BlockSpec(memory_space=pltpu.VMEM)
SMEM = pl.BlockSpec(memory_space=pltpu.SMEM)
ANY = pl.BlockSpec(memory_space=pl.ANY)


def local(body, outs, ins, in_specs, flops, scratch=(), out_specs=None, aliases=None):
    leaves = outs if isinstance(outs, (list, tuple)) else [outs]
    traffic = sum(math.prod(a.shape) * a.dtype.itemsize for a in [*ins, *leaves])
    if out_specs is None:
        out_specs = [VMEM] * len(outs) if isinstance(outs, (list, tuple)) else VMEM
    return pl.pallas_call(
        body,
        out_shape=outs,
        in_specs=in_specs,
        out_specs=out_specs,
        scratch_shapes=list(scratch),
        input_output_aliases=aliases or {},
        compiler_params=pltpu.CompilerParams(vmem_limit_bytes=16 * 2**20),
        cost_estimate=pl.CostEstimate(flops=flops, bytes_accessed=traffic, transcendentals=0),
    )(*ins)


def bf16(*shape):
    return jax.ShapeDtypeStruct(shape, jnp.bfloat16)


def slots(z):
    return [z, z ^ 1, jnp.where(z < 2, 2, 1), jnp.where(z < 2, 3, 0)]


PAIR = [(0, 1), (1, 0), (2, 3), (3, 2)]
INNER = [(1, 2), (2, 1)]
OUTWARD = [(1, 0), (2, 3)]
INWARD = [(0, 1), (3, 2)]


def held(w):
    def body(w_ref, out_ref, sem):
        copy = pltpu.make_async_copy(w_ref, out_ref, sem)
        copy.start()
        copy.wait()

    return local(
        body, pltpu.VMEM(w.shape, w.dtype), [w], [ANY], 0, scratch=[pltpu.SemaphoreType.DMA]
    )


def parted(me, up, block):
    high = up.shape[0]

    def body(me_ref, up_ref, there_ref, *here_refs):
        row = me_ref[0]
        for j in range(2):
            at = pl.multiple_of((row ^ (2 * j + 1)) * block, LANES)
            there_ref[j] = up_ref[:, pl.ds(at, block)]
            at = pl.multiple_of((row ^ (2 * j)) * block, LANES)
            here_refs[j][...] = up_ref[:, pl.ds(at, block)]

    return local(
        body,
        [bf16(2, high, block), bf16(high, block), bf16(high, block)],
        [me, up],
        [SMEM, VMEM],
        0,
    )


def project(me, xs, w, block, other):
    parts, depth, _ = w.shape
    high = xs[0].shape[0]

    def body(me_ref, *refs):
        x_refs, w_ref, out_ref = refs[:-2], refs[-2], refs[-1]
        x = x_refs[0][...]
        if len(xs) > 1:
            z = me_ref[1]
            x = jnp.where((z == 0) | (z == 3), x_refs[1][...], x)
        for j in range(2):
            at = pl.multiple_of((me_ref[0] ^ (2 * j + other)) * block, LANES)
            for c in range(parts):
                out_ref[j, c] = jnp.dot(
                    x, w_ref[c, :, pl.ds(at, block)], preferred_element_type=jnp.float32
                ).astype(jnp.bfloat16)

    return local(
        body,
        bf16(2, parts, high, block),
        [me, *xs, w],
        [SMEM] + [VMEM] * (len(xs) + 1),
        4 * high * depth * parts * block,
    )


def gate(me, groups, ups, feature_taps, inner_taps):
    lags, parts, _ = feature_taps.shape
    long_lags = inner_taps.shape[0]
    high, block = groups[0][2].shape[1:]
    tokens = high * len(groups)
    window = high + 2 * PAD
    n_in, n_up = 3 * len(groups), len(ups)
    count = len(groups)

    def body(me_ref, *refs):
        ins, up_refs = refs[:n_in], refs[n_in : n_in + n_up]
        taps_ref, long_ref = refs[n_in + n_up : n_in + n_up + 2]
        singles = refs[n_in + n_up + 2 :][:count]
        pairs = refs[n_in + n_up + 2 + count :][: count // 2]
        seq, cot = refs[-2:]
        row = me_ref[0]
        places = slots(me_ref[1])
        seq[:, :PAD, :] = jnp.zeros((parts, PAD, LANES), jnp.float32)
        seq[:, PAD + tokens :, :] = jnp.zeros((parts, PAD, LANES), jnp.float32)
        cot[:PAD, :] = jnp.zeros((PAD, LANES), jnp.float32)
        cot[PAD + tokens :, :] = jnp.zeros((PAD, LANES), jnp.float32)

        def back(value, lag):
            return pltpu.roll(value, lag, 0) if lag else value

        def ahead(value, lag):
            return pltpu.roll(value, window - lag, 0) if lag else value

        @pl.loop(0, block // LANES)
        def _(half):
            lanes = pl.ds(pl.multiple_of(half * LANES, LANES), LANES)
            for s in range(count):
                keep, near, far = ins[3 * s : 3 * s + 3]
                to = pl.multiple_of(places[s] * high + PAD, PAD)
                for c in range(parts):
                    total = (
                        keep[0, c, :, lanes].astype(jnp.float32)
                        + near[0, c, :, lanes].astype(jnp.float32)
                        + far[c, :, lanes].astype(jnp.float32)
                    )
                    seq[c, pl.ds(to, high), :] = total.astype(jnp.bfloat16).astype(jnp.float32)
            for i, up in enumerate(up_refs):
                tall = up.shape[0]
                to = pl.multiple_of((row ^ i) * tall + PAD, PAD)
                cot[pl.ds(to, tall), :] = up[:, lanes].astype(jnp.float32)

            wide = pl.ds(pl.multiple_of(row * block + half * LANES, LANES), LANES)
            taps = [[taps_ref[s, c : c + 1, wide] for c in range(parts)] for s in range(lags)]
            long_taps = [long_ref[s : s + 1, wide] for s in range(long_lags)]
            for s in range(count):
                start = pl.multiple_of(places[s] * high, PAD)
                mixed = []
                for c in range(parts):
                    proj = seq[c, pl.ds(start, window), :]
                    total = taps[0][c] * proj
                    for lag in range(1, lags):
                        total = total + taps[lag][c] * back(proj, lag)
                    mixed.append(total)
                query, key, value = mixed
                upstream = cot[pl.ds(start, window), :]
                product = (key * value).astype(jnp.bfloat16).astype(jnp.float32)
                inner = long_taps[0] * product
                for lag in range(1, long_lags):
                    inner = inner + long_taps[lag] * back(product, lag)
                grad_inner = upstream * query
                grad_product = long_taps[0] * grad_inner
                for lag in range(1, long_lags):
                    grad_product = grad_product + long_taps[lag] * ahead(grad_inner, lag)
                grads = (upstream * inner, grad_product * value, grad_product * key)
                for c, grad in enumerate(grads):
                    total = taps[0][c] * grad
                    for lag in range(1, lags):
                        total = total + taps[lag][c] * ahead(grad, lag)
                    done = total[PAD : PAD + high].astype(jnp.bfloat16)
                    singles[s][c, :, lanes] = done
                    pairs[s // 2][s % 2, c, :, lanes] = done

    operands = [a for group in groups for a in group] + list(ups)
    outs = [bf16(parts, high, block)] * count + [bf16(2, parts, high, block)] * (count // 2)
    grads = local(
        body,
        outs,
        [me, *operands, feature_taps, inner_taps],
        [SMEM] + [VMEM] * (len(operands) + 2),
        800 * tokens * block,
        scratch=[
            pltpu.VMEM((parts, tokens + 2 * PAD, LANES), jnp.float32),
            pltpu.VMEM((tokens + 2 * PAD, LANES), jnp.float32),
        ],
    )
    return grads[:count], grads[count:]


def view(ref, index):
    return ref if index is None else ref.at[index]


def input_grads(me, pieces, w, block):
    parts, depth, width = w.shape
    high = pieces[0][0].shape[-2]

    def body(me_ref, *refs):
        w_ref, out_ref, wide = refs[-3:]
        for i, (g, (_, index)) in enumerate(zip(refs, pieces)):
            at = pl.multiple_of((me_ref[0] ^ i) * block, LANES)
            wide[:, :, pl.ds(at, block)] = view(g, index)[...]
        total = None
        for c in range(parts):
            term = lax.dot_general(
                wide[c], w_ref[c], (((1,), (1,)), ((), ())), preferred_element_type=jnp.float32
            )
            total = term if total is None else total + term
        out_ref[...] = total.astype(jnp.bfloat16)

    return local(
        body,
        bf16(high, depth),
        [me, *(g for g, _ in pieces), w],
        [SMEM] + [VMEM] * (len(pieces) + 1),
        2 * high * depth * parts * width,
        scratch=[pltpu.VMEM((parts, high, width), jnp.bfloat16)],
    )


def turned(me, a, b, b_end=None):
    high, depth = a[0].shape
    flat = [*a, *b]

    def pick(me_ref, refs):
        if len(refs) == 1:
            return refs[0][...]
        z = me_ref[1]
        return jnp.where((z == 0) | (z == 3), refs[1][...], refs[0][...])

    def body(me_ref, *refs):
        out_ref = refs[-1]
        out_ref[:, :high] = pick(me_ref, refs[: len(a)]).T
        out_ref[:, high:] = pick(me_ref, refs[len(a) : -1]).T

    return local(
        body, bf16(depth, 2 * high), [me, *flat], [SMEM] + [VMEM] * len(flat), 0
    )


def weight_grads(me, done, xts, blocks, width):
    depth = xts[0].shape[0]
    first = blocks[0][1][0][0]
    parts, high, block = first.shape[-3:]
    flat = [p for _, pieces in blocks for p in pieces]
    unique = []
    for g, _ in flat:
        if not any(g is u for u in unique):
            unique.append(g)
    spot = {id(u): n for n, u in enumerate(unique)}
    tokens = high * len(blocks[0][1])
    steps = len(blocks) * parts

    def body(me_ref, *refs):
        x_refs = refs[: len(xts)]
        g_refs = refs[len(xts) : len(xts) + len(unique)]
        out_ref, xt, gs, held_out, sems = refs[-5:]
        at = 0
        for x in x_refs:
            xt[:, at : at + x.shape[1]] = x[...]
            at += x.shape[1]
        copies = []
        for n, (i, pieces) in enumerate(blocks):
            to = pl.ds(pl.multiple_of((me_ref[0] ^ i) * block, LANES), block)
            for c in range(parts):
                step = n * parts + c
                for k, (g, index) in enumerate(pieces):
                    gs[k * high : (k + 1) * high, :] = view(g_refs[spot[id(g)]], index)[c]
                if step >= 2:
                    copies[step - 2].wait()
                held_out[step % 2] = jnp.dot(xt[...], gs[...], preferred_element_type=jnp.float32)
                copy = pltpu.make_async_copy(
                    held_out.at[step % 2], out_ref.at[c, :, to], sems.at[step % 2]
                )
                copy.start()
                copies.append(copy)
        for copy in copies[-2:]:
            copy.wait()

    ins = [me, *xts, *unique]
    specs = [SMEM] + [VMEM] * (len(ins) - 1)
    aliases = {}
    if done is not None:
        aliases = {len(ins): 0}
        ins.append(done)
        specs.append(ANY)
    return local(
        body,
        jax.ShapeDtypeStruct((parts, depth, width), jnp.float32),
        ins,
        specs,
        2 * tokens * depth * steps * block,
        scratch=[
            pltpu.VMEM((depth, tokens), jnp.bfloat16),
            pltpu.VMEM((tokens, block), jnp.bfloat16),
            pltpu.VMEM((2, depth, block), jnp.float32),
            pltpu.SemaphoreType.DMA((2,)),
        ],
        out_specs=ANY,
        aliases=aliases,
    )


def summed(*terms):
    total = terms[0].astype(jnp.float32)
    for term in terms[1:]:
        total = total + term.astype(jnp.float32)
    return total.astype(jnp.bfloat16)


def by_channels(inputs, weights, feature_taps, inner_taps, grad_out):
    x_own = inputs[0]
    n_row = lax.axis_size("row")
    block = weights.shape[2] // n_row
    width = weights.shape[2]
    me = jnp.stack([lax.axis_index("row"), lax.axis_index("col")]).astype(jnp.int32)

    pair = lax.ppermute(x_own, "col", PAIR)
    inner = lax.ppermute(x_own, "col", INNER)
    w = held(jnp.transpose(weights, (1, 0, 2)))

    there, here, across = parted(me, grad_out[0], block)
    near = swap(there, "row", 1)
    far = swap(jnp.stack([across, near[1]]), "row", CORES)
    ups = [here, near[0], far[0], far[1]]

    inner_far = lax.ppermute(pair, "col", INNER)
    outer = lax.ppermute(inner, "col", OUTWARD)
    outer_far = lax.ppermute(inner_far, "col", OUTWARD)
    xs = [(x_own,), (pair,), (inner, outer), (inner_far, outer_far)]

    groups = []
    for x in xs:
        send = project(me, x, w, block, 1)
        got = swap(send, "row", 1)
        keep = project(me, x, w, block, 0)
        groups.append((keep, got, swap(summed(keep[1], got[1]), "row", CORES)))

    xts = [turned(me, xs[0], xs[1]), turned(me, xs[2], xs[3])]
    xts += [swap(x, "dp", 1) for x in xts]

    g, (gb, ga) = gate(me, groups, ups, feature_taps, inner_taps)
    gy = [None] * 4
    gcy = [None] * 4
    share = [None] * 4
    gca, gcb = swap(ga, "row", 1), swap(gb, "row", 1)
    gc = [(gcb, 0), (gcb, 1), (gca, 0), (gca, 1)]
    for s in (3, 2, 1, 0):
        gy[s] = swap(g[s], "row", CORES)
        gcy[s] = swap(gy[s], "row", 1)
        share[s] = input_grads(
            me, [(g[s], None), gc[s], (gy[s], None), (gcy[s], None)], w, block
        )
    passed = lax.ppermute(share[3], "col", INWARD)
    passed = lax.ppermute(summed(share[3], passed), "col", INNER)
    side = lax.ppermute(share[2], "col", INWARD)
    side = lax.ppermute(summed(share[2], side), "col", INNER)
    passed = lax.ppermute(summed(share[1], passed), "col", PAIR)
    grad_in = summed(share[0], passed, side)

    gxa, gxb = swap(ga, "dp", 1), swap(gb, "dp", 1)
    gcxa, gcxb = swap(gxa, "row", 1), swap(gxb, "row", 1)
    gxya = swap(gxa, "row", CORES)
    gxy = [(swap(gy[0], "dp", 1), None), (swap(gy[1], "dp", 1), None), (gxya, 0), (gxya, 1)]
    gcxya = swap(gxya, "row", 1)
    gcxy = [(swap(a, "row", 1), None) for a, _ in gxy[:2]] + [(gcxya, 0), (gcxya, 1)]
    gx = [(gxb, 0), (gxb, 1), (gxa, 0), (gxa, 1)]
    gcx = [(gcxb, 0), (gcxb, 1), (gcxa, 0), (gcxa, 1)]
    g = [(a, None) for a in g]
    gy = [(a, None) for a in gy]
    gcy = [(a, None) for a in gcy]
    grad_w = weight_grads(me, None, xts, [(0, g + gx), (1, gc + gcx)], width)
    grad_w = weight_grads(me, grad_w, xts, [(2, gy + gxy), (3, gcy + gcxy)], width)
    return (grad_in[None], jnp.transpose(grad_w, (1, 0, 2)))


def solution(mesh):
    placed = (
        P("dp", "col", "row"),
        P("row", None, "col"),
        P(None, None, "col"),
        P(None, "col"),
        P("dp", "row", "col"),
    )

    def on_device(inputs, weights, feature_taps, inner_taps, grad_out):
        n_row = mesh.shape["row"]
        fits = weights.shape[2] % (n_row * LANES) == 0 and inputs.shape[1] % LANES == 0
        small = n_row == 2 * CORES and mesh.shape["dp"] == 2 and mesh.shape["col"] == 4
        plan = by_channels if fits and small else by_tokens
        return plan(inputs, weights, feature_taps, inner_taps, grad_out)

    return jax.shard_map(
        on_device,
        mesh=mesh,
        in_specs=placed,
        out_specs=(P("dp", "col", "row"), P("row", None, "col")),
        check_vma=False,
    )
```

```python
import math

import jax
import jax.numpy as jnp
from jax import lax
from jax.experimental import pallas as pl
from jax.experimental.pallas import tpu as pltpu
from jax.sharding import PartitionSpec as P

LANES = 128
PAD = 8
CORES = 2


def shifted(shard, axis, by):
    length = lax.axis_size(axis)
    pairs = [(i, i + by) for i in range(length) if 0 <= i + by < length]
    return lax.ppermute(shard, axis, pairs)


def with_halo(cells, axis, width):
    head = shifted(cells[:width], axis, -1)
    tail = shifted(cells[-width:], axis, 1)
    return jnp.concatenate([tail, cells, head], axis=0)


def causal(seq, taps):
    total = taps[0] * seq
    for lag in range(1, taps.shape[0]):
        pad = jnp.zeros((lag,) + seq.shape[1:], jnp.float32)
        total = total + taps[lag] * jnp.concatenate([pad, seq[:-lag]], axis=0)
    return total


def anticausal(seq, taps):
    total = taps[0] * seq
    for lag in range(1, taps.shape[0]):
        pad = jnp.zeros((lag,) + seq.shape[1:], jnp.float32)
        total = total + taps[lag] * jnp.concatenate([seq[lag:], pad], axis=0)
    return total


def rounded(value):
    return lax.optimization_barrier(value.astype(jnp.bfloat16)).astype(jnp.float32)


def by_tokens(inputs, weights, feature_taps, inner_taps, grad_out):
    tile = inputs[0]
    upstream_tile = grad_out[0]
    rows_dev = upstream_tile.shape[0]
    width_row = weights.shape[0]
    width_col = weights.shape[2]
    margin = feature_taps.shape[0] - 1 + (inner_taps.shape[0] - 1)
    flat_w = weights.reshape(width_row, 3 * width_col)
    columns = lax.all_gather(tile, "col", axis=0, tiled=True)
    proj = lax.psum_scatter(
        jnp.dot(columns, flat_w, preferred_element_type=jnp.float32).astype(jnp.bfloat16),
        "row",
        scatter_dimension=0,
        tiled=True,
    )
    length = rows_dev + 2 * margin
    window = with_halo(proj, "row", margin).astype(jnp.float32).reshape(length, 3, width_col)
    after = shifted(upstream_tile[:margin], "row", -1)
    upstream = jnp.concatenate(
        [
            jnp.zeros((margin, width_col), jnp.float32),
            upstream_tile.astype(jnp.float32),
            after.astype(jnp.float32),
        ],
        axis=0,
    )
    mixed = causal(window, feature_taps)
    query = mixed[:, 0]
    key = mixed[:, 1]
    value = mixed[:, 2]
    product = rounded(key * value)
    inner = causal(product, inner_taps)
    grad_query = upstream * inner
    grad_product = anticausal(upstream * query, inner_taps)
    grad_mixed = jnp.stack([grad_query, grad_product * value, grad_product * key], axis=1)
    grad_proj = anticausal(grad_mixed, feature_taps)[margin : margin + rows_dev].astype(
        jnp.bfloat16
    )
    gathered = lax.all_gather(grad_proj.reshape(rows_dev, 3 * width_col), "row", axis=0, tiled=True)
    grad_x = lax.psum_scatter(
        lax.dot_general(
            gathered, flat_w, (((1,), (1,)), ((), ())), preferred_element_type=jnp.float32
        ).astype(jnp.bfloat16),
        "col",
        scatter_dimension=0,
        tiled=True,
    )
    local = lax.dot_general(
        columns, gathered, (((0,), (0,)), ((), ())), preferred_element_type=jnp.float32
    )
    grad_w = lax.psum(local.astype(jnp.bfloat16), "dp").astype(jnp.float32)
    return (grad_x[None], grad_w.reshape(width_row, 3, width_col))


def swap(value, axis, step):
    size = lax.axis_size(axis)
    return lax.ppermute(value, axis, [(i, i ^ step) for i in range(size)])


LINE = (0, 2, 3, 1)


def along(value, steps):
    size = len(LINE)
    pairs = [(LINE[i], LINE[(i + steps) % size]) for i in range(size)]
    return lax.ppermute(value, "col", pairs)


def behind(z, steps):
    for _ in range(steps):
        z = jnp.where(z < 2, 2 * z + 1, 2 * z - 4)
    return z


VMEM = pl.BlockSpec(memory_space=pltpu.VMEM)
SMEM = pl.BlockSpec(memory_space=pltpu.SMEM)
HBM = pl.BlockSpec(memory_space=pltpu.HBM)
ANY = pl.BlockSpec(memory_space=pl.ANY)


PER_MICRO = 1.1e9


def hbm(value):
    return pltpu.with_memory_space_constraint(value, pltpu.HBM)


def bf16(*shape):
    return jax.ShapeDtypeStruct(shape, jnp.bfloat16)


def local(me, body, outs, ins, micros, in_specs=None, scratch=(), out_specs=None, aliases=None, late=()):
    def ordered(me_ref, *refs):
        results = refs[len(ins) + len(late) :]
        results[0][0] = me_ref[0]
        results[0][1] = me_ref[1]
        body(me_ref, *refs[: len(ins)], *results[1:])

    me, *results = pl.pallas_call(
        ordered,
        out_shape=[jax.ShapeDtypeStruct(me.shape, me.dtype), *outs],
        in_specs=[SMEM, *(in_specs or [VMEM] * len(ins)), *[ANY] * len(late)],
        out_specs=[SMEM, *(out_specs or [VMEM] * len(outs))],
        scratch_shapes=list(scratch),
        input_output_aliases=aliases or {},
        compiler_params=pltpu.CompilerParams(vmem_limit_bytes=16 * 2**20),
        cost_estimate=pl.CostEstimate(flops=int(micros * PER_MICRO), bytes_accessed=1, transcendentals=0),
    )(me, *ins, *late)
    return me, results


def multiply(x, w_ref, c, block_at, out_ref):
    block = out_ref.shape[-1]
    at = pl.multiple_of(block_at * block, LANES)
    out_ref[c] = jnp.dot(
        x, w_ref[c, :, pl.ds(at, block)], preferred_element_type=jnp.float32
    ).astype(jnp.bfloat16)


def begin(me, x, up, w, block):
    parts, depth, width = w.shape
    high = up.shape[0]

    def body(me_ref, x_hbm, up_hbm, w_hbm, *refs):
        w_ref, x_ref, there_ref, here_ref, across_ref, *away_refs, up_ref, sems = refs
        row = me_ref[0]
        loads = [pltpu.make_async_copy(up_hbm, up_ref, sems.at[0])]
        loads += [pltpu.make_async_copy(x_hbm, x_ref, sems.at[1])]
        loads += [
            pltpu.make_async_copy(w_hbm.at[c], w_ref.at[c], sems.at[2 + c]) for c in range(parts)
        ]
        for load in loads:
            load.start()
        loads[0].wait()
        for j in range(2):
            at = pl.multiple_of((row ^ (2 * j + 1)) * block, LANES)
            there_ref[j] = up_ref[:, pl.ds(at, block)]
        here_ref[...] = up_ref[:, pl.ds(pl.multiple_of(row * block, LANES), block)]
        across_ref[...] = up_ref[:, pl.ds(pl.multiple_of((row ^ 2) * block, LANES), block)]
        loads[1].wait()
        for c in range(parts):
            loads[2 + c].wait()
            for j in range(2):
                multiply(x_ref[...], w_ref, c, row ^ (2 * j + 1), away_refs[j])

    return local(
        me,
        body,
        [
            pltpu.VMEM(w.shape, w.dtype),
            pltpu.VMEM(x.shape, x.dtype),
            bf16(2, high, block),
            bf16(high, block),
            bf16(high, block),
            bf16(parts, high, block),
            bf16(parts, high, block),
        ],
        [hbm(x), hbm(up), hbm(w)],
        3.5,
        [HBM, HBM, HBM],
        scratch=[
            pltpu.VMEM(up.shape, up.dtype),
            pltpu.SemaphoreType.DMA((2 + parts,)),
        ],
    )


def project(me, xs, w, block, other, late=()):
    parts = w.shape[0]
    tall = xs[0].shape[0] * len(xs)

    def body(me_ref, *refs):
        w_ref, out_refs = refs[len(xs)], refs[len(xs) + 1 :]
        x = jnp.concatenate([x[...] for x in refs[: len(xs)]], axis=0)
        for j in (1, 0):
            for c in range(parts):
                multiply(x, w_ref, c, me_ref[0] ^ (2 * j + other), out_refs[j])

    outs = [bf16(parts, tall, block)] * 2
    return local(me, body, outs, [*xs, w], 1.2 * len(xs), late=late)


def laid_out(me, groups, shards, ups, late=()):
    parts, _, block = groups[0][2].shape
    tokens = sum(far.shape[1] for _, _, far in groups)
    high = ups[0].shape[0]
    n_in = 3 * len(groups)

    def body(me_ref, *refs):
        ins, up_refs, (seq, cot) = refs[:n_in], refs[n_in:-2], refs[-2:]
        row, z = me_ref[0], me_ref[1]
        for at in (0, PAD + tokens):
            seq[:, at : at + PAD, :] = jnp.zeros((parts, PAD, block), jnp.float32)
            cot[at : at + PAD, :] = jnp.zeros((PAD, block), jnp.float32)
        for g, which in enumerate(shards):
            keep, near, far = ins[3 * g : 3 * g + 3]
            for n, s in enumerate(which):
                rows = pl.ds(n * high, high)
                to = pl.multiple_of(behind(z, s) * high + PAD, PAD)
                for c in range(parts):
                    total = keep[c, rows, :].astype(jnp.float32)
                    total = total + near[c, rows, :].astype(jnp.float32)
                    total = total + far[c, rows, :].astype(jnp.float32)
                    seq[c, pl.ds(to, high), :] = total.astype(jnp.bfloat16).astype(jnp.float32)
        for i, up in enumerate(up_refs):
            to = pl.multiple_of((row ^ i) * high + PAD, PAD)
            cot[pl.ds(to, high), :] = up[...].astype(jnp.float32)

    operands = [a for group in groups for a in group] + list(ups)
    outs = [
        pltpu.VMEM((parts, tokens + 2 * PAD, block), jnp.float32),
        pltpu.VMEM((tokens + 2 * PAD, block), jnp.float32),
    ]
    return local(me, body, outs, operands, 0.6, late=late)


def gate(me, seq, cot, feature_taps, inner_taps, high, shards, one=None):
    lags, parts, _ = feature_taps.shape
    long_lags = inner_taps.shape[0]
    block = cot.shape[1]
    window = high + 2 * PAD
    ins = [seq, cot, feature_taps, inner_taps] + ([] if one is None else [one])

    def back(value, lag):
        return pltpu.roll(value, lag, 0) if lag else value

    def ahead(value, lag):
        return pltpu.roll(value, window - lag, 0) if lag else value

    def body(me_ref, seq_ref, cot_ref, taps_ref, long_ref, *refs):
        row, z = me_ref[0], me_ref[1]
        if one is not None:
            one_ref, all_ref, last_ref, two_ref = refs
            all_ref[0] = one_ref[...]

        @pl.loop(0, block // LANES)
        def _(half):
            lanes = pl.ds(pl.multiple_of(half * LANES, LANES), LANES)
            wide = pl.ds(pl.multiple_of(row * block + half * LANES, LANES), LANES)
            taps = [[taps_ref[s, c : c + 1, wide] for c in range(parts)] for s in range(lags)]
            long_taps = [long_ref[s : s + 1, wide] for s in range(long_lags)]
            for s in shards:
                rows = pl.ds(pl.multiple_of(behind(z, s) * high, PAD), window)
                mixed = []
                for c in range(parts):
                    proj = seq_ref[c, rows, lanes]
                    total = taps[0][c] * proj
                    for lag in range(1, lags):
                        total = total + taps[lag][c] * back(proj, lag)
                    mixed.append(total)
                query, key, value = mixed
                upstream = cot_ref[rows, lanes]
                product = (key * value).astype(jnp.bfloat16).astype(jnp.float32)
                inner = long_taps[0] * product
                for lag in range(1, long_lags):
                    inner = inner + long_taps[lag] * back(product, lag)
                grad_inner = upstream * query
                grad_product = long_taps[0] * grad_inner
                for lag in range(1, long_lags):
                    grad_product = grad_product + long_taps[lag] * ahead(grad_inner, lag)
                grads = (upstream * inner, grad_product * value, grad_product * key)
                for c, grad in enumerate(grads):
                    total = taps[0][c] * grad
                    for lag in range(1, lags):
                        total = total + taps[lag][c] * ahead(grad, lag)
                    done = total[PAD : PAD + high].astype(jnp.bfloat16)
                    if one is None:
                        refs[0][c, :, lanes] = done
                        continue
                    all_ref[(s - 1) % 4, c, :, lanes] = done
                    if s == 2:
                        two_ref[c, :, lanes] = done
                    else:
                        last_ref[(s - 3) % 4, c, :, lanes] = done

    single = (parts, high, block)
    outs = [bf16(*single)]
    if one is not None:
        outs = [bf16(4, *single), bf16(2, *single), *outs]
    return local(me, body, outs, ins, 0.8 * len(shards))


def relay(me, *values):
    return local(
        me,
        lambda *refs: None,
        [jax.ShapeDtypeStruct(value.shape, value.dtype) for value in values],
        values,
        0.1,
        [ANY] * len(values),
        out_specs=[ANY] * len(values),
        aliases={1 + i: 1 + i for i in range(len(values))},
    )


def input_grads(me, pieces, w, late=()):
    parts, depth, width = w.shape
    high, block = pieces[0][0].shape[-2:]
    shards = len(pieces[0][1])

    def body(me_ref, *refs):
        w_ref, outs, wide = refs[len(pieces)], refs[len(pieces) + 1 : -1], refs[-1]
        for i, (g, (_, which)) in enumerate(zip(refs, pieces)):
            at = pl.multiple_of((me_ref[0] ^ i) * block, LANES)
            for s, index in enumerate(which):
                shard = g if index is None else g.at[index]
                wide[:, s * high : (s + 1) * high, pl.ds(at, block)] = shard[...]
        total = None
        for c in range(parts):
            term = lax.dot_general(
                wide[c], w_ref[c], (((1,), (1,)), ((), ())), preferred_element_type=jnp.float32
            )
            total = term if total is None else total + term
        for s, out in enumerate(outs):
            out[...] = total[s * high : (s + 1) * high].astype(jnp.bfloat16)

    return local(
        me,
        body,
        [bf16(high, depth)] * shards,
        [*(g for g, _ in pieces), w],
        2.8 * shards,
        scratch=[pltpu.VMEM((parts, shards * high, width), jnp.bfloat16)],
        late=late,
    )


def turned(me, xs, late=()):
    high, depth = xs[0].shape

    def body(me_ref, *refs):
        for s, x in enumerate(refs[:-1]):
            refs[-1][:, s * high : (s + 1) * high] = x[...].T

    me, (out,) = local(me, body, [bf16(depth, high * len(xs))], xs, 0.4 * len(xs), late=late)
    return me, out


def weight_grads(me, done, xts, blocks, width):
    depth = xts[0].shape[0]
    flat = [p for _, pieces in blocks for p in pieces]
    parts, high, block = flat[0][0].shape[-3:]
    unique = []
    for g, _ in flat:
        if not any(g is u for u in unique):
            unique.append(g)
    spot = {id(u): n for n, u in enumerate(unique)}
    tokens = high * len(blocks[0][1])
    wide = block * len(blocks)
    cuts = 2
    tall = depth // cuts
    n_in = len(xts) + len(unique) + (done is not None)

    def body(me_ref, *refs):
        x_refs, g_refs = refs[: len(xts)], refs[len(xts) : n_in]
        out_ref, xt, gs, held, sems = refs[n_in:]
        at = 0
        for x in x_refs:
            xt[:, at : at + x.shape[1]] = x[...]
            at += x.shape[1]
        row = me_ref[0]
        start = pl.multiple_of((row ^ blocks[0][0]) // CORES * wide, wide)
        copies = []
        for c in range(parts):
            for i, pieces in blocks:
                lanes = pl.ds(pl.multiple_of((row ^ i) % CORES * block, LANES), block)
                for k, (g, index) in enumerate(pieces):
                    g_ref = g_refs[spot[id(g)]]
                    shard = g_ref if index is None else g_ref.at[index]
                    gs[c % 2, k * high : (k + 1) * high, lanes] = shard[c]
            for m in range(cuts):
                slot = len(copies) % 2
                if len(copies) >= 2:
                    copies[-2].wait()
                rows = pl.ds(m * tall, tall)
                held[slot] = jnp.dot(
                    xt[rows, :], gs[c % 2], preferred_element_type=jnp.float32
                )
                copies.append(
                    pltpu.make_async_copy(
                        held.at[slot], out_ref.at[c, rows, pl.ds(start, wide)], sems.at[slot]
                    )
                )
                copies[-1].start()
        for copy in copies[-2:]:
            copy.wait()

    ins = [*xts, *unique]
    specs = [VMEM] * len(ins)
    aliases = {}
    if done is not None:
        aliases = {1 + len(ins): 1}
        ins.append(done)
        specs.append(ANY)
    me, (out,) = local(
        me,
        body,
        [jax.ShapeDtypeStruct((parts, depth, width), jnp.float32)],
        ins,
        6.0,
        specs,
        scratch=[
            pltpu.VMEM((depth, tokens), jnp.bfloat16),
            pltpu.VMEM((2, tokens, wide), jnp.bfloat16),
            pltpu.VMEM((2, tall, wide), jnp.float32),
            pltpu.SemaphoreType.DMA((2,)),
        ],
        out_specs=[ANY],
        aliases=aliases,
    )
    return me, out


def total(me, terms, late=()):
    def body(me_ref, *refs):
        acc = refs[0][...].astype(jnp.float32)
        for ref in refs[1:-1]:
            acc = acc + ref[...].astype(jnp.float32)
        refs[-1][...] = acc.astype(jnp.bfloat16)

    me, (out,) = local(me, body, [bf16(*terms[0].shape)], terms, 0.5, late=late)
    return me, out


def by_channels(inputs, weights, feature_taps, inner_taps, grad_out):
    x_own = inputs[0]
    block = weights.shape[2] // lax.axis_size("row")
    width = weights.shape[2]
    me = jnp.stack([lax.axis_index("row"), lax.axis_index("col")]).astype(jnp.int32)

    def send(name, value, axis, step):
        with jax.named_scope(name):
            return along(value, step) if axis == "col" else swap(value, axis, step)

    x1, x3, x2 = [send("x%d" % step, x_own, "col", step) for step in (1, 3, 2)]
    with jax.named_scope("begin"):
        me, (w, x_own, there, here, across, *away) = begin(
            me, x_own, grad_out[0], jnp.transpose(weights, (1, 0, 2)), block
        )
    near = send("up_core", there, "row", 1)
    far = send("up_y", jnp.stack([across, near[1]]), "row", CORES)
    ups = [here, near[0], far[0], far[1]]

    def spread(me, name, xs, away, late=()):
        got = [send(name + "_core%d" % j, away[j], "row", 1) for j in range(2)]
        with jax.named_scope(name + "_keep"):
            me, keep = project(me, xs, w, block, 0)
        with jax.named_scope(name + "_join"):
            me, both = total(me, [keep[1], got[1]], late)
        return me, (keep[0], got[0], send(name + "_y", both, "row", CORES))

    me, group = spread(me, "proj0", [x_own], away)
    groups = [group]
    with jax.named_scope("proj13_away"):
        me, away = project(me, [x1, x3], w, block, 1, [group[1]])
    me, group = spread(me, "proj13", [x1, x3], away)
    groups.append(group)
    with jax.named_scope("proj13_turned"):
        me, xt0 = turned(me, [x_own, x1, x3])
    with jax.named_scope("proj2_away"):
        me, away = project(me, [x2], w, block, 1, [groups[0][2], far, group[1]])
    me, group = spread(me, "proj2", [x2], away)
    groups.append(group)
    with jax.named_scope("proj2_turned"):
        me, xt1 = turned(me, [x2], [groups[1][2], group[1]])
    xts = [xt0, xt1]
    others = [send("xt%d_x" % n, x, "dp", 1) for n, x in enumerate(xts)]

    with jax.named_scope("laid_out"):
        me, (seq, cot) = laid_out(me, groups, ((0,), (1, 3), (2,)), ups, others)
    high = x_own.shape[0]
    with jax.named_scope("gate1"):
        me, (g1,) = gate(me, seq, cot, feature_taps, inner_taps, high, (1,))
    y1 = send("g1_y", g1, "row", CORES)
    with jax.named_scope("gate230"):
        me, (g, g30, g2) = gate(me, seq, cot, feature_taps, inner_taps, high, (2, 3, 0), g1)
    y2, y30 = send("g2_y", g2, "row", CORES), send("g30_y", g30, "row", CORES)
    c, x = send("g_core", g, "row", 1), send("g_x", g, "dp", 1)
    cy1, cy2 = send("gy1_core", y1, "row", 1), send("gy2_core", y2, "row", 1)

    with jax.named_scope("input_grads1"):
        pieces = [(g, [0]), (c, [0]), (y1, [None]), (cy1, [None])]
        me, (share1,) = input_grads(me, pieces, w)
    passed = send("share1", share1, "col", 1)
    with jax.named_scope("input_grads2"):
        pieces = [(g, [1]), (c, [1]), (y2, [None]), (cy2, [None])]
        me, (share2,) = input_grads(me, pieces, w)
    with jax.named_scope("total2"):
        me, share2 = total(me, [share2, passed])
    passed = send("share2", share2, "col", 1)
    with jax.named_scope("relay"):
        me, (x, y30) = relay(me, x, y30)
    xy, cx, cy30 = send("gx_y", x, "row", CORES), send("gx_core", x, "row", 1), send("gy30_core", y30, "row", 1)
    with jax.named_scope("input_grads30"):
        pieces = [(g, [2, 3]), (c, [2, 3]), (y30, [0, 1]), (cy30, [0, 1])]
        me, (share3, share0) = input_grads(me, pieces, w)

    def whole(a):
        return [(a, 3), (a, 0), (a, 2), (a, 1)]

    def cut(last, one, two):
        return [(last, 1), (one, None), (last, 0), (two, None)]

    near_blocks = [(0, whole(g) + whole(x)), (1, whole(c) + whole(cx))]
    xts += others
    with jax.named_scope("weight_grads_near"):
        me, grad_w = weight_grads(me, None, xts, near_blocks, width)
    with jax.named_scope("total3"):
        me, share3 = total(me, [share3, passed])
    passed = send("share3", share3, "col", 1)
    with jax.named_scope("relay_xy"):
        me, (xy,) = relay(me, xy)
    cxy = send("gxy_core", xy, "row", 1)
    far_blocks = [(2, cut(y30, y1, y2) + whole(xy)), (3, cut(cy30, cy1, cy2) + whole(cxy))]
    with jax.named_scope("weight_grads_far"):
        me, grad_w = weight_grads(me, grad_w, xts, far_blocks, width)
    with jax.named_scope("total0"):
        me, grad_in = total(me, [share0, passed])
    return (grad_in[None], jnp.transpose(grad_w, (1, 0, 2)))


def solution(mesh):
    placed = (
        P("dp", "col", "row"),
        P("row", None, "col"),
        P(None, None, "col"),
        P(None, "col"),
        P("dp", "row", "col"),
    )

    def on_device(inputs, weights, feature_taps, inner_taps, grad_out):
        n_row = mesh.shape["row"]
        fits = weights.shape[2] % (n_row * LANES) == 0 and inputs.shape[1] % LANES == 0
        small = n_row == 2 * CORES and mesh.shape["dp"] == 2 and mesh.shape["col"] == 4
        plan = by_channels if fits and small else by_tokens
        return plan(inputs, weights, feature_taps, inner_taps, grad_out)

    return jax.shard_map(
        on_device,
        mesh=mesh,
        in_specs=placed,
        out_specs=(P("dp", "col", "row"), P("row", None, "col")),
        check_vma=False,
    )
```

```python
import math

import jax
import jax.numpy as jnp
from jax import lax
from jax.experimental import pallas as pl
from jax.experimental.pallas import tpu as pltpu
from jax.sharding import PartitionSpec as P

LANES = 128
PAD = 8
CORES = 2


def shifted(shard, axis, by):
    length = lax.axis_size(axis)
    pairs = [(i, i + by) for i in range(length) if 0 <= i + by < length]
    return lax.ppermute(shard, axis, pairs)


def with_halo(cells, axis, width):
    head = shifted(cells[:width], axis, -1)
    tail = shifted(cells[-width:], axis, 1)
    return jnp.concatenate([tail, cells, head], axis=0)


def causal(seq, taps):
    total = taps[0] * seq
    for lag in range(1, taps.shape[0]):
        pad = jnp.zeros((lag,) + seq.shape[1:], jnp.float32)
        total = total + taps[lag] * jnp.concatenate([pad, seq[:-lag]], axis=0)
    return total


def anticausal(seq, taps):
    total = taps[0] * seq
    for lag in range(1, taps.shape[0]):
        pad = jnp.zeros((lag,) + seq.shape[1:], jnp.float32)
        total = total + taps[lag] * jnp.concatenate([seq[lag:], pad], axis=0)
    return total


def rounded(value):
    return lax.optimization_barrier(value.astype(jnp.bfloat16)).astype(jnp.float32)


def by_tokens(inputs, weights, feature_taps, inner_taps, grad_out):
    tile = inputs[0]
    upstream_tile = grad_out[0]
    rows_dev = upstream_tile.shape[0]
    width_row = weights.shape[0]
    width_col = weights.shape[2]
    margin = feature_taps.shape[0] - 1 + (inner_taps.shape[0] - 1)
    flat_w = weights.reshape(width_row, 3 * width_col)
    columns = lax.all_gather(tile, "col", axis=0, tiled=True)
    proj = lax.psum_scatter(
        jnp.dot(columns, flat_w, preferred_element_type=jnp.float32).astype(jnp.bfloat16),
        "row",
        scatter_dimension=0,
        tiled=True,
    )
    length = rows_dev + 2 * margin
    window = with_halo(proj, "row", margin).astype(jnp.float32).reshape(length, 3, width_col)
    after = shifted(upstream_tile[:margin], "row", -1)
    upstream = jnp.concatenate(
        [
            jnp.zeros((margin, width_col), jnp.float32),
            upstream_tile.astype(jnp.float32),
            after.astype(jnp.float32),
        ],
        axis=0,
    )
    mixed = causal(window, feature_taps)
    query = mixed[:, 0]
    key = mixed[:, 1]
    value = mixed[:, 2]
    product = rounded(key * value)
    inner = causal(product, inner_taps)
    grad_query = upstream * inner
    grad_product = anticausal(upstream * query, inner_taps)
    grad_mixed = jnp.stack([grad_query, grad_product * value, grad_product * key], axis=1)
    grad_proj = anticausal(grad_mixed, feature_taps)[margin : margin + rows_dev].astype(
        jnp.bfloat16
    )
    gathered = lax.all_gather(grad_proj.reshape(rows_dev, 3 * width_col), "row", axis=0, tiled=True)
    grad_x = lax.psum_scatter(
        lax.dot_general(
            gathered, flat_w, (((1,), (1,)), ((), ())), preferred_element_type=jnp.float32
        ).astype(jnp.bfloat16),
        "col",
        scatter_dimension=0,
        tiled=True,
    )
    local = lax.dot_general(
        columns, gathered, (((0,), (0,)), ((), ())), preferred_element_type=jnp.float32
    )
    grad_w = lax.psum(local.astype(jnp.bfloat16), "dp").astype(jnp.float32)
    return (grad_x[None], grad_w.reshape(width_row, 3, width_col))


def swap(value, axis, step):
    size = lax.axis_size(axis)
    return lax.ppermute(value, axis, [(i, i ^ step) for i in range(size)])


LINE = (0, 2, 3, 1)


def along(value, steps):
    size = len(LINE)
    pairs = [(LINE[i], LINE[(i + steps) % size]) for i in range(size)]
    return lax.ppermute(value, "col", pairs)


def behind(z, steps):
    for _ in range(steps):
        z = jnp.where(z < 2, 2 * z + 1, 2 * z - 4)
    return z


VMEM = pl.BlockSpec(memory_space=pltpu.VMEM)
SMEM = pl.BlockSpec(memory_space=pltpu.SMEM)
HBM = pl.BlockSpec(memory_space=pltpu.HBM)
ANY = pl.BlockSpec(memory_space=pl.ANY)


PER_MICRO = 1.1e9


def hbm(value):
    return pltpu.with_memory_space_constraint(value, pltpu.HBM)


def bf16(*shape):
    return jax.ShapeDtypeStruct(shape, jnp.bfloat16)


def local(me, body, outs, ins, micros, in_specs=None, scratch=(), out_specs=None, aliases=None, late=()):
    place, *turn = me
    late = [*turn, *late]
    n_in = 1 + len(ins)

    def ordered(place_ref, *refs):
        body(place_ref, *refs[: len(ins)], *refs[len(ins) + len(late) + 1 :])

    turns = {n_in: 0} if turn else {}
    turn, *results = pl.pallas_call(
        ordered,
        out_shape=[jax.ShapeDtypeStruct((8, LANES), jnp.float32), *outs],
        in_specs=[SMEM, *(in_specs or [VMEM] * len(ins)), *[ANY] * len(late)],
        out_specs=[ANY, *(out_specs or [VMEM] * len(outs))],
        scratch_shapes=list(scratch),
        input_output_aliases={**turns, **{1 + i: 1 + o for i, o in (aliases or {}).items()}},
        compiler_params=pltpu.CompilerParams(vmem_limit_bytes=16 * 2**20),
        cost_estimate=pl.CostEstimate(
            flops=int(micros * PER_MICRO), bytes_accessed=1, transcendentals=0
        ),
    )(place, *ins, *late)
    return (place, turn), results


def multiply(x, w_ref, c, block_at, out_ref):
    block = out_ref.shape[-1]
    at = pl.multiple_of(block_at * block, LANES)
    out_ref[c] = jnp.dot(
        x, w_ref[c, :, pl.ds(at, block)], preferred_element_type=jnp.float32
    ).astype(jnp.bfloat16)


def begin(me, x, up, w, block):
    parts, depth, width = w.shape
    high = up.shape[0]

    def body(me_ref, x_hbm, up_hbm, w_hbm, *refs):
        w_ref, x_ref, there_ref, here_ref, across_ref, *away_refs, up_ref, sems = refs
        row = me_ref[0]
        loads = [pltpu.make_async_copy(up_hbm, up_ref, sems.at[0])]
        loads += [pltpu.make_async_copy(x_hbm, x_ref, sems.at[1])]
        loads += [
            pltpu.make_async_copy(w_hbm.at[c], w_ref.at[c], sems.at[2 + c]) for c in range(parts)
        ]
        for load in loads:
            load.start()
        loads[0].wait()
        for j in range(2):
            at = pl.multiple_of((row ^ (2 * j + 1)) * block, LANES)
            there_ref[j] = up_ref[:, pl.ds(at, block)]
        here_ref[...] = up_ref[:, pl.ds(pl.multiple_of(row * block, LANES), block)]
        across_ref[...] = up_ref[:, pl.ds(pl.multiple_of((row ^ 2) * block, LANES), block)]
        loads[1].wait()
        for c in range(parts):
            loads[2 + c].wait()
            for j in range(2):
                multiply(x_ref[...], w_ref, c, row ^ (2 * j + 1), away_refs[j])

    return local(
        me,
        body,
        [
            pltpu.VMEM(w.shape, w.dtype),
            pltpu.VMEM(x.shape, x.dtype),
            bf16(2, high, block),
            bf16(high, block),
            bf16(high, block),
            bf16(parts, high, block),
            bf16(parts, high, block),
        ],
        [hbm(x), hbm(up), hbm(w)],
        3.5,
        [HBM, HBM, HBM],
        scratch=[
            pltpu.VMEM(up.shape, up.dtype),
            pltpu.SemaphoreType.DMA((2 + parts,)),
        ],
    )


def project(me, xs, w, block, other, late=()):
    parts = w.shape[0]
    tall = xs[0].shape[0] * len(xs)

    def body(me_ref, *refs):
        w_ref, out_refs = refs[len(xs)], refs[len(xs) + 1 :]
        x = jnp.concatenate([x[...] for x in refs[: len(xs)]], axis=0)
        for j in (1, 0):
            for c in range(parts):
                multiply(x, w_ref, c, me_ref[0] ^ (2 * j + other), out_refs[j])

    outs = [bf16(parts, tall, block)] * 2
    return local(me, body, outs, [*xs, w], 1.2 * len(xs), late=late)


def laid_out(me, groups, shards, ups, late=()):
    parts, _, block = groups[0][2].shape
    tokens = sum(far.shape[1] for _, _, far in groups)
    high = ups[0].shape[0]
    n_in = 3 * len(groups)

    def body(me_ref, *refs):
        ins, up_refs, (seq, cot) = refs[:n_in], refs[n_in:-2], refs[-2:]
        row, z = me_ref[0], me_ref[1]
        for at in (0, PAD + tokens):
            seq[:, at : at + PAD, :] = jnp.zeros((parts, PAD, block), jnp.float32)
            cot[at : at + PAD, :] = jnp.zeros((PAD, block), jnp.float32)
        for g, which in enumerate(shards):
            keep, near, far = ins[3 * g : 3 * g + 3]
            for n, s in enumerate(which):
                rows = pl.ds(n * high, high)
                to = pl.multiple_of(behind(z, s) * high + PAD, PAD)
                for c in range(parts):
                    total = keep[c, rows, :].astype(jnp.float32)
                    total = total + near[c, rows, :].astype(jnp.float32)
                    total = total + far[c, rows, :].astype(jnp.float32)
                    seq[c, pl.ds(to, high), :] = total.astype(jnp.bfloat16).astype(jnp.float32)
        for i, up in enumerate(up_refs):
            to = pl.multiple_of((row ^ i) * high + PAD, PAD)
            cot[pl.ds(to, high), :] = up[...].astype(jnp.float32)

    operands = [a for group in groups for a in group] + list(ups)
    outs = [
        pltpu.VMEM((parts, tokens + 2 * PAD, block), jnp.float32),
        pltpu.VMEM((tokens + 2 * PAD, block), jnp.float32),
    ]
    return local(me, body, outs, operands, 0.6, late=late)


def gate(me, seq, cot, feature_taps, inner_taps, high, shards, one=None, late=()):
    lags, parts, _ = feature_taps.shape
    long_lags = inner_taps.shape[0]
    block = cot.shape[1]
    window = high + 2 * PAD
    ins = [seq, cot, feature_taps, inner_taps] + ([] if one is None else [one])

    def back(value, lag):
        return pltpu.roll(value, lag, 0) if lag else value

    def ahead(value, lag):
        return pltpu.roll(value, window - lag, 0) if lag else value

    def body(me_ref, seq_ref, cot_ref, taps_ref, long_ref, *refs):
        row, z = me_ref[0], me_ref[1]
        if one is not None:
            one_ref, all_ref, last_ref, two_ref = refs
            all_ref[0] = one_ref[...]

        @pl.loop(0, block // LANES)
        def _(half):
            lanes = pl.ds(pl.multiple_of(half * LANES, LANES), LANES)
            wide = pl.ds(pl.multiple_of(row * block + half * LANES, LANES), LANES)
            taps = [[taps_ref[s, c : c + 1, wide] for c in range(parts)] for s in range(lags)]
            long_taps = [long_ref[s : s + 1, wide] for s in range(long_lags)]
            for s in shards:
                rows = pl.ds(pl.multiple_of(behind(z, s) * high, PAD), window)
                mixed = []
                for c in range(parts):
                    proj = seq_ref[c, rows, lanes]
                    total = taps[0][c] * proj
                    for lag in range(1, lags):
                        total = total + taps[lag][c] * back(proj, lag)
                    mixed.append(total)
                query, key, value = mixed
                upstream = cot_ref[rows, lanes]
                product = (key * value).astype(jnp.bfloat16).astype(jnp.float32)
                inner = long_taps[0] * product
                for lag in range(1, long_lags):
                    inner = inner + long_taps[lag] * back(product, lag)
                grad_inner = upstream * query
                grad_product = long_taps[0] * grad_inner
                for lag in range(1, long_lags):
                    grad_product = grad_product + long_taps[lag] * ahead(grad_inner, lag)
                grads = (upstream * inner, grad_product * value, grad_product * key)
                for c, grad in enumerate(grads):
                    total = taps[0][c] * grad
                    for lag in range(1, lags):
                        total = total + taps[lag][c] * ahead(grad, lag)
                    done = total[PAD : PAD + high].astype(jnp.bfloat16)
                    if one is None:
                        refs[0][c, :, lanes] = done
                        continue
                    all_ref[(s - 1) % 4, c, :, lanes] = done
                    if s == 2:
                        two_ref[c, :, lanes] = done
                    else:
                        last_ref[(s - 3) % 4, c, :, lanes] = done

    single = (parts, high, block)
    outs = [bf16(*single)]
    if one is not None:
        outs = [bf16(4, *single), bf16(2, *single), *outs]
    return local(me, body, outs, ins, 0.8 * len(shards), late=late)


def relay(me, *values):
    return local(
        me,
        lambda *refs: None,
        [jax.ShapeDtypeStruct(value.shape, value.dtype) for value in values],
        values,
        0.1,
        [ANY] * len(values),
        out_specs=[ANY] * len(values),
        aliases={i: i for i in range(len(values))},
    )


def input_grads(me, pieces, w, late=()):
    parts, depth, width = w.shape
    high, block = pieces[0][0].shape[-2:]
    shards = len(pieces[0][1])

    def body(me_ref, *refs):
        w_ref, outs, wide = refs[len(pieces)], refs[len(pieces) + 1 : -1], refs[-1]
        for i, (g, (_, which)) in enumerate(zip(refs, pieces)):
            at = pl.multiple_of((me_ref[0] ^ i) * block, LANES)
            for s, index in enumerate(which):
                shard = g if index is None else g.at[index]
                wide[:, s * high : (s + 1) * high, pl.ds(at, block)] = shard[...]
        total = None
        for c in range(parts):
            term = lax.dot_general(
                wide[c], w_ref[c], (((1,), (1,)), ((), ())), preferred_element_type=jnp.float32
            )
            total = term if total is None else total + term
        for s, out in enumerate(outs):
            out[...] = total[s * high : (s + 1) * high].astype(jnp.bfloat16)

    return local(
        me,
        body,
        [bf16(high, depth)] * shards,
        [*(g for g, _ in pieces), w],
        0.8 * shards,
        scratch=[pltpu.VMEM((parts, shards * high, width), jnp.bfloat16)],
        late=late,
    )


def turned(me, xs, late=()):
    high, depth = xs[0].shape

    def body(me_ref, *refs):
        for s, x in enumerate(refs[:-1]):
            refs[-1][:, s * high : (s + 1) * high] = x[...].T

    me, (out,) = local(me, body, [bf16(depth, high * len(xs))], xs, 0.4 * len(xs), late=late)
    return me, out


def weight_grads(me, done, xts, blocks, width):
    depth = xts[0].shape[0]
    flat = [p for _, pieces in blocks for p in pieces]
    parts, high, block = flat[0][0].shape[-3:]
    unique = []
    for g, _ in flat:
        if not any(g is u for u in unique):
            unique.append(g)
    spot = {id(u): n for n, u in enumerate(unique)}
    tokens = high * len(blocks[0][1])
    wide = block * len(blocks)
    cuts = 2
    tall = depth // cuts
    n_in = len(xts) + len(unique) + (done is not None)

    def body(me_ref, *refs):
        x_refs, g_refs = refs[: len(xts)], refs[len(xts) : n_in]
        out_ref, xt, gs, held, sems = refs[n_in:]
        at = 0
        for x in x_refs:
            xt[:, at : at + x.shape[1]] = x[...]
            at += x.shape[1]
        row = me_ref[0]
        start = pl.multiple_of((row ^ blocks[0][0]) // CORES * wide, wide)
        copies = []
        for c in range(parts):
            for i, pieces in blocks:
                lanes = pl.ds(pl.multiple_of((row ^ i) % CORES * block, LANES), block)
                for k, (g, index) in enumerate(pieces):
                    g_ref = g_refs[spot[id(g)]]
                    shard = g_ref if index is None else g_ref.at[index]
                    gs[c % 2, k * high : (k + 1) * high, lanes] = shard[c]
            for m in range(cuts):
                slot = len(copies) % 2
                if len(copies) >= 2:
                    copies[-2].wait()
                rows = pl.ds(m * tall, tall)
                held[slot] = jnp.dot(
                    xt[rows, :], gs[c % 2], preferred_element_type=jnp.float32
                )
                copies.append(
                    pltpu.make_async_copy(
                        held.at[slot], out_ref.at[c, rows, pl.ds(start, wide)], sems.at[slot]
                    )
                )
                copies[-1].start()
        for copy in copies[-2:]:
            copy.wait()

    ins = [*xts, *unique]
    specs = [VMEM] * len(ins)
    aliases = {}
    if done is not None:
        aliases = {len(ins): 0}
        ins.append(done)
        specs.append(ANY)
    me, (out,) = local(
        me,
        body,
        [jax.ShapeDtypeStruct((parts, depth, width), jnp.float32)],
        ins,
        6.0,
        specs,
        scratch=[
            pltpu.VMEM((depth, tokens), jnp.bfloat16),
            pltpu.VMEM((2, tokens, wide), jnp.bfloat16),
            pltpu.VMEM((2, tall, wide), jnp.float32),
            pltpu.SemaphoreType.DMA((2,)),
        ],
        out_specs=[ANY],
        aliases=aliases,
    )
    return me, out


def total(me, terms, late=()):
    def body(me_ref, *refs):
        acc = refs[0][...].astype(jnp.float32)
        for ref in refs[1:-1]:
            acc = acc + ref[...].astype(jnp.float32)
        refs[-1][...] = acc.astype(jnp.bfloat16)

    me, (out,) = local(me, body, [bf16(*terms[0].shape)], terms, 0.5, late=late)
    return me, out


def by_channels(inputs, weights, feature_taps, inner_taps, grad_out):
    x_own = inputs[0]
    block = weights.shape[2] // lax.axis_size("row")
    width = weights.shape[2]
    me = (jnp.stack([lax.axis_index("row"), lax.axis_index("col")]).astype(jnp.int32),)

    def send(name, value, axis, step):
        with jax.named_scope(name):
            return along(value, step) if axis == "col" else swap(value, axis, step)

    x1, x3, x2 = [send("x%d" % step, x_own, "col", step) for step in (1, 3, 2)]
    with jax.named_scope("begin"):
        me, (w, x_own, there, here, across, *away) = begin(
            me, x_own, grad_out[0], jnp.transpose(weights, (1, 0, 2)), block
        )
    def spread(me, name, xs, away, late, soon=()):
        got = [send(name + "_core%d" % j, away[j], "row", 1) for j in range(2)]
        with jax.named_scope(name + "_keep"):
            me, keep = project(me, xs, w, block, 0, soon)
        with jax.named_scope(name + "_turned"):
            me, xt = turned(me, xs)
        xts.append(xt)
        others.append(send(name + "_xt_x", xt, "dp", 1))
        with jax.named_scope(name + "_join"):
            me, both = total(me, [keep[1], got[1]], [got[0], *late])
        groups.append((keep[0], got[0], send(name + "_y", both, "row", CORES)))
        return me

    groups, xts, others = [], [], []
    me = spread(me, "proj0", [x_own], away, [])
    with jax.named_scope("relay_up"):
        me, (there,) = relay(me, there)
    near = send("up_core", there, "row", 1)
    far = send("up_y", jnp.stack([across, near[1]]), "row", CORES)
    ups = [here, near[0], far[0], far[1]]
    with jax.named_scope("proj13_away"):
        me, away = project(me, [x1, x3], w, block, 1)
    me = spread(me, "proj13", [x1, x3], away, [], [groups[0][2], others[0], near])
    with jax.named_scope("proj2_away"):
        me, away = project(me, [x2], w, block, 1, [far])
    me = spread(me, "proj2", [x2], away, [groups[1][2]])
    with jax.named_scope("laid_out"):
        me, (seq, cot) = laid_out(me, groups, ((0,), (1, 3), (2,)), ups, others[1:2])
    high = x_own.shape[0]
    with jax.named_scope("gate1"):
        me, (g1,) = gate(me, seq, cot, feature_taps, inner_taps, high, (1,))
    y1 = send("g1_y", g1, "row", CORES)
    with jax.named_scope("gate230"):
        me, (g, g30, g2) = gate(
            me, seq, cot, feature_taps, inner_taps, high, (2, 3, 0), g1, others[2:]
        )
    y2, y30 = send("g2_y", g2, "row", CORES), send("g30_y", g30, "row", CORES)
    c, x = send("g_core", g, "row", 1), send("g_x", g, "dp", 1)
    cy1, cy2 = send("gy1_core", y1, "row", 1), send("gy2_core", y2, "row", 1)

    with jax.named_scope("input_grads1"):
        pieces = [(g, [0]), (c, [0]), (y1, [None]), (cy1, [None])]
        me, (share1,) = input_grads(me, pieces, w)
    passed = send("share1", share1, "col", 1)
    with jax.named_scope("input_grads2"):
        pieces = [(g, [1]), (c, [1]), (y2, [None]), (cy2, [None])]
        me, (share2,) = input_grads(me, pieces, w)
    with jax.named_scope("total2"):
        me, share2 = total(me, [share2, passed])
    passed = send("share2", share2, "col", 1)
    with jax.named_scope("relay"):
        me, (x, y30) = relay(me, x, y30)
    xy, cx, cy30 = send("gx_y", x, "row", CORES), send("gx_core", x, "row", 1), send("gy30_core", y30, "row", 1)
    with jax.named_scope("input_grads30"):
        pieces = [(g, [2, 3]), (c, [2, 3]), (y30, [0, 1]), (cy30, [0, 1])]
        me, (share3, share0) = input_grads(me, pieces, w)

    def whole(a):
        return [(a, 3), (a, 0), (a, 2), (a, 1)]

    def cut(last, one, two):
        return [(last, 1), (one, None), (last, 0), (two, None)]

    near_blocks = [(0, whole(g) + whole(x)), (1, whole(c) + whole(cx))]
    xts += others
    with jax.named_scope("weight_grads_near"):
        me, grad_w = weight_grads(me, None, xts, near_blocks, width)
    with jax.named_scope("total3"):
        me, share3 = total(me, [share3, passed])
    passed = send("share3", share3, "col", 1)
    with jax.named_scope("relay_xy"):
        me, (xy,) = relay(me, xy)
    cxy = send("gxy_core", xy, "row", 1)
    far_blocks = [(2, cut(y30, y1, y2) + whole(xy)), (3, cut(cy30, cy1, cy2) + whole(cxy))]
    with jax.named_scope("weight_grads_far"):
        me, grad_w = weight_grads(me, grad_w, xts, far_blocks, width)
    with jax.named_scope("total0"):
        me, grad_in = total(me, [share0, passed])
    return (grad_in[None], jnp.transpose(grad_w, (1, 0, 2)))


def solution(mesh):
    placed = (
        P("dp", "col", "row"),
        P("row", None, "col"),
        P(None, None, "col"),
        P(None, "col"),
        P("dp", "row", "col"),
    )

    def on_device(inputs, weights, feature_taps, inner_taps, grad_out):
        n_row = mesh.shape["row"]
        fits = weights.shape[2] % (n_row * LANES) == 0 and inputs.shape[1] % LANES == 0
        small = n_row == 2 * CORES and mesh.shape["dp"] == 2 and mesh.shape["col"] == 4
        plan = by_channels if fits and small else by_tokens
        return plan(inputs, weights, feature_taps, inner_taps, grad_out)

    return jax.shard_map(
        on_device,
        mesh=mesh,
        in_specs=placed,
        out_specs=(P("dp", "col", "row"), P("row", None, "col")),
        check_vma=False,
    )
```

```python
import math

import jax
import jax.numpy as jnp
from jax import lax
from jax.experimental import pallas as pl
from jax.experimental.pallas import tpu as pltpu
from jax.sharding import PartitionSpec as P

LANES = 128
PAD = 8
CORES = 2


def shifted(shard, axis, by):
    length = lax.axis_size(axis)
    pairs = [(i, i + by) for i in range(length) if 0 <= i + by < length]
    return lax.ppermute(shard, axis, pairs)


def with_halo(cells, axis, width):
    head = shifted(cells[:width], axis, -1)
    tail = shifted(cells[-width:], axis, 1)
    return jnp.concatenate([tail, cells, head], axis=0)


def causal(seq, taps):
    total = taps[0] * seq
    for lag in range(1, taps.shape[0]):
        pad = jnp.zeros((lag,) + seq.shape[1:], jnp.float32)
        total = total + taps[lag] * jnp.concatenate([pad, seq[:-lag]], axis=0)
    return total


def anticausal(seq, taps):
    total = taps[0] * seq
    for lag in range(1, taps.shape[0]):
        pad = jnp.zeros((lag,) + seq.shape[1:], jnp.float32)
        total = total + taps[lag] * jnp.concatenate([seq[lag:], pad], axis=0)
    return total


def rounded(value):
    return lax.optimization_barrier(value.astype(jnp.bfloat16)).astype(jnp.float32)


def by_tokens(inputs, weights, feature_taps, inner_taps, grad_out):
    tile = inputs[0]
    upstream_tile = grad_out[0]
    rows_dev = upstream_tile.shape[0]
    width_row = weights.shape[0]
    width_col = weights.shape[2]
    margin = feature_taps.shape[0] - 1 + (inner_taps.shape[0] - 1)
    flat_w = weights.reshape(width_row, 3 * width_col)
    columns = lax.all_gather(tile, "col", axis=0, tiled=True)
    proj = lax.psum_scatter(
        jnp.dot(columns, flat_w, preferred_element_type=jnp.float32).astype(jnp.bfloat16),
        "row",
        scatter_dimension=0,
        tiled=True,
    )
    length = rows_dev + 2 * margin
    window = with_halo(proj, "row", margin).astype(jnp.float32).reshape(length, 3, width_col)
    after = shifted(upstream_tile[:margin], "row", -1)
    upstream = jnp.concatenate(
        [
            jnp.zeros((margin, width_col), jnp.float32),
            upstream_tile.astype(jnp.float32),
            after.astype(jnp.float32),
        ],
        axis=0,
    )
    mixed = causal(window, feature_taps)
    query = mixed[:, 0]
    key = mixed[:, 1]
    value = mixed[:, 2]
    product = rounded(key * value)
    inner = causal(product, inner_taps)
    grad_query = upstream * inner
    grad_product = anticausal(upstream * query, inner_taps)
    grad_mixed = jnp.stack([grad_query, grad_product * value, grad_product * key], axis=1)
    grad_proj = anticausal(grad_mixed, feature_taps)[margin : margin + rows_dev].astype(
        jnp.bfloat16
    )
    gathered = lax.all_gather(grad_proj.reshape(rows_dev, 3 * width_col), "row", axis=0, tiled=True)
    grad_x = lax.psum_scatter(
        lax.dot_general(
            gathered, flat_w, (((1,), (1,)), ((), ())), preferred_element_type=jnp.float32
        ).astype(jnp.bfloat16),
        "col",
        scatter_dimension=0,
        tiled=True,
    )
    local = lax.dot_general(
        columns, gathered, (((0,), (0,)), ((), ())), preferred_element_type=jnp.float32
    )
    grad_w = lax.psum(local.astype(jnp.bfloat16), "dp").astype(jnp.float32)
    return (grad_x[None], grad_w.reshape(width_row, 3, width_col))


def swap(value, axis, step):
    size = lax.axis_size(axis)
    return lax.ppermute(value, axis, [(i, i ^ step) for i in range(size)])


LINE = (0, 2, 3, 1)


def along(value, steps):
    size = len(LINE)
    pairs = [(LINE[i], LINE[(i + steps) % size]) for i in range(size)]
    return lax.ppermute(value, "col", pairs)


def behind(z, steps):
    for _ in range(steps):
        z = jnp.where(z < 2, 2 * z + 1, 2 * z - 4)
    return z


VMEM = pl.BlockSpec(memory_space=pltpu.VMEM)
SMEM = pl.BlockSpec(memory_space=pltpu.SMEM)
HBM = pl.BlockSpec(memory_space=pltpu.HBM)
ANY = pl.BlockSpec(memory_space=pl.ANY)


PER_MICRO = 1.1e9


def hbm(value):
    return pltpu.with_memory_space_constraint(value, pltpu.HBM)


def bf16(*shape):
    return jax.ShapeDtypeStruct(shape, jnp.bfloat16)


def local(
    me, body, outs, ins, micros, in_specs=None, scratch=(), out_specs=None, aliases=None, late=(), placed=True
):
    place, *turn = me
    first = [place] if placed else []
    late = [*turn, *late]
    n_in = len(first) + len(ins)

    def ordered(*refs):
        body(*refs[:n_in], *refs[n_in + len(late) + 1 :])

    turns = {n_in: 0} if turn else {}
    moved = {len(first) + i: 1 + o for i, o in (aliases or {}).items()}
    turn, *results = pl.pallas_call(
        ordered,
        out_shape=[jax.ShapeDtypeStruct((8, LANES), jnp.float32), *outs],
        in_specs=[SMEM] * len(first) + [*(in_specs or [VMEM] * len(ins)), *[ANY] * len(late)],
        out_specs=[ANY, *(out_specs or [VMEM] * len(outs))],
        scratch_shapes=list(scratch),
        input_output_aliases={**turns, **moved},
        compiler_params=pltpu.CompilerParams(vmem_limit_bytes=16 * 2**20),
        cost_estimate=pl.CostEstimate(
            flops=int(micros * PER_MICRO), bytes_accessed=1, transcendentals=0
        ),
    )(*first, *ins, *late)
    return (place, turn), results


def multiply(x, w_ref, c, block_at, out_ref):
    block = out_ref.shape[-1]
    at = pl.multiple_of(block_at * block, LANES)
    out_ref[c] = jnp.dot(
        x, w_ref[c, :, pl.ds(at, block)], preferred_element_type=jnp.float32
    ).astype(jnp.bfloat16)


def begin(me, x, up, w, block):
    parts, depth, width = w.shape
    high = up.shape[0]

    def body(me_ref, x_hbm, up_hbm, w_hbm, *refs):
        w_ref, x_ref, there_ref, here_ref, across_ref, *away_refs, place_ref, up_ref, sems = refs
        row = me_ref[0]
        place_ref[0] = row
        place_ref[1] = me_ref[1]
        loads = [pltpu.make_async_copy(up_hbm, up_ref, sems.at[0])]
        loads += [pltpu.make_async_copy(x_hbm, x_ref, sems.at[1])]
        loads += [
            pltpu.make_async_copy(w_hbm.at[c], w_ref.at[c], sems.at[2 + c]) for c in range(parts)
        ]
        for load in loads:
            load.start()
        loads[0].wait()
        for j in range(2):
            at = pl.multiple_of((row ^ (2 * j + 1)) * block, LANES)
            there_ref[j] = up_ref[:, pl.ds(at, block)]
        here_ref[...] = up_ref[:, pl.ds(pl.multiple_of(row * block, LANES), block)]
        across_ref[...] = up_ref[:, pl.ds(pl.multiple_of((row ^ 2) * block, LANES), block)]
        loads[1].wait()
        for c in range(parts):
            loads[2 + c].wait()
            for j in range(2):
                multiply(x_ref[...], w_ref, c, row ^ (2 * j + 1), away_refs[j])

    return local(
        me,
        body,
        [
            pltpu.VMEM(w.shape, w.dtype),
            pltpu.VMEM(x.shape, x.dtype),
            bf16(2, high, block),
            bf16(high, block),
            bf16(high, block),
            bf16(parts, high, block),
            bf16(parts, high, block),
            pltpu.SMEM((2,), jnp.int32),
        ],
        [hbm(x), hbm(up), hbm(w)],
        3.5,
        [HBM, HBM, HBM],
        out_specs=[VMEM] * 7 + [SMEM],
        scratch=[
            pltpu.VMEM(up.shape, up.dtype),
            pltpu.SemaphoreType.DMA((2 + parts,)),
        ],
    )


def project(me, xs, w, block, other, late=()):
    parts = w.shape[0]
    tall = xs[0].shape[0] * len(xs)

    def body(me_ref, *refs):
        w_ref, out_refs = refs[len(xs)], refs[len(xs) + 1 :]
        x = jnp.concatenate([x[...] for x in refs[: len(xs)]], axis=0)
        for j in (1, 0):
            for c in range(parts):
                multiply(x, w_ref, c, me_ref[0] ^ (2 * j + other), out_refs[j])

    outs = [bf16(parts, tall, block)] * 2
    return local(me, body, outs, [*xs, w], 1.2 * len(xs), late=late)


def laid_out(me, groups, shards, ups, late=()):
    parts, _, block = groups[0][2].shape
    tokens = sum(far.shape[1] for _, _, far in groups)
    high = ups[0].shape[0]
    n_in = 3 * len(groups)

    def body(me_ref, *refs):
        ins, up_refs, (seq, cot) = refs[:n_in], refs[n_in:-2], refs[-2:]
        row, z = me_ref[0], me_ref[1]
        for at in (0, PAD + tokens):
            seq[:, at : at + PAD, :] = jnp.zeros((parts, PAD, block), jnp.float32)
            cot[at : at + PAD, :] = jnp.zeros((PAD, block), jnp.float32)
        for g, which in enumerate(shards):
            keep, near, far = ins[3 * g : 3 * g + 3]
            for n, s in enumerate(which):
                rows = pl.ds(n * high, high)
                to = pl.multiple_of(behind(z, s) * high + PAD, PAD)
                for c in range(parts):
                    total = keep[c, rows, :].astype(jnp.float32)
                    total = total + near[c, rows, :].astype(jnp.float32)
                    total = total + far[c, rows, :].astype(jnp.float32)
                    seq[c, pl.ds(to, high), :] = total.astype(jnp.bfloat16).astype(jnp.float32)
        for i, up in enumerate(up_refs):
            to = pl.multiple_of((row ^ i) * high + PAD, PAD)
            cot[pl.ds(to, high), :] = up[...].astype(jnp.float32)

    operands = [a for group in groups for a in group] + list(ups)
    outs = [
        pltpu.VMEM((parts, tokens + 2 * PAD, block), jnp.float32),
        pltpu.VMEM((tokens + 2 * PAD, block), jnp.float32),
    ]
    return local(me, body, outs, operands, 0.6, late=late)


def gate(me, seq, cot, feature_taps, inner_taps, high, shards, one=None, late=()):
    lags, parts, _ = feature_taps.shape
    long_lags = inner_taps.shape[0]
    block = cot.shape[1]
    window = high + 2 * PAD
    ins = [seq, cot, feature_taps, inner_taps] + ([] if one is None else [one])

    def back(value, lag):
        return pltpu.roll(value, lag, 0) if lag else value

    def ahead(value, lag):
        return pltpu.roll(value, window - lag, 0) if lag else value

    def body(me_ref, seq_ref, cot_ref, taps_ref, long_ref, *refs):
        row, z = me_ref[0], me_ref[1]
        if one is not None:
            one_ref, all_ref, last_ref, two_ref = refs
            all_ref[0] = one_ref[...]

        @pl.loop(0, block // LANES)
        def _(half):
            lanes = pl.ds(pl.multiple_of(half * LANES, LANES), LANES)
            wide = pl.ds(pl.multiple_of(row * block + half * LANES, LANES), LANES)
            taps = [[taps_ref[s, c : c + 1, wide] for c in range(parts)] for s in range(lags)]
            long_taps = [long_ref[s : s + 1, wide] for s in range(long_lags)]
            for s in shards:
                rows = pl.ds(pl.multiple_of(behind(z, s) * high, PAD), window)
                mixed = []
                for c in range(parts):
                    proj = seq_ref[c, rows, lanes]
                    total = taps[0][c] * proj
                    for lag in range(1, lags):
                        total = total + taps[lag][c] * back(proj, lag)
                    mixed.append(total)
                query, key, value = mixed
                upstream = cot_ref[rows, lanes]
                product = (key * value).astype(jnp.bfloat16).astype(jnp.float32)
                inner = long_taps[0] * product
                for lag in range(1, long_lags):
                    inner = inner + long_taps[lag] * back(product, lag)
                grad_inner = upstream * query
                grad_product = long_taps[0] * grad_inner
                for lag in range(1, long_lags):
                    grad_product = grad_product + long_taps[lag] * ahead(grad_inner, lag)
                grads = (upstream * inner, grad_product * value, grad_product * key)
                for c, grad in enumerate(grads):
                    total = taps[0][c] * grad
                    for lag in range(1, lags):
                        total = total + taps[lag][c] * ahead(grad, lag)
                    done = total[PAD : PAD + high].astype(jnp.bfloat16)
                    if one is None:
                        refs[0][c, :, lanes] = done
                        continue
                    all_ref[(s - 1) % 4, c, :, lanes] = done
                    if s == 2:
                        two_ref[c, :, lanes] = done
                    else:
                        last_ref[(s - 3) % 4, c, :, lanes] = done

    single = (parts, high, block)
    outs = [bf16(*single)]
    if one is not None:
        outs = [bf16(4, *single), bf16(2, *single), *outs]
    return local(me, body, outs, ins, 0.8 * len(shards), late=late)


def relay(me, *values, late=()):
    return local(
        me,
        lambda *refs: None,
        [jax.ShapeDtypeStruct(value.shape, value.dtype) for value in values],
        values,
        0.1,
        [ANY] * len(values),
        out_specs=[ANY] * len(values),
        aliases={i: i for i in range(len(values))},
        late=late,
        placed=False,
    )


def input_grads(me, pieces, w, late=()):
    parts, depth, width = w.shape
    high, block = pieces[0][0].shape[-2:]
    shards = len(pieces[0][1])

    def body(me_ref, *refs):
        w_ref, outs, wide = refs[len(pieces)], refs[len(pieces) + 1 : -1], refs[-1]
        for i, (g, (_, which)) in enumerate(zip(refs, pieces)):
            at = pl.multiple_of((me_ref[0] ^ i) * block, LANES)
            for s, index in enumerate(which):
                shard = g if index is None else g.at[index]
                wide[:, s * high : (s + 1) * high, pl.ds(at, block)] = shard[...]
        total = None
        for c in range(parts):
            term = lax.dot_general(
                wide[c], w_ref[c], (((1,), (1,)), ((), ())), preferred_element_type=jnp.float32
            )
            total = term if total is None else total + term
        for s, out in enumerate(outs):
            out[...] = total[s * high : (s + 1) * high].astype(jnp.bfloat16)

    return local(
        me,
        body,
        [bf16(high, depth)] * shards,
        [*(g for g, _ in pieces), w],
        0.8 * shards,
        scratch=[pltpu.VMEM((parts, shards * high, width), jnp.bfloat16)],
        late=late,
    )


def turned(me, xs):
    high, depth = xs[0].shape

    def body(*refs):
        for s, x in enumerate(refs[:-1]):
            refs[-1][:, s * high : (s + 1) * high] = x[...].T

    me, (out,) = local(me, body, [bf16(depth, high * len(xs))], xs, 0.4 * len(xs), placed=False)
    return me, out


def weight_grads(me, done, xts, blocks, width):
    depth = xts[0].shape[0]
    flat = [p for _, pieces in blocks for p in pieces]
    parts, high, block = flat[0][0].shape[-3:]
    unique = []
    for g, _ in flat:
        if not any(g is u for u in unique):
            unique.append(g)
    spot = {id(u): n for n, u in enumerate(unique)}
    tokens = high * len(blocks[0][1])
    wide = block * len(blocks)
    cuts, spare = 4, 4
    tall = depth // cuts
    n_in = len(xts) + len(unique) + (done is not None)

    def body(me_ref, *refs):
        x_refs, g_refs = refs[: len(xts)], refs[len(xts) : n_in]
        out_ref, xt, gs, held, sems = refs[n_in:]
        at = 0
        for x in x_refs:
            xt[:, at : at + x.shape[1]] = x[...]
            at += x.shape[1]
        row = me_ref[0]
        start = pl.multiple_of((row ^ blocks[0][0]) // CORES * wide, wide)
        copies = []
        for c in range(parts):
            for i, pieces in blocks:
                lanes = pl.ds(pl.multiple_of((row ^ i) % CORES * block, LANES), block)
                for k, (g, index) in enumerate(pieces):
                    g_ref = g_refs[spot[id(g)]]
                    shard = g_ref if index is None else g_ref.at[index]
                    gs[c % 2, k * high : (k + 1) * high, lanes] = shard[c]
            for m in range(cuts):
                slot = len(copies) % spare
                if len(copies) >= spare:
                    copies[-spare].wait()
                rows = pl.ds(m * tall, tall)
                held[slot] = jnp.dot(
                    xt[rows, :], gs[c % 2], preferred_element_type=jnp.float32
                )
                copies.append(
                    pltpu.make_async_copy(
                        held.at[slot], out_ref.at[c, rows, pl.ds(start, wide)], sems.at[slot]
                    )
                )
                copies[-1].start()
        for copy in copies[-spare:]:
            copy.wait()

    ins = [*xts, *unique]
    specs = [VMEM] * len(ins)
    aliases = {}
    if done is not None:
        aliases = {len(ins): 0}
        ins.append(done)
        specs.append(ANY)
    me, (out,) = local(
        me,
        body,
        [jax.ShapeDtypeStruct((parts, depth, width), jnp.float32)],
        ins,
        6.0,
        specs,
        scratch=[
            pltpu.VMEM((depth, tokens), jnp.bfloat16),
            pltpu.VMEM((2, tokens, wide), jnp.bfloat16),
            pltpu.VMEM((spare, tall, wide), jnp.float32),
            pltpu.SemaphoreType.DMA((spare,)),
        ],
        out_specs=[ANY],
        aliases=aliases,
    )
    return me, out


def total(me, terms, late=()):
    def body(*refs):
        acc = refs[0][...].astype(jnp.float32)
        for ref in refs[1:-1]:
            acc = acc + ref[...].astype(jnp.float32)
        refs[-1][...] = acc.astype(jnp.bfloat16)

    me, (out,) = local(me, body, [bf16(*terms[0].shape)], terms, 0.5, late=late, placed=False)
    return me, out


def by_channels(inputs, weights, feature_taps, inner_taps, grad_out):
    x_own = inputs[0]
    block = weights.shape[2] // lax.axis_size("row")
    width = weights.shape[2]
    me = (jnp.stack([lax.axis_index("row"), lax.axis_index("col")]).astype(jnp.int32),)

    def send(name, value, axis, step):
        with jax.named_scope(name):
            return along(value, step) if axis == "col" else swap(value, axis, step)

    x1, x3, x2 = [send("x%d" % step, x_own, "col", step) for step in (1, 3, 2)]
    with jax.named_scope("begin"):
        me, (w, x_own, there, here, across, *away, place) = begin(
            me, x_own, grad_out[0], jnp.transpose(weights, (1, 0, 2)), block
        )
    me = (place, *me[1:])
    def spread(me, name, xs, away, late, soon=()):
        got = [send(name + "_core%d" % j, away[j], "row", 1) for j in range(2)]
        with jax.named_scope(name + "_keep"):
            me, keep = project(me, xs, w, block, 0, soon)
        with jax.named_scope(name + "_turned"):
            me, xt = turned(me, xs)
        xts.append(xt)
        others.append(send(name + "_xt_x", xt, "dp", 1))
        with jax.named_scope(name + "_join"):
            me, both = total(me, [keep[1], got[1]], [got[0], *late])
        groups.append((keep[0], got[0], send(name + "_y", both, "row", CORES)))
        return me

    groups, xts, others = [], [], []
    me = spread(me, "proj0", [x_own], away, [])
    with jax.named_scope("relay_up"):
        me, (there,) = relay(me, there)
    near = send("up_core", there, "row", 1)
    far = send("up_y", jnp.stack([across, near[1]]), "row", CORES)
    ups = [here, near[0], far[0], far[1]]
    with jax.named_scope("proj13_away"):
        me, away = project(me, [x1, x3], w, block, 1)
    me = spread(me, "proj13", [x1, x3], away, [], [groups[0][2], others[0], near])
    with jax.named_scope("proj2_away"):
        me, away = project(me, [x2], w, block, 1, [far])
    me = spread(me, "proj2", [x2], away, [groups[1][2]])
    with jax.named_scope("laid_out"):
        me, (seq, cot) = laid_out(me, groups, ((0,), (1, 3), (2,)), ups, others[1:2])
    high = x_own.shape[0]
    with jax.named_scope("gate1"):
        me, (g1,) = gate(me, seq, cot, feature_taps, inner_taps, high, (1,))
    y1 = send("g1_y", g1, "row", CORES)
    with jax.named_scope("gate230"):
        me, (g, g30, g2) = gate(
            me, seq, cot, feature_taps, inner_taps, high, (2, 3, 0), g1, others[2:]
        )
    with jax.named_scope("relay_g"):
        me, (g2, g30) = relay(me, g2, g30, late=[y1])
    y2, y30 = send("g2_y", g2, "row", CORES), send("g30_y", g30, "row", CORES)
    c, x = send("g_core", g, "row", 1), send("g_x", g, "dp", 1)
    cy1, cy2 = send("gy1_core", y1, "row", 1), send("gy2_core", y2, "row", 1)

    with jax.named_scope("input_grads1"):
        pieces = [(g, [0]), (c, [0]), (y1, [None]), (cy1, [None])]
        me, (share1,) = input_grads(me, pieces, w)
    passed = send("share1", share1, "col", 1)
    with jax.named_scope("input_grads2"):
        pieces = [(g, [1]), (c, [1]), (y2, [None]), (cy2, [None])]
        me, (share2,) = input_grads(me, pieces, w)
    with jax.named_scope("total2"):
        me, share2 = total(me, [share2, passed])
    passed = send("share2", share2, "col", 1)
    with jax.named_scope("relay"):
        me, (x, y30) = relay(me, x, y30)
    xy12, xy30 = send("gx12_y", x[:2], "row", CORES), send("gy30_x", y30, "dp", 1)
    cx, cy30 = send("gx_core", x, "row", 1), send("gy30_core", y30, "row", 1)
    with jax.named_scope("input_grads30"):
        pieces = [(g, [2, 3]), (c, [2, 3]), (y30, [0, 1]), (cy30, [0, 1])]
        me, (share3, share0) = input_grads(me, pieces, w)

    def whole(a):
        return [(a, 3), (a, 0), (a, 2), (a, 1)]

    def cut(last, one, two):
        return [(last, 1), (one, None), (last, 0), (two, None)]

    near_blocks = [(0, whole(g) + whole(x)), (1, whole(c) + whole(cx))]
    xts += others
    with jax.named_scope("weight_grads_near"):
        me, grad_w = weight_grads(me, None, xts, near_blocks, width)
    with jax.named_scope("total3"):
        me, share3 = total(me, [share3, passed])
    passed = send("share3", share3, "col", 1)
    with jax.named_scope("relay_xy"):
        me, (xy12, xy30) = relay(me, xy12, xy30)
    cxy12, cxy30 = send("gxy12_core", xy12, "row", 1), send("gxy30_core", xy30, "row", 1)

    def halves(low, high):
        return [(high, 1), (low, 0), (high, 0), (low, 1)]

    far_blocks = [
        (2, cut(y30, y1, y2) + halves(xy12, xy30)),
        (3, cut(cy30, cy1, cy2) + halves(cxy12, cxy30)),
    ]
    with jax.named_scope("weight_grads_far"):
        me, grad_w = weight_grads(me, grad_w, xts, far_blocks, width)
    with jax.named_scope("total0"):
        me, grad_in = total(me, [share0, passed])
    return (grad_in[None], jnp.transpose(grad_w, (1, 0, 2)))


def solution(mesh):
    placed = (
        P("dp", "col", "row"),
        P("row", None, "col"),
        P(None, None, "col"),
        P(None, "col"),
        P("dp", "row", "col"),
    )

    def on_device(inputs, weights, feature_taps, inner_taps, grad_out):
        n_row = mesh.shape["row"]
        fits = weights.shape[2] % (n_row * LANES) == 0 and inputs.shape[1] % LANES == 0
        small = n_row == 2 * CORES and mesh.shape["dp"] == 2 and mesh.shape["col"] == 4
        plan = by_channels if fits and small else by_tokens
        return plan(inputs, weights, feature_taps, inner_taps, grad_out)

    return jax.shard_map(
        on_device,
        mesh=mesh,
        in_specs=placed,
        out_specs=(P("dp", "col", "row"), P("row", None, "col")),
        check_vma=False,
    )
```

```python
import math

import jax
import jax.numpy as jnp
from jax import lax
from jax.experimental import pallas as pl
from jax.experimental.pallas import tpu as pltpu
from jax.sharding import PartitionSpec as P

LANES = 128
PAD = 8
CORES = 2


def shifted(shard, axis, by):
    length = lax.axis_size(axis)
    pairs = [(i, i + by) for i in range(length) if 0 <= i + by < length]
    return lax.ppermute(shard, axis, pairs)


def with_halo(cells, axis, width):
    head = shifted(cells[:width], axis, -1)
    tail = shifted(cells[-width:], axis, 1)
    return jnp.concatenate([tail, cells, head], axis=0)


def causal(seq, taps):
    total = taps[0] * seq
    for lag in range(1, taps.shape[0]):
        pad = jnp.zeros((lag,) + seq.shape[1:], jnp.float32)
        total = total + taps[lag] * jnp.concatenate([pad, seq[:-lag]], axis=0)
    return total


def anticausal(seq, taps):
    total = taps[0] * seq
    for lag in range(1, taps.shape[0]):
        pad = jnp.zeros((lag,) + seq.shape[1:], jnp.float32)
        total = total + taps[lag] * jnp.concatenate([seq[lag:], pad], axis=0)
    return total


def rounded(value):
    return lax.optimization_barrier(value.astype(jnp.bfloat16)).astype(jnp.float32)


def by_tokens(inputs, weights, feature_taps, inner_taps, grad_out):
    tile = inputs[0]
    upstream_tile = grad_out[0]
    rows_dev = upstream_tile.shape[0]
    width_row = weights.shape[0]
    width_col = weights.shape[2]
    margin = feature_taps.shape[0] - 1 + (inner_taps.shape[0] - 1)
    flat_w = weights.reshape(width_row, 3 * width_col)
    columns = lax.all_gather(tile, "col", axis=0, tiled=True)
    proj = lax.psum_scatter(
        jnp.dot(columns, flat_w, preferred_element_type=jnp.float32).astype(jnp.bfloat16),
        "row",
        scatter_dimension=0,
        tiled=True,
    )
    length = rows_dev + 2 * margin
    window = with_halo(proj, "row", margin).astype(jnp.float32).reshape(length, 3, width_col)
    after = shifted(upstream_tile[:margin], "row", -1)
    upstream = jnp.concatenate(
        [
            jnp.zeros((margin, width_col), jnp.float32),
            upstream_tile.astype(jnp.float32),
            after.astype(jnp.float32),
        ],
        axis=0,
    )
    mixed = causal(window, feature_taps)
    query = mixed[:, 0]
    key = mixed[:, 1]
    value = mixed[:, 2]
    product = rounded(key * value)
    inner = causal(product, inner_taps)
    grad_query = upstream * inner
    grad_product = anticausal(upstream * query, inner_taps)
    grad_mixed = jnp.stack([grad_query, grad_product * value, grad_product * key], axis=1)
    grad_proj = anticausal(grad_mixed, feature_taps)[margin : margin + rows_dev].astype(
        jnp.bfloat16
    )
    gathered = lax.all_gather(grad_proj.reshape(rows_dev, 3 * width_col), "row", axis=0, tiled=True)
    grad_x = lax.psum_scatter(
        lax.dot_general(
            gathered, flat_w, (((1,), (1,)), ((), ())), preferred_element_type=jnp.float32
        ).astype(jnp.bfloat16),
        "col",
        scatter_dimension=0,
        tiled=True,
    )
    local = lax.dot_general(
        columns, gathered, (((0,), (0,)), ((), ())), preferred_element_type=jnp.float32
    )
    grad_w = lax.psum(local.astype(jnp.bfloat16), "dp").astype(jnp.float32)
    return (grad_x[None], grad_w.reshape(width_row, 3, width_col))


def swap(value, axis, step):
    size = lax.axis_size(axis)
    return lax.ppermute(value, axis, [(i, i ^ step) for i in range(size)])


LINE = (0, 2, 3, 1)


def along(value, steps):
    size = len(LINE)
    pairs = [(LINE[i], LINE[(i + steps) % size]) for i in range(size)]
    return lax.ppermute(value, "col", pairs)


def behind(z, steps):
    for _ in range(steps):
        z = jnp.where(z < 2, 2 * z + 1, 2 * z - 4)
    return z


VMEM = pl.BlockSpec(memory_space=pltpu.VMEM)
SMEM = pl.BlockSpec(memory_space=pltpu.SMEM)
HBM = pl.BlockSpec(memory_space=pltpu.HBM)
ANY = pl.BlockSpec(memory_space=pl.ANY)


PER_MICRO = 1.1e9


def hbm(value):
    return pltpu.with_memory_space_constraint(value, pltpu.HBM)


def bf16(*shape):
    return jax.ShapeDtypeStruct(shape, jnp.bfloat16)


def local(
    me, body, outs, ins, micros, in_specs=None, scratch=(), out_specs=None, aliases=None, late=(), placed=True
):
    place, *turn = me
    first = [place] if placed else []
    late = [*turn, *late]
    n_in = len(first) + len(ins)

    def ordered(*refs):
        body(*refs[:n_in], *refs[n_in + len(late) + 1 :])

    turns = {n_in: 0} if turn else {}
    moved = {len(first) + i: 1 + o for i, o in (aliases or {}).items()}
    turn, *results = pl.pallas_call(
        ordered,
        out_shape=[jax.ShapeDtypeStruct((8, LANES), jnp.float32), *outs],
        in_specs=[SMEM] * len(first) + [*(in_specs or [VMEM] * len(ins)), *[ANY] * len(late)],
        out_specs=[ANY, *(out_specs or [VMEM] * len(outs))],
        scratch_shapes=list(scratch),
        input_output_aliases={**turns, **moved},
        compiler_params=pltpu.CompilerParams(vmem_limit_bytes=16 * 2**20),
        cost_estimate=pl.CostEstimate(
            flops=int(micros * PER_MICRO), bytes_accessed=1, transcendentals=0
        ),
    )(*first, *ins, *late)
    return (place, turn), results


def multiply(x, w_ref, c, block_at, out_ref):
    block = out_ref.shape[-1]
    at = pl.multiple_of(block_at * block, LANES)
    out_ref[c] = jnp.dot(
        x, w_ref[c, :, pl.ds(at, block)], preferred_element_type=jnp.float32
    ).astype(jnp.bfloat16)


def begin(me, x, up, w, block):
    parts, depth, width = w.shape
    high = up.shape[0]

    def body(me_ref, x_hbm, up_hbm, w_hbm, *refs):
        w_ref, x_ref, there_ref, here_ref, across_ref, *away_refs, place_ref, up_ref, sems = refs
        row = me_ref[0]
        place_ref[0] = row
        place_ref[1] = me_ref[1]
        loads = [pltpu.make_async_copy(up_hbm, up_ref, sems.at[0])]
        loads += [pltpu.make_async_copy(x_hbm, x_ref, sems.at[1])]
        loads += [
            pltpu.make_async_copy(w_hbm.at[c], w_ref.at[c], sems.at[2 + c]) for c in range(parts)
        ]
        for load in loads:
            load.start()
        loads[0].wait()
        for j in range(2):
            at = pl.multiple_of((row ^ (2 * j + 1)) * block, LANES)
            there_ref[j] = up_ref[:, pl.ds(at, block)]
        here_ref[...] = up_ref[:, pl.ds(pl.multiple_of(row * block, LANES), block)]
        across_ref[...] = up_ref[:, pl.ds(pl.multiple_of((row ^ 2) * block, LANES), block)]
        loads[1].wait()
        for c in range(parts):
            loads[2 + c].wait()
            for j in range(2):
                multiply(x_ref[...], w_ref, c, row ^ (2 * j + 1), away_refs[j])

    return local(
        me,
        body,
        [
            pltpu.VMEM(w.shape, w.dtype),
            pltpu.VMEM(x.shape, x.dtype),
            bf16(2, high, block),
            bf16(high, block),
            bf16(high, block),
            bf16(parts, high, block),
            bf16(parts, high, block),
            pltpu.SMEM((2,), jnp.int32),
        ],
        [hbm(x), hbm(up), hbm(w)],
        3.5,
        [HBM, HBM, HBM],
        out_specs=[VMEM] * 7 + [SMEM],
        scratch=[
            pltpu.VMEM(up.shape, up.dtype),
            pltpu.SemaphoreType.DMA((2 + parts,)),
        ],
    )


def project(me, xs, w, block, other, late=()):
    parts = w.shape[0]
    tall = xs[0].shape[0] * len(xs)

    def body(me_ref, *refs):
        w_ref, out_refs = refs[len(xs)], refs[len(xs) + 1 :]
        x = jnp.concatenate([x[...] for x in refs[: len(xs)]], axis=0)
        for j in (1, 0):
            for c in range(parts):
                multiply(x, w_ref, c, me_ref[0] ^ (2 * j + other), out_refs[j])

    outs = [bf16(parts, tall, block)] * 2
    return local(me, body, outs, [*xs, w], 2.0 * len(xs), late=late)


def laid_out(me, groups, ups, late=()):
    parts, _, block = groups[0][2].shape
    tokens = sum(far.shape[1] for _, _, far in groups)
    high = ups[0].shape[0]
    n_in = 3 * len(groups)

    def body(me_ref, *refs):
        ins, up_refs, (seq, cot) = refs[:n_in], refs[n_in:-2], refs[-2:]
        row, z = me_ref[0], me_ref[1]
        for at in (0, PAD + tokens):
            seq[:, at : at + PAD, :] = jnp.zeros((parts, PAD, block), jnp.float32)
            cot[at : at + PAD, :] = jnp.zeros((PAD, block), jnp.float32)
        for s in range(len(groups)):
            keep, near, far = ins[3 * s : 3 * s + 3]
            to = pl.multiple_of(behind(z, s) * high + PAD, PAD)
            for c in range(parts):
                total = keep[c].astype(jnp.float32) + near[c].astype(jnp.float32)
                total = total + far[c].astype(jnp.float32)
                seq[c, pl.ds(to, high), :] = total.astype(jnp.bfloat16).astype(jnp.float32)
        for i, up in enumerate(up_refs):
            to = pl.multiple_of((row ^ i) * high + PAD, PAD)
            cot[pl.ds(to, high), :] = up[...].astype(jnp.float32)

    operands = [a for group in groups for a in group] + list(ups)
    outs = [
        pltpu.VMEM((parts, tokens + 2 * PAD, block), jnp.float32),
        pltpu.VMEM((tokens + 2 * PAD, block), jnp.float32),
    ]
    return local(me, body, outs, operands, 0.6, late=late)


def gate(me, seq, cot, feature_taps, inner_taps, high, shards, one=None, late=()):
    lags, parts, _ = feature_taps.shape
    long_lags = inner_taps.shape[0]
    block = cot.shape[1]
    window = high + 2 * PAD
    ins = [seq, cot, feature_taps, inner_taps] + ([] if one is None else [one])

    def back(value, lag):
        return pltpu.roll(value, lag, 0) if lag else value

    def ahead(value, lag):
        return pltpu.roll(value, window - lag, 0) if lag else value

    def body(me_ref, seq_ref, cot_ref, taps_ref, long_ref, *refs):
        row, z = me_ref[0], me_ref[1]
        if one is not None:
            one_ref, all_ref, last_ref, two_ref = refs
            all_ref[0] = one_ref[...]

        @pl.loop(0, block // LANES)
        def _(half):
            lanes = pl.ds(pl.multiple_of(half * LANES, LANES), LANES)
            wide = pl.ds(pl.multiple_of(row * block + half * LANES, LANES), LANES)
            taps = [[taps_ref[s, c : c + 1, wide] for c in range(parts)] for s in range(lags)]
            long_taps = [long_ref[s : s + 1, wide] for s in range(long_lags)]
            for s in shards:
                rows = pl.ds(pl.multiple_of(behind(z, s) * high, PAD), window)
                mixed = []
                for c in range(parts):
                    proj = seq_ref[c, rows, lanes]
                    total = taps[0][c] * proj
                    for lag in range(1, lags):
                        total = total + taps[lag][c] * back(proj, lag)
                    mixed.append(total)
                query, key, value = mixed
                upstream = cot_ref[rows, lanes]
                product = (key * value).astype(jnp.bfloat16).astype(jnp.float32)
                inner = long_taps[0] * product
                for lag in range(1, long_lags):
                    inner = inner + long_taps[lag] * back(product, lag)
                grad_inner = upstream * query
                grad_product = long_taps[0] * grad_inner
                for lag in range(1, long_lags):
                    grad_product = grad_product + long_taps[lag] * ahead(grad_inner, lag)
                grads = (upstream * inner, grad_product * value, grad_product * key)
                for c, grad in enumerate(grads):
                    total = taps[0][c] * grad
                    for lag in range(1, lags):
                        total = total + taps[lag][c] * ahead(grad, lag)
                    done = total[PAD : PAD + high].astype(jnp.bfloat16)
                    if one is None:
                        refs[0][c, :, lanes] = done
                        continue
                    all_ref[(s - 1) % 4, c, :, lanes] = done
                    if s == 2:
                        two_ref[c, :, lanes] = done
                    else:
                        last_ref[(s - 3) % 4, c, :, lanes] = done

    single = (parts, high, block)
    outs = [bf16(*single)]
    if one is not None:
        outs = [bf16(4, *single), bf16(2, *single), *outs]
    return local(me, body, outs, ins, 0.8 * len(shards), late=late)


def relay(me, *values, late=()):
    return local(
        me,
        lambda *refs: None,
        [jax.ShapeDtypeStruct(value.shape, value.dtype) for value in values],
        values,
        0.01,
        [ANY] * len(values),
        out_specs=[ANY] * len(values),
        aliases={i: i for i in range(len(values))},
        late=late,
        placed=False,
    )


def input_grads(me, pieces, w, late=()):
    parts, depth, width = w.shape
    high, block = pieces[0][0].shape[-2:]
    shards = len(pieces[0][1])

    def body(me_ref, *refs):
        w_ref, outs, wide = refs[len(pieces)], refs[len(pieces) + 1 : -1], refs[-1]
        for i, (g, (_, which)) in enumerate(zip(refs, pieces)):
            at = pl.multiple_of((me_ref[0] ^ i) * block, LANES)
            for s, index in enumerate(which):
                shard = g if index is None else g.at[index]
                wide[:, s * high : (s + 1) * high, pl.ds(at, block)] = shard[...]
        total = None
        for c in range(parts):
            term = lax.dot_general(
                wide[c], w_ref[c], (((1,), (1,)), ((), ())), preferred_element_type=jnp.float32
            )
            total = term if total is None else total + term
        for s, out in enumerate(outs):
            out[...] = total[s * high : (s + 1) * high].astype(jnp.bfloat16)

    return local(
        me,
        body,
        [bf16(high, depth)] * shards,
        [*(g for g, _ in pieces), w],
        0.8 * shards,
        scratch=[pltpu.VMEM((parts, shards * high, width), jnp.bfloat16)],
        late=late,
    )


def turned(me, xs):
    high, depth = xs[0].shape

    def body(*refs):
        for s, x in enumerate(refs[:-1]):
            refs[-1][:, s * high : (s + 1) * high] = x[...].T

    me, (out,) = local(me, body, [bf16(depth, high * len(xs))], xs, 0.1 * len(xs), placed=False)
    return me, out


def weight_grads(me, done, xts, blocks, width):
    depth = xts[0].shape[0]
    flat = [p for _, pieces in blocks for p in pieces]
    parts, high, block = flat[0][0].shape[-3:]
    unique = []
    for g, _ in flat:
        if not any(g is u for u in unique):
            unique.append(g)
    spot = {id(u): n for n, u in enumerate(unique)}
    tokens = high * len(blocks[0][1])
    wide = block * len(blocks)
    cuts, spare = 4, 4
    tall = depth // cuts
    n_in = len(xts) + len(unique) + (done is not None)

    def body(me_ref, *refs):
        x_refs, g_refs = refs[: len(xts)], refs[len(xts) : n_in]
        out_ref, xt, gs, held, sems = refs[n_in:]
        at = 0
        for x in x_refs:
            xt[:, at : at + x.shape[1]] = x[...]
            at += x.shape[1]
        row = me_ref[0]
        start = pl.multiple_of((row ^ blocks[0][0]) // CORES * wide, wide)
        copies = []
        for c in range(parts):
            for i, pieces in blocks:
                lanes = pl.ds(pl.multiple_of((row ^ i) % CORES * block, LANES), block)
                for k, (g, index) in enumerate(pieces):
                    g_ref = g_refs[spot[id(g)]]
                    shard = g_ref if index is None else g_ref.at[index]
                    gs[c % 2, k * high : (k + 1) * high, lanes] = shard[c]
            for m in range(cuts):
                slot = len(copies) % spare
                if len(copies) >= spare:
                    copies[-spare].wait()
                rows = pl.ds(m * tall, tall)
                held[slot] = jnp.dot(
                    xt[rows, :], gs[c % 2], preferred_element_type=jnp.float32
                )
                copies.append(
                    pltpu.make_async_copy(
                        held.at[slot], out_ref.at[c, rows, pl.ds(start, wide)], sems.at[slot]
                    )
                )
                copies[-1].start()
        for copy in copies[-spare:]:
            copy.wait()

    ins = [*xts, *unique]
    specs = [VMEM] * len(ins)
    aliases = {}
    if done is not None:
        aliases = {len(ins): 0}
        ins.append(done)
        specs.append(ANY)
    me, (out,) = local(
        me,
        body,
        [jax.ShapeDtypeStruct((parts, depth, width), jnp.float32)],
        ins,
        6.0,
        specs,
        scratch=[
            pltpu.VMEM((depth, tokens), jnp.bfloat16),
            pltpu.VMEM((2, tokens, wide), jnp.bfloat16),
            pltpu.VMEM((spare, tall, wide), jnp.float32),
            pltpu.SemaphoreType.DMA((spare,)),
        ],
        out_specs=[ANY],
        aliases=aliases,
    )
    return me, out


def total(me, terms, late=()):
    def body(*refs):
        acc = refs[0][...].astype(jnp.float32)
        for ref in refs[1:-1]:
            acc = acc + ref[...].astype(jnp.float32)
        refs[-1][...] = acc.astype(jnp.bfloat16)

    me, (out,) = local(me, body, [bf16(*terms[0].shape)], terms, 0.05, late=late, placed=False)
    return me, out


def by_channels(inputs, weights, feature_taps, inner_taps, grad_out):
    x_own = inputs[0]
    block = weights.shape[2] // lax.axis_size("row")
    width = weights.shape[2]
    me = (jnp.stack([lax.axis_index("row"), lax.axis_index("col")]).astype(jnp.int32),)

    def send(name, value, axis, step):
        with jax.named_scope(name):
            return along(value, step) if axis == "col" else swap(value, axis, step)

    x1 = send("x1", x_own, "col", 1)
    x2 = send("x2", x1, "col", 1)
    x3 = send("x3", x2, "col", 1)
    with jax.named_scope("begin"):
        me, (w, x_own, there, here, across, *away, place) = begin(
            me, x_own, grad_out[0], jnp.transpose(weights, (1, 0, 2)), block
        )
    me = (place, *me[1:])
    def spread(me, name, x, away, turn, late, soon=()):
        got = [send(name + "_core%d" % j, away[j], "row", 1) for j in range(2)]
        with jax.named_scope(name + "_keep"):
            me, keep = project(me, [x], w, block, 0, soon)
        if turn:
            with jax.named_scope(name + "_turned"):
                me, xt = turned(me, turn)
            xts.append(xt)
            others.append(send(name + "_xt_x", xt, "dp", 1))
        with jax.named_scope(name + "_join"):
            me, both = total(me, [keep[1], got[1]], [got[0], *late])
        groups.append((keep[0], got[0], send(name + "_y", both, "row", CORES)))
        return me

    groups, xts, others = [], [], []
    me = spread(me, "proj0", x_own, away, [], [])
    with jax.named_scope("relay_up"):
        me, (there,) = relay(me, there)
    near = send("up_core", there, "row", 1)
    far = send("up_y", jnp.stack([across, near[1]]), "row", CORES)
    ups = [here, near[0], far[0], far[1]]
    with jax.named_scope("proj1_away"):
        me, away = project(me, [x1], w, block, 1)
    me = spread(me, "proj1", x1, away, [x_own, x1], [], [groups[0][2], near])
    with jax.named_scope("proj2_away"):
        me, away = project(me, [x2], w, block, 1, [far])
    me = spread(me, "proj2", x2, away, [x2], [], [groups[1][2]])
    with jax.named_scope("proj3_away"):
        me, away = project(me, [x3], w, block, 1, [others[0]])
    me = spread(me, "proj3", x3, away, [x3], [], [groups[2][2]])
    with jax.named_scope("laid_out"):
        me, (seq, cot) = laid_out(me, groups, ups, others[1:2])
    high = x_own.shape[0]
    with jax.named_scope("gate1"):
        me, (g1,) = gate(me, seq, cot, feature_taps, inner_taps, high, (1,))
    y1 = send("g1_y", g1, "row", CORES)
    with jax.named_scope("gate230"):
        me, (g, g30, g2) = gate(
            me, seq, cot, feature_taps, inner_taps, high, (2, 3, 0), g1, others[2:]
        )
    with jax.named_scope("relay_g"):
        me, (g2, g30) = relay(me, g2, g30, late=[y1])
    y2, y30 = send("g2_y", g2, "row", CORES), send("g30_y", g30, "row", CORES)
    c, x = send("g_core", g, "row", 1), send("g_x", g, "dp", 1)
    cy1, cy2 = send("gy1_core", y1, "row", 1), send("gy2_core", y2, "row", 1)

    with jax.named_scope("input_grads1"):
        pieces = [(g, [0]), (c, [0]), (y1, [None]), (cy1, [None])]
        me, (share1,) = input_grads(me, pieces, w)
    passed = send("share1", share1, "col", 1)
    with jax.named_scope("input_grads2"):
        pieces = [(g, [1]), (c, [1]), (y2, [None]), (cy2, [None])]
        me, (share2,) = input_grads(me, pieces, w)
    with jax.named_scope("total2"):
        me, share2 = total(me, [share2, passed])
    passed = send("share2", share2, "col", 1)
    with jax.named_scope("relay"):
        me, (x, y30) = relay(me, x, y30)
    xy12, xy30 = send("gx12_y", x[:2], "row", CORES), send("gy30_x", y30, "dp", 1)
    cx, cy30 = send("gx_core", x, "row", 1), send("gy30_core", y30, "row", 1)
    with jax.named_scope("input_grads30"):
        pieces = [(g, [2, 3]), (c, [2, 3]), (y30, [0, 1]), (cy30, [0, 1])]
        me, (share3, share0) = input_grads(me, pieces, w)

    def whole(a):
        return [(a, 3), (a, 0), (a, 1), (a, 2)]

    def cut(last, one, two):
        return [(last, 1), (one, None), (two, None), (last, 0)]

    near_blocks = [(0, whole(g) + whole(x)), (1, whole(c) + whole(cx))]
    xts += others
    with jax.named_scope("weight_grads_near"):
        me, grad_w = weight_grads(me, None, xts, near_blocks, width)
    with jax.named_scope("total3"):
        me, share3 = total(me, [share3, passed])
    passed = send("share3", share3, "col", 1)
    with jax.named_scope("relay_xy"):
        me, (xy12, xy30) = relay(me, xy12, xy30)
    cxy12, cxy30 = send("gxy12_core", xy12, "row", 1), send("gxy30_core", xy30, "row", 1)

    def halves(low, high):
        return [(high, 1), (low, 0), (low, 1), (high, 0)]

    far_blocks = [
        (2, cut(y30, y1, y2) + halves(xy12, xy30)),
        (3, cut(cy30, cy1, cy2) + halves(cxy12, cxy30)),
    ]
    with jax.named_scope("weight_grads_far"):
        me, grad_w = weight_grads(me, grad_w, xts, far_blocks, width)
    with jax.named_scope("total0"):
        me, grad_in = total(me, [share0, passed])
    return (grad_in[None], jnp.transpose(grad_w, (1, 0, 2)))


def solution(mesh):
    placed = (
        P("dp", "col", "row"),
        P("row", None, "col"),
        P(None, None, "col"),
        P(None, "col"),
        P("dp", "row", "col"),
    )

    def on_device(inputs, weights, feature_taps, inner_taps, grad_out):
        n_row = mesh.shape["row"]
        fits = weights.shape[2] % (n_row * LANES) == 0 and inputs.shape[1] % LANES == 0
        small = n_row == 2 * CORES and mesh.shape["dp"] == 2 and mesh.shape["col"] == 4
        plan = by_channels if fits and small else by_tokens
        return plan(inputs, weights, feature_taps, inner_taps, grad_out)

    return jax.shard_map(
        on_device,
        mesh=mesh,
        in_specs=placed,
        out_specs=(P("dp", "col", "row"), P("row", None, "col")),
        check_vma=False,
    )
```

```python
import math

import jax
import jax.numpy as jnp
from jax import lax
from jax.experimental import pallas as pl
from jax.experimental.pallas import tpu as pltpu
from jax.sharding import PartitionSpec as P

LANES = 128
PAD = 8
CORES = 2


def shifted(shard, axis, by):
    length = lax.axis_size(axis)
    pairs = [(i, i + by) for i in range(length) if 0 <= i + by < length]
    return lax.ppermute(shard, axis, pairs)


def with_halo(cells, axis, width):
    head = shifted(cells[:width], axis, -1)
    tail = shifted(cells[-width:], axis, 1)
    return jnp.concatenate([tail, cells, head], axis=0)


def causal(seq, taps):
    total = taps[0] * seq
    for lag in range(1, taps.shape[0]):
        pad = jnp.zeros((lag,) + seq.shape[1:], jnp.float32)
        total = total + taps[lag] * jnp.concatenate([pad, seq[:-lag]], axis=0)
    return total


def anticausal(seq, taps):
    total = taps[0] * seq
    for lag in range(1, taps.shape[0]):
        pad = jnp.zeros((lag,) + seq.shape[1:], jnp.float32)
        total = total + taps[lag] * jnp.concatenate([seq[lag:], pad], axis=0)
    return total


def rounded(value):
    return lax.optimization_barrier(value.astype(jnp.bfloat16)).astype(jnp.float32)


def by_tokens(inputs, weights, feature_taps, inner_taps, grad_out):
    tile = inputs[0]
    upstream_tile = grad_out[0]
    rows_dev = upstream_tile.shape[0]
    width_row = weights.shape[0]
    width_col = weights.shape[2]
    margin = feature_taps.shape[0] - 1 + (inner_taps.shape[0] - 1)
    flat_w = weights.reshape(width_row, 3 * width_col)
    columns = lax.all_gather(tile, "col", axis=0, tiled=True)
    proj = lax.psum_scatter(
        jnp.dot(columns, flat_w, preferred_element_type=jnp.float32).astype(jnp.bfloat16),
        "row",
        scatter_dimension=0,
        tiled=True,
    )
    length = rows_dev + 2 * margin
    window = with_halo(proj, "row", margin).astype(jnp.float32).reshape(length, 3, width_col)
    after = shifted(upstream_tile[:margin], "row", -1)
    upstream = jnp.concatenate(
        [
            jnp.zeros((margin, width_col), jnp.float32),
            upstream_tile.astype(jnp.float32),
            after.astype(jnp.float32),
        ],
        axis=0,
    )
    mixed = causal(window, feature_taps)
    query = mixed[:, 0]
    key = mixed[:, 1]
    value = mixed[:, 2]
    product = rounded(key * value)
    inner = causal(product, inner_taps)
    grad_query = upstream * inner
    grad_product = anticausal(upstream * query, inner_taps)
    grad_mixed = jnp.stack([grad_query, grad_product * value, grad_product * key], axis=1)
    grad_proj = anticausal(grad_mixed, feature_taps)[margin : margin + rows_dev].astype(
        jnp.bfloat16
    )
    gathered = lax.all_gather(grad_proj.reshape(rows_dev, 3 * width_col), "row", axis=0, tiled=True)
    grad_x = lax.psum_scatter(
        lax.dot_general(
            gathered, flat_w, (((1,), (1,)), ((), ())), preferred_element_type=jnp.float32
        ).astype(jnp.bfloat16),
        "col",
        scatter_dimension=0,
        tiled=True,
    )
    local = lax.dot_general(
        columns, gathered, (((0,), (0,)), ((), ())), preferred_element_type=jnp.float32
    )
    grad_w = lax.psum(local.astype(jnp.bfloat16), "dp").astype(jnp.float32)
    return (grad_x[None], grad_w.reshape(width_row, 3, width_col))


def swap(value, axis, step):
    size = lax.axis_size(axis)
    return lax.ppermute(value, axis, [(i, i ^ step) for i in range(size)])


LINE = (0, 2, 3, 1)


def along(value, steps):
    size = len(LINE)
    pairs = [(LINE[i], LINE[(i + steps) % size]) for i in range(size)]
    return lax.ppermute(value, "col", pairs)


def behind(z, steps):
    for _ in range(steps):
        z = jnp.where(z < 2, 2 * z + 1, 2 * z - 4)
    return z


VMEM = pl.BlockSpec(memory_space=pltpu.VMEM)
SMEM = pl.BlockSpec(memory_space=pltpu.SMEM)
HBM = pl.BlockSpec(memory_space=pltpu.HBM)
ANY = pl.BlockSpec(memory_space=pl.ANY)


PER_MICRO = 1.1e9


def hbm(value):
    return pltpu.with_memory_space_constraint(value, pltpu.HBM)


def bf16(*shape):
    return jax.ShapeDtypeStruct(shape, jnp.bfloat16)


def local(
    me, body, outs, ins, micros, in_specs=None, scratch=(), out_specs=None, aliases=None, late=(), placed=True
):
    place, *turn = me
    first = [place] if placed else []
    late = [*turn, *late]
    n_in = len(first) + len(ins)

    def ordered(*refs):
        body(*refs[:n_in], *refs[n_in + len(late) + 1 :])

    turns = {n_in: 0} if turn else {}
    moved = {len(first) + i: 1 + o for i, o in (aliases or {}).items()}
    turn, *results = pl.pallas_call(
        ordered,
        out_shape=[jax.ShapeDtypeStruct((8, LANES), jnp.float32), *outs],
        in_specs=[SMEM] * len(first) + [*(in_specs or [VMEM] * len(ins)), *[ANY] * len(late)],
        out_specs=[ANY, *(out_specs or [VMEM] * len(outs))],
        scratch_shapes=list(scratch),
        input_output_aliases={**turns, **moved},
        compiler_params=pltpu.CompilerParams(vmem_limit_bytes=16 * 2**20),
        cost_estimate=pl.CostEstimate(
            flops=int(micros * PER_MICRO), bytes_accessed=1, transcendentals=0
        ),
    )(*first, *ins, *late)
    return (place, turn), results


def multiply(x, w_ref, c, block_at, out_ref):
    block = out_ref.shape[-1]
    at = pl.multiple_of(block_at * block, LANES)
    out_ref[c] = jnp.dot(
        x, w_ref[c, :, pl.ds(at, block)], preferred_element_type=jnp.float32
    ).astype(jnp.bfloat16)


def begin(me, x, up, w, block):
    parts, depth, width = w.shape
    high = up.shape[0]

    def body(me_ref, x_hbm, up_hbm, w_hbm, *refs):
        w_ref, x_ref, there_ref, here_ref, across_ref, *away_refs, place_ref, up_ref, sems = refs
        row = me_ref[0]
        place_ref[0] = row
        place_ref[1] = me_ref[1]
        loads = [pltpu.make_async_copy(up_hbm, up_ref, sems.at[0])]
        loads += [pltpu.make_async_copy(x_hbm, x_ref, sems.at[1])]
        loads += [
            pltpu.make_async_copy(w_hbm.at[c], w_ref.at[c], sems.at[2 + c]) for c in range(parts)
        ]
        for load in loads:
            load.start()
        loads[0].wait()
        for j in range(2):
            at = pl.multiple_of((row ^ (2 * j + 1)) * block, LANES)
            there_ref[j] = up_ref[:, pl.ds(at, block)]
        here_ref[...] = up_ref[:, pl.ds(pl.multiple_of(row * block, LANES), block)]
        across_ref[...] = up_ref[:, pl.ds(pl.multiple_of((row ^ 2) * block, LANES), block)]
        loads[1].wait()
        for c in range(parts):
            loads[2 + c].wait()
            for j in range(2):
                multiply(x_ref[...], w_ref, c, row ^ (2 * j + 1), away_refs[j])

    return local(
        me,
        body,
        [
            pltpu.VMEM(w.shape, w.dtype),
            pltpu.VMEM(x.shape, x.dtype),
            bf16(2, high, block),
            bf16(high, block),
            bf16(high, block),
            bf16(parts, high, block),
            bf16(parts, high, block),
            pltpu.SMEM((2,), jnp.int32),
        ],
        [hbm(x), hbm(up), hbm(w)],
        3.5,
        [HBM, HBM, HBM],
        out_specs=[VMEM] * 7 + [SMEM],
        scratch=[
            pltpu.VMEM(up.shape, up.dtype),
            pltpu.SemaphoreType.DMA((2 + parts,)),
        ],
    )


def project(me, xs, w, block, other, late=()):
    parts = w.shape[0]
    tall = xs[0].shape[0] * len(xs)

    def body(me_ref, *refs):
        w_ref, out_refs = refs[len(xs)], refs[len(xs) + 1 :]
        x = jnp.concatenate([x[...] for x in refs[: len(xs)]], axis=0)
        for j in (1, 0):
            for c in range(parts):
                multiply(x, w_ref, c, me_ref[0] ^ (2 * j + other), out_refs[j])

    outs = [bf16(parts, tall, block)] * 2
    return local(me, body, outs, [*xs, w], 2.0 * len(xs), late=late)


def laid_out(me, groups, ups, late=()):
    parts, _, block = groups[0][2].shape
    tokens = sum(far.shape[1] for _, _, far in groups)
    high = ups[0].shape[0]
    n_in = 3 * len(groups)

    def body(me_ref, *refs):
        ins, up_refs, (seq, cot) = refs[:n_in], refs[n_in:-2], refs[-2:]
        row, z = me_ref[0], me_ref[1]
        for at in (0, PAD + tokens):
            seq[:, at : at + PAD, :] = jnp.zeros((parts, PAD, block), jnp.float32)
            cot[at : at + PAD, :] = jnp.zeros((PAD, block), jnp.float32)
        for s in range(len(groups)):
            keep, near, far = ins[3 * s : 3 * s + 3]
            to = pl.multiple_of(behind(z, s) * high + PAD, PAD)
            for c in range(parts):
                total = keep[c].astype(jnp.float32) + near[c].astype(jnp.float32)
                total = total + far[c].astype(jnp.float32)
                seq[c, pl.ds(to, high), :] = total.astype(jnp.bfloat16).astype(jnp.float32)
        for i, up in enumerate(up_refs):
            to = pl.multiple_of((row ^ i) * high + PAD, PAD)
            cot[pl.ds(to, high), :] = up[...].astype(jnp.float32)

    operands = [a for group in groups for a in group] + list(ups)
    outs = [
        pltpu.VMEM((parts, tokens + 2 * PAD, block), jnp.float32),
        pltpu.VMEM((tokens + 2 * PAD, block), jnp.float32),
    ]
    return local(me, body, outs, operands, 0.6, late=late)


def gate(me, seq, cot, feature_taps, inner_taps, high, shards, one=None, late=()):
    lags, parts, _ = feature_taps.shape
    long_lags = inner_taps.shape[0]
    block = cot.shape[1]
    window = high + 2 * PAD
    ins = [seq, cot, feature_taps, inner_taps] + ([] if one is None else [one])

    def back(value, lag):
        return pltpu.roll(value, lag, 0) if lag else value

    def ahead(value, lag):
        return pltpu.roll(value, window - lag, 0) if lag else value

    def body(me_ref, seq_ref, cot_ref, taps_ref, long_ref, *refs):
        row, z = me_ref[0], me_ref[1]
        if one is not None:
            one_ref, all_ref, last_ref, two_ref = refs
            all_ref[0] = one_ref[...]

        @pl.loop(0, block // LANES)
        def _(half):
            lanes = pl.ds(pl.multiple_of(half * LANES, LANES), LANES)
            wide = pl.ds(pl.multiple_of(row * block + half * LANES, LANES), LANES)
            taps = [[taps_ref[s, c : c + 1, wide] for c in range(parts)] for s in range(lags)]
            long_taps = [long_ref[s : s + 1, wide] for s in range(long_lags)]
            for s in shards:
                rows = pl.ds(pl.multiple_of(behind(z, s) * high, PAD), window)
                mixed = []
                for c in range(parts):
                    proj = seq_ref[c, rows, lanes]
                    total = taps[0][c] * proj
                    for lag in range(1, lags):
                        total = total + taps[lag][c] * back(proj, lag)
                    mixed.append(total)
                query, key, value = mixed
                upstream = cot_ref[rows, lanes]
                product = (key * value).astype(jnp.bfloat16).astype(jnp.float32)
                inner = long_taps[0] * product
                for lag in range(1, long_lags):
                    inner = inner + long_taps[lag] * back(product, lag)
                grad_inner = upstream * query
                grad_product = long_taps[0] * grad_inner
                for lag in range(1, long_lags):
                    grad_product = grad_product + long_taps[lag] * ahead(grad_inner, lag)
                grads = (upstream * inner, grad_product * value, grad_product * key)
                for c, grad in enumerate(grads):
                    total = taps[0][c] * grad
                    for lag in range(1, lags):
                        total = total + taps[lag][c] * ahead(grad, lag)
                    done = total[PAD : PAD + high].astype(jnp.bfloat16)
                    if one is None:
                        refs[0][c, :, lanes] = done
                        continue
                    all_ref[(s - 1) % 4, c, :, lanes] = done
                    if s == 2:
                        two_ref[c, :, lanes] = done
                    else:
                        last_ref[(s - 3) % 4, c, :, lanes] = done

    single = (parts, high, block)
    outs = [bf16(*single)]
    if one is not None:
        outs = [bf16(4, *single), bf16(2, *single), *outs]
    return local(me, body, outs, ins, 0.8 * len(shards), late=late)


def relay(me, *values, late=()):
    return local(
        me,
        lambda *refs: None,
        [jax.ShapeDtypeStruct(value.shape, value.dtype) for value in values],
        values,
        0.01,
        [ANY] * len(values),
        out_specs=[ANY] * len(values),
        aliases={i: i for i in range(len(values))},
        late=late,
        placed=False,
    )


def input_grads(me, pieces, w, late=()):
    parts, depth, width = w.shape
    high, block = pieces[0][0].shape[-2:]
    shards = len(pieces[0][1])

    def body(me_ref, *refs):
        w_ref, outs, wide = refs[len(pieces)], refs[len(pieces) + 1 : -1], refs[-1]
        for i, (g, (_, which)) in enumerate(zip(refs, pieces)):
            at = pl.multiple_of((me_ref[0] ^ i) * block, LANES)
            for s, index in enumerate(which):
                shard = g if index is None else g.at[index]
                wide[:, s * high : (s + 1) * high, pl.ds(at, block)] = shard[...]
        total = None
        for c in range(parts):
            term = lax.dot_general(
                wide[c], w_ref[c], (((1,), (1,)), ((), ())), preferred_element_type=jnp.float32
            )
            total = term if total is None else total + term
        for s, out in enumerate(outs):
            out[...] = total[s * high : (s + 1) * high].astype(jnp.bfloat16)

    return local(
        me,
        body,
        [bf16(high, depth)] * shards,
        [*(g for g, _ in pieces), w],
        0.8 * shards,
        scratch=[pltpu.VMEM((parts, shards * high, width), jnp.bfloat16)],
        late=late,
    )


def turned(me, xs, late=()):
    high, depth = xs[0].shape

    def body(*refs):
        for s, x in enumerate(refs[:-1]):
            refs[-1][:, s * high : (s + 1) * high] = x[...].T

    me, (out,) = local(me, body, [bf16(depth, high * len(xs))], xs, 0.1 * len(xs), late=late, placed=False)
    return me, out


def weight_grads(me, done, xts, blocks, width, begun=None, final=True):
    depth = xts[0].shape[0]
    flat = [p for _, pieces in blocks for p in pieces]
    parts, high, block = flat[0][0].shape[-3:]
    unique = []
    for g, _ in flat:
        if not any(g is u for u in unique):
            unique.append(g)
    spot = {id(u): n for n, u in enumerate(unique)}
    tokens = high * len(blocks[0][1])
    wide = block * len(blocks)
    cuts, spare = 4, 4
    tall = depth // cuts
    n_in = len(xts) + len(unique) + (begun is not None) + (done is not None)

    def body(me_ref, *refs):
        x_refs, g_refs = refs[: len(xts)], refs[len(xts) : n_in]
        out_ref, xt, gs, *rest = refs[n_in:]
        at = 0
        for x in x_refs:
            xt[:, at : at + x.shape[1]] = x[...]
            at += x.shape[1]
        row = me_ref[0]
        start = pl.multiple_of((row ^ blocks[0][0]) // CORES * wide, wide)
        copies = []
        for c in range(parts):
            for i, pieces in blocks:
                lanes = pl.ds(pl.multiple_of((row ^ i) % CORES * block, LANES), block)
                for k, (g, index) in enumerate(pieces):
                    g_ref = g_refs[spot[id(g)]]
                    shard = g_ref if index is None else g_ref.at[index]
                    gs[c % 2, k * high : (k + 1) * high, lanes] = shard[c]
            for m in range(cuts):
                rows = pl.ds(m * tall, tall)
                part = jnp.dot(xt[rows, :], gs[c % 2], preferred_element_type=jnp.float32)
                if begun is not None:
                    part = part + g_refs[len(unique)][c, rows, :]
                if not final:
                    out_ref[c, rows, :] = part
                    continue
                held, sems = rest
                slot = len(copies) % spare
                if len(copies) >= spare:
                    copies[-spare].wait()
                held[slot] = part
                copies.append(
                    pltpu.make_async_copy(
                        held.at[slot], out_ref.at[c, rows, pl.ds(start, wide)], sems.at[slot]
                    )
                )
                copies[-1].start()
        for copy in copies[-spare:]:
            copy.wait()

    ins = [*xts, *unique] + ([] if begun is None else [begun])
    specs = [VMEM] * len(ins)
    aliases = {}
    if done is not None:
        aliases = {len(ins): 0}
        ins.append(done)
        specs.append(ANY)
    scratch = [
        pltpu.VMEM((depth, tokens), jnp.bfloat16),
        pltpu.VMEM((2, tokens, wide), jnp.bfloat16),
    ]
    out = pltpu.VMEM((parts, depth, wide), jnp.float32)
    if final:
        out = jax.ShapeDtypeStruct((parts, depth, width), jnp.float32)
        scratch += [
            pltpu.VMEM((spare, tall, wide), jnp.float32),
            pltpu.SemaphoreType.DMA((spare,)),
        ]
    me, (out,) = local(
        me,
        body,
        [out],
        ins,
        6.0 if final else 1.0,
        specs,
        scratch=scratch,
        out_specs=[ANY if final else VMEM],
        aliases=aliases,
    )
    return me, out


def total(me, terms, late=()):
    def body(*refs):
        acc = refs[0][...].astype(jnp.float32)
        for ref in refs[1:-1]:
            acc = acc + ref[...].astype(jnp.float32)
        refs[-1][...] = acc.astype(jnp.bfloat16)

    me, (out,) = local(me, body, [bf16(*terms[0].shape)], terms, 0.05, late=late, placed=False)
    return me, out


def by_channels(inputs, weights, feature_taps, inner_taps, grad_out):
    x_own = inputs[0]
    block = weights.shape[2] // lax.axis_size("row")
    width = weights.shape[2]
    me = (jnp.stack([lax.axis_index("row"), lax.axis_index("col")]).astype(jnp.int32),)

    def send(name, value, axis, step):
        with jax.named_scope(name):
            return along(value, step) if axis == "col" else swap(value, axis, step)

    x1 = send("x1", x_own, "col", 1)
    x2 = send("x2", x1, "col", 1)
    x3 = send("x3", x2, "col", 1)
    with jax.named_scope("begin"):
        me, (w, x_own, there, here, across, *away, place) = begin(
            me, x_own, grad_out[0], jnp.transpose(weights, (1, 0, 2)), block
        )
    me = (place, *me[1:])
    def spread(me, name, x, away, turn=(), late=()):
        got = [send(name + "_core%d" % j, away[j], "row", 1) for j in range(2)]
        with jax.named_scope(name + "_keep"):
            me, keep = project(me, [x], w, block, 0)
        with jax.named_scope(name + "_join"):
            me, both = total(me, [keep[1], got[1]], [got[0]])
        groups.append((keep[0], got[0], send(name + "_y", both, "row", CORES)))
        if turn:
            with jax.named_scope(name + "_turned"):
                me, xt = turned(me, turn, late)
            xts.append(xt)
            others.append(send(name + "_xt_x", xt, "dp", 1))
        return me

    groups, xts, others = [], [], []
    me = spread(me, "proj0", x_own, away)
    with jax.named_scope("proj1_away"):
        me, away = project(me, [x1], w, block, 1)
    me = spread(me, "proj1", x1, away, [x_own, x1], [groups[0][2]])
    with jax.named_scope("proj2_away"):
        me, away = project(me, [x2], w, block, 1)
    me = spread(me, "proj2", x2, away, [x2], [groups[1][2]])
    with jax.named_scope("relay_up"):
        me, (there,) = relay(me, there)
    near = send("up_core", there, "row", 1)
    far = send("up_y", jnp.stack([across, near[1]]), "row", CORES)
    ups = [here, near[0], far[0], far[1]]
    with jax.named_scope("proj3_away"):
        me, away = project(me, [x3], w, block, 1)
    me = spread(me, "proj3", x3, away, [x3], [groups[2][2], others[0]])
    with jax.named_scope("laid_out"):
        me, (seq, cot) = laid_out(me, groups, ups)
    high = x_own.shape[0]
    with jax.named_scope("gate1"):
        me, (g1,) = gate(me, seq, cot, feature_taps, inner_taps, high, (1,))
    y1 = send("g1_y", g1, "row", CORES)
    with jax.named_scope("gate230"):
        me, (g, g30, g2) = gate(
            me, seq, cot, feature_taps, inner_taps, high, (2, 3, 0), g1, others[1:]
        )
    with jax.named_scope("relay_g"):
        me, (g2, g30) = relay(me, g2, g30, late=[y1])
    y2, y30 = send("g2_y", g2, "row", CORES), send("g30_y", g30, "row", CORES)
    c, x = send("g_core", g, "row", 1), send("g_x", g, "dp", 1)
    cy1, cy2 = send("gy1_core", y1, "row", 1), send("gy2_core", y2, "row", 1)

    with jax.named_scope("input_grads1"):
        pieces = [(g, [0]), (c, [0]), (y1, [None]), (cy1, [None])]
        me, (share1,) = input_grads(me, pieces, w)
    passed = send("share1", share1, "col", 1)
    def whole(a):
        return [(a, 3), (a, 0), (a, 1), (a, 2)]

    def cut(last, one, two):
        return [(last, 1), (one, None), (two, None), (last, 0)]

    def halves(low, high):
        return [(high, 1), (low, 0), (low, 1), (high, 0)]

    with jax.named_scope("weight_grads_near_own"):
        blocks = [(0, whole(g)), (1, whole(c))]
        me, begun = weight_grads(me, None, xts, blocks, width, final=False)
    with jax.named_scope("relay_x"):
        me, (x,) = relay(me, x)
    xy12, cx = send("gx12_y", x[:2], "row", CORES), send("gx_core", x, "row", 1)
    with jax.named_scope("input_grads2"):
        pieces = [(g, [1]), (c, [1]), (y2, [None]), (cy2, [None])]
        me, (share2,) = input_grads(me, pieces, w)
    with jax.named_scope("total2"):
        me, share2 = total(me, [share2, passed])
    passed = send("share2", share2, "col", 1)
    with jax.named_scope("relay_y30"):
        me, (y30,) = relay(me, y30)
    xy30, cy30 = send("gy30_x", y30, "dp", 1), send("gy30_core", y30, "row", 1)
    with jax.named_scope("input_grads30"):
        pieces = [(g, [2, 3]), (c, [2, 3]), (y30, [0, 1]), (cy30, [0, 1])]
        me, (share3, share0) = input_grads(me, pieces, w)
    with jax.named_scope("weight_grads_near"):
        blocks = [(0, whole(x)), (1, whole(cx))]
        me, grad_w = weight_grads(me, None, others, blocks, width, begun)
    with jax.named_scope("total3"):
        me, share3 = total(me, [share3, passed])
    passed = send("share3", share3, "col", 1)
    with jax.named_scope("relay_xy"):
        me, (xy12, xy30) = relay(me, xy12, xy30)
    cxy12, cxy30 = send("gxy12_core", xy12, "row", 1), send("gxy30_core", xy30, "row", 1)
    with jax.named_scope("weight_grads_far"):
        blocks = [
            (2, cut(y30, y1, y2) + halves(xy12, xy30)),
            (3, cut(cy30, cy1, cy2) + halves(cxy12, cxy30)),
        ]
        me, grad_w = weight_grads(me, grad_w, xts + others, blocks, width)
    with jax.named_scope("total0"):
        me, grad_in = total(me, [share0, passed])
    return (grad_in[None], jnp.transpose(grad_w, (1, 0, 2)))


def solution(mesh):
    placed = (
        P("dp", "col", "row"),
        P("row", None, "col"),
        P(None, None, "col"),
        P(None, "col"),
        P("dp", "row", "col"),
    )

    def on_device(inputs, weights, feature_taps, inner_taps, grad_out):
        n_row = mesh.shape["row"]
        fits = weights.shape[2] % (n_row * LANES) == 0 and inputs.shape[1] % LANES == 0
        small = n_row == 2 * CORES and mesh.shape["dp"] == 2 and mesh.shape["col"] == 4
        plan = by_channels if fits and small else by_tokens
        return plan(inputs, weights, feature_taps, inner_taps, grad_out)

    return jax.shard_map(
        on_device,
        mesh=mesh,
        in_specs=placed,
        out_specs=(P("dp", "col", "row"), P("row", None, "col")),
        check_vma=False,
    )
```

```python
import math

import jax
import jax.numpy as jnp
from jax import lax
from jax.experimental import pallas as pl
from jax.experimental.pallas import tpu as pltpu
from jax.sharding import PartitionSpec as P

LANES = 128
PAD = 8
CORES = 2


def shifted(shard, axis, by):
    length = lax.axis_size(axis)
    pairs = [(i, i + by) for i in range(length) if 0 <= i + by < length]
    return lax.ppermute(shard, axis, pairs)


def with_halo(cells, axis, width):
    head = shifted(cells[:width], axis, -1)
    tail = shifted(cells[-width:], axis, 1)
    return jnp.concatenate([tail, cells, head], axis=0)


def causal(seq, taps):
    total = taps[0] * seq
    for lag in range(1, taps.shape[0]):
        pad = jnp.zeros((lag,) + seq.shape[1:], jnp.float32)
        total = total + taps[lag] * jnp.concatenate([pad, seq[:-lag]], axis=0)
    return total


def anticausal(seq, taps):
    total = taps[0] * seq
    for lag in range(1, taps.shape[0]):
        pad = jnp.zeros((lag,) + seq.shape[1:], jnp.float32)
        total = total + taps[lag] * jnp.concatenate([seq[lag:], pad], axis=0)
    return total


def rounded(value):
    return lax.optimization_barrier(value.astype(jnp.bfloat16)).astype(jnp.float32)


def by_tokens(inputs, weights, feature_taps, inner_taps, grad_out):
    tile = inputs[0]
    upstream_tile = grad_out[0]
    rows_dev = upstream_tile.shape[0]
    width_row = weights.shape[0]
    width_col = weights.shape[2]
    margin = feature_taps.shape[0] - 1 + (inner_taps.shape[0] - 1)
    flat_w = weights.reshape(width_row, 3 * width_col)
    columns = lax.all_gather(tile, "col", axis=0, tiled=True)
    proj = lax.psum_scatter(
        jnp.dot(columns, flat_w, preferred_element_type=jnp.float32).astype(jnp.bfloat16),
        "row",
        scatter_dimension=0,
        tiled=True,
    )
    length = rows_dev + 2 * margin
    window = with_halo(proj, "row", margin).astype(jnp.float32).reshape(length, 3, width_col)
    after = shifted(upstream_tile[:margin], "row", -1)
    upstream = jnp.concatenate(
        [
            jnp.zeros((margin, width_col), jnp.float32),
            upstream_tile.astype(jnp.float32),
            after.astype(jnp.float32),
        ],
        axis=0,
    )
    mixed = causal(window, feature_taps)
    query = mixed[:, 0]
    key = mixed[:, 1]
    value = mixed[:, 2]
    product = rounded(key * value)
    inner = causal(product, inner_taps)
    grad_query = upstream * inner
    grad_product = anticausal(upstream * query, inner_taps)
    grad_mixed = jnp.stack([grad_query, grad_product * value, grad_product * key], axis=1)
    grad_proj = anticausal(grad_mixed, feature_taps)[margin : margin + rows_dev].astype(
        jnp.bfloat16
    )
    gathered = lax.all_gather(grad_proj.reshape(rows_dev, 3 * width_col), "row", axis=0, tiled=True)
    grad_x = lax.psum_scatter(
        lax.dot_general(
            gathered, flat_w, (((1,), (1,)), ((), ())), preferred_element_type=jnp.float32
        ).astype(jnp.bfloat16),
        "col",
        scatter_dimension=0,
        tiled=True,
    )
    local = lax.dot_general(
        columns, gathered, (((0,), (0,)), ((), ())), preferred_element_type=jnp.float32
    )
    grad_w = lax.psum(local.astype(jnp.bfloat16), "dp").astype(jnp.float32)
    return (grad_x[None], grad_w.reshape(width_row, 3, width_col))


def swap(value, axis, step):
    size = lax.axis_size(axis)
    return lax.ppermute(value, axis, [(i, i ^ step) for i in range(size)])


LINE = (0, 2, 3, 1)


def along(value, steps):
    size = len(LINE)
    pairs = [(LINE[i], LINE[(i + steps) % size]) for i in range(size)]
    return lax.ppermute(value, "col", pairs)


def behind(z, steps):
    for _ in range(steps):
        z = jnp.where(z < 2, 2 * z + 1, 2 * z - 4)
    return z


VMEM = pl.BlockSpec(memory_space=pltpu.VMEM)
SMEM = pl.BlockSpec(memory_space=pltpu.SMEM)
HBM = pl.BlockSpec(memory_space=pltpu.HBM)
ANY = pl.BlockSpec(memory_space=pl.ANY)


PER_MICRO = 1.1e9


def hbm(value):
    return pltpu.with_memory_space_constraint(value, pltpu.HBM)


def bf16(*shape):
    return jax.ShapeDtypeStruct(shape, jnp.bfloat16)


def local(
    me, body, outs, ins, micros, in_specs=None, scratch=(), out_specs=None, aliases=None, late=(), placed=True
):
    place, *turn = me
    first = [place] if placed else []
    late = [*turn, *late]
    n_in = len(first) + len(ins)

    def ordered(*refs):
        body(*refs[:n_in], *refs[n_in + len(late) + 1 :])

    turns = {n_in: 0} if turn else {}
    moved = {len(first) + i: 1 + o for i, o in (aliases or {}).items()}
    turn, *results = pl.pallas_call(
        ordered,
        out_shape=[jax.ShapeDtypeStruct((8, LANES), jnp.float32), *outs],
        in_specs=[SMEM] * len(first) + [*(in_specs or [VMEM] * len(ins)), *[ANY] * len(late)],
        out_specs=[ANY, *(out_specs or [VMEM] * len(outs))],
        scratch_shapes=list(scratch),
        input_output_aliases={**turns, **moved},
        compiler_params=pltpu.CompilerParams(vmem_limit_bytes=16 * 2**20),
        cost_estimate=pl.CostEstimate(
            flops=int(micros * PER_MICRO), bytes_accessed=1, transcendentals=0
        ),
    )(*first, *ins, *late)
    return (place, turn), results


def multiply(x, w_ref, c, block_at, out_ref):
    block = out_ref.shape[-1]
    at = pl.multiple_of(block_at * block, LANES)
    out_ref[c] = jnp.dot(
        x, w_ref[c, :, pl.ds(at, block)], preferred_element_type=jnp.float32
    ).astype(jnp.bfloat16)


def begin(me, x, up, w, block):
    parts, depth, width = w.shape
    high = up.shape[0]

    def body(me_ref, x_hbm, up_hbm, w_hbm, *refs):
        w_ref, x_ref, there_ref, here_ref, across_ref, *away_refs, place_ref, up_ref, sems = refs
        row = me_ref[0]
        place_ref[0] = row
        place_ref[1] = me_ref[1]
        loads = [pltpu.make_async_copy(up_hbm, up_ref, sems.at[0])]
        loads += [pltpu.make_async_copy(x_hbm, x_ref, sems.at[1])]
        loads += [
            pltpu.make_async_copy(w_hbm.at[c], w_ref.at[c], sems.at[2 + c]) for c in range(parts)
        ]
        for load in loads:
            load.start()
        loads[0].wait()
        for j in range(2):
            at = pl.multiple_of((row ^ (2 * j + 1)) * block, LANES)
            there_ref[j] = up_ref[:, pl.ds(at, block)]
        here_ref[...] = up_ref[:, pl.ds(pl.multiple_of(row * block, LANES), block)]
        across_ref[...] = up_ref[:, pl.ds(pl.multiple_of((row ^ 2) * block, LANES), block)]
        loads[1].wait()
        for c in range(parts):
            loads[2 + c].wait()
            for j in range(2):
                multiply(x_ref[...], w_ref, c, row ^ (2 * j + 1), away_refs[j])

    return local(
        me,
        body,
        [
            pltpu.VMEM(w.shape, w.dtype),
            pltpu.VMEM(x.shape, x.dtype),
            bf16(2, high, block),
            bf16(high, block),
            bf16(high, block),
            bf16(parts, high, block),
            bf16(parts, high, block),
            pltpu.SMEM((2,), jnp.int32),
        ],
        [hbm(x), hbm(up), hbm(w)],
        3.5,
        [HBM, HBM, HBM],
        out_specs=[VMEM] * 7 + [SMEM],
        scratch=[
            pltpu.VMEM(up.shape, up.dtype),
            pltpu.SemaphoreType.DMA((2 + parts,)),
        ],
    )


def project(me, xs, w, block, other, late=()):
    parts = w.shape[0]
    tall = xs[0].shape[0] * len(xs)

    def body(me_ref, *refs):
        w_ref, out_refs = refs[len(xs)], refs[len(xs) + 1 :]
        x = jnp.concatenate([x[...] for x in refs[: len(xs)]], axis=0)
        for j in (1, 0):
            for c in range(parts):
                multiply(x, w_ref, c, me_ref[0] ^ (2 * j + other), out_refs[j])

    outs = [bf16(parts, tall, block)] * 2
    return local(me, body, outs, [*xs, w], 2.0 * len(xs), late=late)


def laid_out(me, groups, ups, late=()):
    parts, _, block = groups[0][2].shape
    tokens = sum(far.shape[1] for _, _, far in groups)
    high = ups[0].shape[0]
    n_in = 3 * len(groups)

    def body(me_ref, *refs):
        ins, up_refs, (seq, cot) = refs[:n_in], refs[n_in:-2], refs[-2:]
        row, z = me_ref[0], me_ref[1]
        for at in (0, PAD + tokens):
            seq[:, at : at + PAD, :] = jnp.zeros((parts, PAD, block), jnp.float32)
            cot[at : at + PAD, :] = jnp.zeros((PAD, block), jnp.float32)
        for s in range(len(groups)):
            keep, near, far = ins[3 * s : 3 * s + 3]
            to = pl.multiple_of(behind(z, s) * high + PAD, PAD)
            for c in range(parts):
                total = keep[c].astype(jnp.float32) + near[c].astype(jnp.float32)
                total = total + far[c].astype(jnp.float32)
                seq[c, pl.ds(to, high), :] = total.astype(jnp.bfloat16).astype(jnp.float32)
        for i, up in enumerate(up_refs):
            to = pl.multiple_of((row ^ i) * high + PAD, PAD)
            cot[pl.ds(to, high), :] = up[...].astype(jnp.float32)

    operands = [a for group in groups for a in group] + list(ups)
    outs = [
        pltpu.VMEM((parts, tokens + 2 * PAD, block), jnp.float32),
        pltpu.VMEM((tokens + 2 * PAD, block), jnp.float32),
    ]
    return local(me, body, outs, operands, 0.6, late=late)


def gate(me, seq, cot, feature_taps, inner_taps, high, shards, one=None, late=()):
    lags, parts, _ = feature_taps.shape
    long_lags = inner_taps.shape[0]
    block = cot.shape[1]
    window = high + 2 * PAD
    ins = [seq, cot, feature_taps, inner_taps] + ([] if one is None else [one])

    def back(value, lag):
        return pltpu.roll(value, lag, 0) if lag else value

    def ahead(value, lag):
        return pltpu.roll(value, window - lag, 0) if lag else value

    def body(me_ref, seq_ref, cot_ref, taps_ref, long_ref, *refs):
        row, z = me_ref[0], me_ref[1]
        if one is not None:
            one_ref, all_ref, last_ref, two_ref = refs
            all_ref[0] = one_ref[...]

        @pl.loop(0, block // LANES)
        def _(half):
            lanes = pl.ds(pl.multiple_of(half * LANES, LANES), LANES)
            wide = pl.ds(pl.multiple_of(row * block + half * LANES, LANES), LANES)
            taps = [[taps_ref[s, c : c + 1, wide] for c in range(parts)] for s in range(lags)]
            long_taps = [long_ref[s : s + 1, wide] for s in range(long_lags)]
            for s in shards:
                rows = pl.ds(pl.multiple_of(behind(z, s) * high, PAD), window)
                mixed = []
                for c in range(parts):
                    proj = seq_ref[c, rows, lanes]
                    total = taps[0][c] * proj
                    for lag in range(1, lags):
                        total = total + taps[lag][c] * back(proj, lag)
                    mixed.append(total)
                query, key, value = mixed
                upstream = cot_ref[rows, lanes]
                product = (key * value).astype(jnp.bfloat16).astype(jnp.float32)
                inner = long_taps[0] * product
                for lag in range(1, long_lags):
                    inner = inner + long_taps[lag] * back(product, lag)
                grad_inner = upstream * query
                grad_product = long_taps[0] * grad_inner
                for lag in range(1, long_lags):
                    grad_product = grad_product + long_taps[lag] * ahead(grad_inner, lag)
                grads = (upstream * inner, grad_product * value, grad_product * key)
                for c, grad in enumerate(grads):
                    total = taps[0][c] * grad
                    for lag in range(1, lags):
                        total = total + taps[lag][c] * ahead(grad, lag)
                    done = total[PAD : PAD + high].astype(jnp.bfloat16)
                    if one is None:
                        refs[0][c, :, lanes] = done
                        continue
                    all_ref[(s - 1) % 4, c, :, lanes] = done
                    if s == 2:
                        two_ref[c, :, lanes] = done
                    else:
                        last_ref[(s - 3) % 4, c, :, lanes] = done

    single = (parts, high, block)
    outs = [bf16(*single)]
    if one is not None:
        outs = [bf16(4, *single), bf16(2, *single), *outs]
    return local(me, body, outs, ins, 0.8 * len(shards), late=late)


def relay(me, *values, late=()):
    return local(
        me,
        lambda *refs: None,
        [jax.ShapeDtypeStruct(value.shape, value.dtype) for value in values],
        values,
        0.01,
        [ANY] * len(values),
        out_specs=[ANY] * len(values),
        aliases={i: i for i in range(len(values))},
        late=late,
        placed=False,
    )


def input_grads(me, pieces, w, late=()):
    parts, depth, width = w.shape
    high, block = pieces[0][0].shape[-2:]
    shards = len(pieces[0][1])

    def body(me_ref, *refs):
        w_ref, outs, wide = refs[len(pieces)], refs[len(pieces) + 1 : -1], refs[-1]
        for i, (g, (_, which)) in enumerate(zip(refs, pieces)):
            at = pl.multiple_of((me_ref[0] ^ i) * block, LANES)
            for s, index in enumerate(which):
                shard = g if index is None else g.at[index]
                wide[:, s * high : (s + 1) * high, pl.ds(at, block)] = shard[...]
        total = None
        for c in range(parts):
            term = lax.dot_general(
                wide[c], w_ref[c], (((1,), (1,)), ((), ())), preferred_element_type=jnp.float32
            )
            total = term if total is None else total + term
        for s, out in enumerate(outs):
            out[...] = total[s * high : (s + 1) * high].astype(jnp.bfloat16)

    return local(
        me,
        body,
        [bf16(high, depth)] * shards,
        [*(g for g, _ in pieces), w],
        0.8 * shards,
        scratch=[pltpu.VMEM((parts, shards * high, width), jnp.bfloat16)],
        late=late,
    )


def turned(me, xs, late=()):
    high, depth = xs[0].shape

    def body(*refs):
        for s, x in enumerate(refs[:-1]):
            refs[-1][:, s * high : (s + 1) * high] = x[...].T

    me, (out,) = local(me, body, [bf16(depth, high * len(xs))], xs, 0.1 * len(xs), late=late, placed=False)
    return me, out


def weight_grads(me, done, xts, blocks, width, begun=None, final=True):
    depth = xts[0].shape[0]
    flat = [p for _, pieces in blocks for p in pieces]
    parts, high, block = flat[0][0].shape[-3:]
    unique = []
    for g, _ in flat:
        if not any(g is u for u in unique):
            unique.append(g)
    spot = {id(u): n for n, u in enumerate(unique)}
    tokens = high * len(blocks[0][1])
    wide = block * len(blocks)
    cuts, spare = 4, 4
    tall = depth // cuts
    n_in = len(xts) + len(unique) + (begun is not None) + (done is not None)

    def body(me_ref, *refs):
        x_refs, g_refs = refs[: len(xts)], refs[len(xts) : n_in]
        out_ref, xt, gs, *rest = refs[n_in:]
        at = 0
        for x in x_refs:
            xt[:, at : at + x.shape[1]] = x[...]
            at += x.shape[1]
        row = me_ref[0]
        start = pl.multiple_of((row ^ blocks[0][0]) // CORES * wide, wide)
        copies = []
        for c in range(parts):
            for i, pieces in blocks:
                lanes = pl.ds(pl.multiple_of((row ^ i) % CORES * block, LANES), block)
                for k, (g, index) in enumerate(pieces):
                    g_ref = g_refs[spot[id(g)]]
                    shard = g_ref if index is None else g_ref.at[index]
                    gs[c % 2, k * high : (k + 1) * high, lanes] = shard[c]
            for m in range(cuts):
                rows = pl.ds(m * tall, tall)
                part = jnp.dot(xt[rows, :], gs[c % 2], preferred_element_type=jnp.float32)
                if begun is not None:
                    part = part + g_refs[len(unique)][c, rows, :]
                if not final:
                    out_ref[c, rows, :] = part
                    continue
                held, sems = rest
                slot = len(copies) % spare
                if len(copies) >= spare:
                    copies[-spare].wait()
                held[slot] = part
                copies.append(
                    pltpu.make_async_copy(
                        held.at[slot], out_ref.at[c, rows, pl.ds(start, wide)], sems.at[slot]
                    )
                )
                copies[-1].start()
        for copy in copies[-spare:]:
            copy.wait()

    ins = [*xts, *unique] + ([] if begun is None else [begun])
    specs = [VMEM] * len(ins)
    aliases = {}
    if done is not None:
        aliases = {len(ins): 0}
        ins.append(done)
        specs.append(ANY)
    scratch = [
        pltpu.VMEM((depth, tokens), jnp.bfloat16),
        pltpu.VMEM((2, tokens, wide), jnp.bfloat16),
    ]
    out = pltpu.VMEM((parts, depth, wide), jnp.float32)
    if final:
        out = jax.ShapeDtypeStruct((parts, depth, width), jnp.float32)
        scratch += [
            pltpu.VMEM((spare, tall, wide), jnp.float32),
            pltpu.SemaphoreType.DMA((spare,)),
        ]
    me, (out,) = local(
        me,
        body,
        [out],
        ins,
        6.0 if final else 2.0,
        specs,
        scratch=scratch,
        out_specs=[ANY if final else VMEM],
        aliases=aliases,
    )
    return me, out


def total(me, terms, late=()):
    def body(*refs):
        acc = refs[0][...].astype(jnp.float32)
        for ref in refs[1:-1]:
            acc = acc + ref[...].astype(jnp.float32)
        refs[-1][...] = acc.astype(jnp.bfloat16)

    me, (out,) = local(me, body, [bf16(*terms[0].shape)], terms, 0.05, late=late, placed=False)
    return me, out


def by_channels(inputs, weights, feature_taps, inner_taps, grad_out):
    x_own = inputs[0]
    block = weights.shape[2] // lax.axis_size("row")
    width = weights.shape[2]
    me = (jnp.stack([lax.axis_index("row"), lax.axis_index("col")]).astype(jnp.int32),)

    def send(name, value, axis, step):
        with jax.named_scope(name):
            return along(value, step) if axis == "col" else swap(value, axis, step)

    x1 = send("x1", x_own, "col", 1)
    x2 = send("x2", x1, "col", 1)
    x3 = send("x3", x2, "col", 1)
    with jax.named_scope("begin"):
        me, (w, x_own, there, here, across, *away, place) = begin(
            me, x_own, grad_out[0], jnp.transpose(weights, (1, 0, 2)), block
        )
    me = (place, *me[1:])
    def spread(me, name, x, away, turn=(), late=()):
        got = [send(name + "_core%d" % j, away[j], "row", 1) for j in range(2)]
        with jax.named_scope(name + "_keep"):
            me, keep = project(me, [x], w, block, 0)
        with jax.named_scope(name + "_join"):
            me, both = total(me, [keep[1], got[1]], [got[0]])
        groups.append((keep[0], got[0], send(name + "_y", both, "row", CORES)))
        if turn:
            with jax.named_scope(name + "_turned"):
                me, xt = turned(me, turn, late)
            xts.append(xt)
            others.append(send(name + "_xt_x", xt, "dp", 1))
        return me

    groups, xts, others = [], [], []
    me = spread(me, "proj0", x_own, away)
    with jax.named_scope("proj1_away"):
        me, away = project(me, [x1], w, block, 1)
    me = spread(me, "proj1", x1, away, [x_own, x1], [groups[0][2]])
    with jax.named_scope("proj2_away"):
        me, away = project(me, [x2], w, block, 1)
    me = spread(me, "proj2", x2, away, [x2], [groups[1][2]])
    with jax.named_scope("relay_up"):
        me, (there,) = relay(me, there)
    near = send("up_core", there, "row", 1)
    far = send("up_y", jnp.stack([across, near[1]]), "row", CORES)
    ups = [here, near[0], far[0], far[1]]
    with jax.named_scope("proj3_away"):
        me, away = project(me, [x3], w, block, 1)
    me = spread(me, "proj3", x3, away, [x3], [groups[2][2], others[0]])
    with jax.named_scope("laid_out"):
        me, (seq, cot) = laid_out(me, groups, ups)
    high = x_own.shape[0]
    with jax.named_scope("gate1"):
        me, (g1,) = gate(me, seq, cot, feature_taps, inner_taps, high, (1,), late=others[1:2])
    y1 = send("g1_y", g1, "row", CORES)
    with jax.named_scope("gate230"):
        me, (g, g30, g2) = gate(me, seq, cot, feature_taps, inner_taps, high, (2, 3, 0), g1)
    with jax.named_scope("relay_g2"):
        me, (g2,) = relay(me, g2, late=[y1])
    y2 = send("g2_y", g2, "row", CORES)
    c, x = send("g_core", g, "row", 1), send("g_x", g, "dp", 1)
    cy1, cy2 = send("gy1_core", y1, "row", 1), send("gy2_core", y2, "row", 1)
    with jax.named_scope("input_grads1"):
        pieces = [(g, [0]), (c, [0]), (y1, [None]), (cy1, [None])]
        me, (share1,) = input_grads(me, pieces, w)
    passed = send("share1", share1, "col", 1)
    with jax.named_scope("relay_g30"):
        me, (g30,) = relay(me, g30)
    y30 = send("g30_y", g30, "row", CORES)

    def whole(a):
        return [(a, 3), (a, 0), (a, 1), (a, 2)]

    def cut(last, one, two):
        return [(last, 1), (one, None), (two, None), (last, 0)]

    def halves(low, high):
        return [(high, 1), (low, 0), (low, 1), (high, 0)]

    with jax.named_scope("weight_grads_near_own"):
        blocks = [(0, whole(g)), (1, whole(c))]
        me, begun = weight_grads(me, None, xts, blocks, width, final=False)
    with jax.named_scope("relay_x"):
        me, (x,) = relay(me, x, late=others[2:])
    xy12, cx = send("gx12_y", x[:2], "row", CORES), send("gx_core", x, "row", 1)
    with jax.named_scope("input_grads2"):
        pieces = [(g, [1]), (c, [1]), (y2, [None]), (cy2, [None])]
        me, (share2,) = input_grads(me, pieces, w)
    with jax.named_scope("total2"):
        me, share2 = total(me, [share2, passed])
    passed = send("share2", share2, "col", 1)
    with jax.named_scope("relay_y30"):
        me, (y30,) = relay(me, y30)
    xy30, cy30 = send("gy30_x", y30, "dp", 1), send("gy30_core", y30, "row", 1)
    with jax.named_scope("input_grads30"):
        pieces = [(g, [2, 3]), (c, [2, 3]), (y30, [0, 1]), (cy30, [0, 1])]
        me, (share3, share0) = input_grads(me, pieces, w)
    with jax.named_scope("weight_grads_near"):
        blocks = [(0, whole(x)), (1, whole(cx))]
        me, grad_w = weight_grads(me, None, others, blocks, width, begun)
    with jax.named_scope("total3"):
        me, share3 = total(me, [share3, passed])
    passed = send("share3", share3, "col", 1)
    with jax.named_scope("relay_xy"):
        me, (xy12, xy30) = relay(me, xy12, xy30)
    cxy12, cxy30 = send("gxy12_core", xy12, "row", 1), send("gxy30_core", xy30, "row", 1)
    with jax.named_scope("weight_grads_far"):
        blocks = [
            (2, cut(y30, y1, y2) + halves(xy12, xy30)),
            (3, cut(cy30, cy1, cy2) + halves(cxy12, cxy30)),
        ]
        me, grad_w = weight_grads(me, grad_w, xts + others, blocks, width)
    with jax.named_scope("total0"):
        me, grad_in = total(me, [share0, passed])
    return (grad_in[None], jnp.transpose(grad_w, (1, 0, 2)))


def solution(mesh):
    placed = (
        P("dp", "col", "row"),
        P("row", None, "col"),
        P(None, None, "col"),
        P(None, "col"),
        P("dp", "row", "col"),
    )

    def on_device(inputs, weights, feature_taps, inner_taps, grad_out):
        n_row = mesh.shape["row"]
        fits = weights.shape[2] % (n_row * LANES) == 0 and inputs.shape[1] % LANES == 0
        small = n_row == 2 * CORES and mesh.shape["dp"] == 2 and mesh.shape["col"] == 4
        plan = by_channels if fits and small else by_tokens
        return plan(inputs, weights, feature_taps, inner_taps, grad_out)

    return jax.shard_map(
        on_device,
        mesh=mesh,
        in_specs=placed,
        out_specs=(P("dp", "col", "row"), P("row", None, "col")),
        check_vma=False,
    )
```

```python
import math

import jax
import jax.numpy as jnp
from jax import lax
from jax.experimental import pallas as pl
from jax.experimental.pallas import tpu as pltpu
from jax.sharding import PartitionSpec as P

LANES = 128
PAD = 8
CORES = 2


def shifted(shard, axis, by):
    length = lax.axis_size(axis)
    pairs = [(i, i + by) for i in range(length) if 0 <= i + by < length]
    return lax.ppermute(shard, axis, pairs)


def with_halo(cells, axis, width):
    head = shifted(cells[:width], axis, -1)
    tail = shifted(cells[-width:], axis, 1)
    return jnp.concatenate([tail, cells, head], axis=0)


def causal(seq, taps):
    total = taps[0] * seq
    for lag in range(1, taps.shape[0]):
        pad = jnp.zeros((lag,) + seq.shape[1:], jnp.float32)
        total = total + taps[lag] * jnp.concatenate([pad, seq[:-lag]], axis=0)
    return total


def anticausal(seq, taps):
    total = taps[0] * seq
    for lag in range(1, taps.shape[0]):
        pad = jnp.zeros((lag,) + seq.shape[1:], jnp.float32)
        total = total + taps[lag] * jnp.concatenate([seq[lag:], pad], axis=0)
    return total


def rounded(value):
    return lax.optimization_barrier(value.astype(jnp.bfloat16)).astype(jnp.float32)


def by_tokens(inputs, weights, feature_taps, inner_taps, grad_out):
    tile = inputs[0]
    upstream_tile = grad_out[0]
    rows_dev = upstream_tile.shape[0]
    width_row = weights.shape[0]
    width_col = weights.shape[2]
    margin = feature_taps.shape[0] - 1 + (inner_taps.shape[0] - 1)
    flat_w = weights.reshape(width_row, 3 * width_col)
    columns = lax.all_gather(tile, "col", axis=0, tiled=True)
    proj = lax.psum_scatter(
        jnp.dot(columns, flat_w, preferred_element_type=jnp.float32).astype(jnp.bfloat16),
        "row",
        scatter_dimension=0,
        tiled=True,
    )
    length = rows_dev + 2 * margin
    window = with_halo(proj, "row", margin).astype(jnp.float32).reshape(length, 3, width_col)
    after = shifted(upstream_tile[:margin], "row", -1)
    upstream = jnp.concatenate(
        [
            jnp.zeros((margin, width_col), jnp.float32),
            upstream_tile.astype(jnp.float32),
            after.astype(jnp.float32),
        ],
        axis=0,
    )
    mixed = causal(window, feature_taps)
    query = mixed[:, 0]
    key = mixed[:, 1]
    value = mixed[:, 2]
    product = rounded(key * value)
    inner = causal(product, inner_taps)
    grad_query = upstream * inner
    grad_product = anticausal(upstream * query, inner_taps)
    grad_mixed = jnp.stack([grad_query, grad_product * value, grad_product * key], axis=1)
    grad_proj = anticausal(grad_mixed, feature_taps)[margin : margin + rows_dev].astype(
        jnp.bfloat16
    )
    gathered = lax.all_gather(grad_proj.reshape(rows_dev, 3 * width_col), "row", axis=0, tiled=True)
    grad_x = lax.psum_scatter(
        lax.dot_general(
            gathered, flat_w, (((1,), (1,)), ((), ())), preferred_element_type=jnp.float32
        ).astype(jnp.bfloat16),
        "col",
        scatter_dimension=0,
        tiled=True,
    )
    local = lax.dot_general(
        columns, gathered, (((0,), (0,)), ((), ())), preferred_element_type=jnp.float32
    )
    grad_w = lax.psum(local.astype(jnp.bfloat16), "dp").astype(jnp.float32)
    return (grad_x[None], grad_w.reshape(width_row, 3, width_col))


def swap(value, axis, step):
    size = lax.axis_size(axis)
    return lax.ppermute(value, axis, [(i, i ^ step) for i in range(size)])


LINE = (0, 2, 3, 1)


def along(value, steps):
    size = len(LINE)
    pairs = [(LINE[i], LINE[(i + steps) % size]) for i in range(size)]
    return lax.ppermute(value, "col", pairs)


def behind(z, steps):
    for _ in range(steps):
        z = jnp.where(z < 2, 2 * z + 1, 2 * z - 4)
    return z


VMEM = pl.BlockSpec(memory_space=pltpu.VMEM)
SMEM = pl.BlockSpec(memory_space=pltpu.SMEM)
HBM = pl.BlockSpec(memory_space=pltpu.HBM)
ANY = pl.BlockSpec(memory_space=pl.ANY)


PER_MICRO = 1.1e9


def hbm(value):
    return pltpu.with_memory_space_constraint(value, pltpu.HBM)


def bf16(*shape):
    return jax.ShapeDtypeStruct(shape, jnp.bfloat16)


def local(
    me, body, outs, ins, micros, in_specs=None, scratch=(), out_specs=None, aliases=None, late=(), placed=True
):
    place, *turn = me
    first = [place] if placed else []
    late = [*turn, *late]
    n_in = len(first) + len(ins)

    def ordered(*refs):
        body(*refs[:n_in], *refs[n_in + len(late) + 1 :])

    turns = {n_in: 0} if turn else {}
    moved = {len(first) + i: 1 + o for i, o in (aliases or {}).items()}
    turn, *results = pl.pallas_call(
        ordered,
        out_shape=[jax.ShapeDtypeStruct((8, LANES), jnp.float32), *outs],
        in_specs=[SMEM] * len(first) + [*(in_specs or [VMEM] * len(ins)), *[ANY] * len(late)],
        out_specs=[ANY, *(out_specs or [VMEM] * len(outs))],
        scratch_shapes=list(scratch),
        input_output_aliases={**turns, **moved},
        compiler_params=pltpu.CompilerParams(vmem_limit_bytes=16 * 2**20),
        cost_estimate=pl.CostEstimate(
            flops=int(micros * PER_MICRO), bytes_accessed=1, transcendentals=0
        ),
    )(*first, *ins, *late)
    return (place, turn), results


def multiply(x, w_ref, c, block_at, out_ref):
    block = out_ref.shape[-1]
    at = pl.multiple_of(block_at * block, LANES)
    out_ref[c] = jnp.dot(
        x, w_ref[c, :, pl.ds(at, block)], preferred_element_type=jnp.float32
    ).astype(jnp.bfloat16)


def begin(me, x, up, w, block):
    parts, depth, width = w.shape
    high = up.shape[0]

    def body(me_ref, x_hbm, up_hbm, w_hbm, *refs):
        w_ref, x_ref, there_ref, here_ref, across_ref, *away_refs, place_ref, up_ref, sems = refs
        row = me_ref[0]
        place_ref[0] = row
        place_ref[1] = me_ref[1]
        loads = [pltpu.make_async_copy(up_hbm, up_ref, sems.at[0])]
        loads += [pltpu.make_async_copy(x_hbm, x_ref, sems.at[1])]
        loads += [
            pltpu.make_async_copy(w_hbm.at[c], w_ref.at[c], sems.at[2 + c]) for c in range(parts)
        ]
        for load in loads:
            load.start()
        loads[0].wait()
        for j in range(2):
            at = pl.multiple_of((row ^ (2 * j + 1)) * block, LANES)
            there_ref[j] = up_ref[:, pl.ds(at, block)]
        here_ref[...] = up_ref[:, pl.ds(pl.multiple_of(row * block, LANES), block)]
        across_ref[...] = up_ref[:, pl.ds(pl.multiple_of((row ^ 2) * block, LANES), block)]
        loads[1].wait()
        for c in range(parts):
            loads[2 + c].wait()
            for j in range(2):
                multiply(x_ref[...], w_ref, c, row ^ (2 * j + 1), away_refs[j])

    return local(
        me,
        body,
        [
            pltpu.VMEM(w.shape, w.dtype),
            pltpu.VMEM(x.shape, x.dtype),
            bf16(2, high, block),
            bf16(high, block),
            bf16(high, block),
            bf16(parts, high, block),
            bf16(parts, high, block),
            pltpu.SMEM((2,), jnp.int32),
        ],
        [hbm(x), hbm(up), hbm(w)],
        3.5,
        [HBM, HBM, HBM],
        out_specs=[VMEM] * 7 + [SMEM],
        scratch=[
            pltpu.VMEM(up.shape, up.dtype),
            pltpu.SemaphoreType.DMA((2 + parts,)),
        ],
    )


def project(me, xs, w, block, other, late=()):
    parts = w.shape[0]
    tall = xs[0].shape[0] * len(xs)

    def body(me_ref, *refs):
        w_ref, out_refs = refs[len(xs)], refs[len(xs) + 1 :]
        x = jnp.concatenate([x[...] for x in refs[: len(xs)]], axis=0)
        for j in (1, 0):
            for c in range(parts):
                multiply(x, w_ref, c, me_ref[0] ^ (2 * j + other), out_refs[j])

    outs = [bf16(parts, tall, block)] * 2
    return local(me, body, outs, [*xs, w], 2.0 * len(xs), late=late)


def laid_out(me, groups, ups, late=()):
    parts, _, block = groups[0][2].shape
    tokens = sum(far.shape[1] for _, _, far in groups)
    high = ups[0].shape[0]
    n_in = 3 * len(groups)

    def body(me_ref, *refs):
        ins, up_refs, (seq, cot) = refs[:n_in], refs[n_in:-2], refs[-2:]
        row, z = me_ref[0], me_ref[1]
        for at in (0, PAD + tokens):
            seq[:, at : at + PAD, :] = jnp.zeros((parts, PAD, block), jnp.float32)
            cot[at : at + PAD, :] = jnp.zeros((PAD, block), jnp.float32)
        for s in range(len(groups)):
            keep, near, far = ins[3 * s : 3 * s + 3]
            to = pl.multiple_of(behind(z, s) * high + PAD, PAD)
            for c in range(parts):
                total = keep[c].astype(jnp.float32) + near[c].astype(jnp.float32)
                total = total + far[c].astype(jnp.float32)
                seq[c, pl.ds(to, high), :] = total.astype(jnp.bfloat16).astype(jnp.float32)
        for i, up in enumerate(up_refs):
            to = pl.multiple_of((row ^ i) * high + PAD, PAD)
            cot[pl.ds(to, high), :] = up[...].astype(jnp.float32)

    operands = [a for group in groups for a in group] + list(ups)
    outs = [
        pltpu.VMEM((parts, tokens + 2 * PAD, block), jnp.float32),
        pltpu.VMEM((tokens + 2 * PAD, block), jnp.float32),
    ]
    return local(me, body, outs, operands, 0.6, late=late)


def gate(me, seq, cot, feature_taps, inner_taps, high, shards, one=None, late=()):
    lags, parts, _ = feature_taps.shape
    long_lags = inner_taps.shape[0]
    block = cot.shape[1]
    window = high + 2 * PAD
    ins = [seq, cot, feature_taps, inner_taps] + ([] if one is None else [one])

    def back(value, lag):
        return pltpu.roll(value, lag, 0) if lag else value

    def ahead(value, lag):
        return pltpu.roll(value, window - lag, 0) if lag else value

    def body(me_ref, seq_ref, cot_ref, taps_ref, long_ref, *refs):
        row, z = me_ref[0], me_ref[1]
        if one is not None:
            one_ref, all_ref, last_ref, two_ref = refs
            all_ref[0] = one_ref[...]

        @pl.loop(0, block // LANES)
        def _(half):
            lanes = pl.ds(pl.multiple_of(half * LANES, LANES), LANES)
            wide = pl.ds(pl.multiple_of(row * block + half * LANES, LANES), LANES)
            taps = [[taps_ref[s, c : c + 1, wide] for c in range(parts)] for s in range(lags)]
            long_taps = [long_ref[s : s + 1, wide] for s in range(long_lags)]
            for s in shards:
                rows = pl.ds(pl.multiple_of(behind(z, s) * high, PAD), window)
                mixed = []
                for c in range(parts):
                    proj = seq_ref[c, rows, lanes]
                    total = taps[0][c] * proj
                    for lag in range(1, lags):
                        total = total + taps[lag][c] * back(proj, lag)
                    mixed.append(total)
                query, key, value = mixed
                upstream = cot_ref[rows, lanes]
                product = (key * value).astype(jnp.bfloat16).astype(jnp.float32)
                inner = long_taps[0] * product
                for lag in range(1, long_lags):
                    inner = inner + long_taps[lag] * back(product, lag)
                grad_inner = upstream * query
                grad_product = long_taps[0] * grad_inner
                for lag in range(1, long_lags):
                    grad_product = grad_product + long_taps[lag] * ahead(grad_inner, lag)
                grads = (upstream * inner, grad_product * value, grad_product * key)
                for c, grad in enumerate(grads):
                    total = taps[0][c] * grad
                    for lag in range(1, lags):
                        total = total + taps[lag][c] * ahead(grad, lag)
                    done = total[PAD : PAD + high].astype(jnp.bfloat16)
                    if one is None:
                        refs[0][c, :, lanes] = done
                        continue
                    all_ref[(s - 1) % 4, c, :, lanes] = done
                    if s == 2:
                        two_ref[c, :, lanes] = done
                    else:
                        last_ref[(s - 3) % 4, c, :, lanes] = done

    single = (parts, high, block)
    outs = [bf16(*single)]
    if one is not None:
        outs = [bf16(4, *single), bf16(2, *single), *outs]
    return local(me, body, outs, ins, 0.8 * len(shards), late=late)


def relay(me, *values, late=()):
    return local(
        me,
        lambda *refs: None,
        [jax.ShapeDtypeStruct(value.shape, value.dtype) for value in values],
        values,
        0.01,
        [ANY] * len(values),
        out_specs=[ANY] * len(values),
        aliases={i: i for i in range(len(values))},
        late=late,
        placed=False,
    )


def input_grads(me, pieces, w, late=()):
    parts, depth, width = w.shape
    high, block = pieces[0][0].shape[-2:]
    shards = len(pieces[0][1])

    def body(me_ref, *refs):
        w_ref, outs, wide = refs[len(pieces)], refs[len(pieces) + 1 : -1], refs[-1]
        for i, (g, (_, which)) in enumerate(zip(refs, pieces)):
            at = pl.multiple_of((me_ref[0] ^ i) * block, LANES)
            for s, index in enumerate(which):
                shard = g if index is None else g.at[index]
                wide[:, s * high : (s + 1) * high, pl.ds(at, block)] = shard[...]
        total = None
        for c in range(parts):
            term = lax.dot_general(
                wide[c], w_ref[c], (((1,), (1,)), ((), ())), preferred_element_type=jnp.float32
            )
            total = term if total is None else total + term
        for s, out in enumerate(outs):
            out[...] = total[s * high : (s + 1) * high].astype(jnp.bfloat16)

    return local(
        me,
        body,
        [bf16(high, depth)] * shards,
        [*(g for g, _ in pieces), w],
        0.8 * shards,
        scratch=[pltpu.VMEM((parts, shards * high, width), jnp.bfloat16)],
        late=late,
    )


def turned(me, xs, late=()):
    high, depth = xs[0].shape

    def body(*refs):
        for s, x in enumerate(refs[:-1]):
            refs[-1][:, s * high : (s + 1) * high] = x[...].T

    me, (out,) = local(me, body, [bf16(depth, high * len(xs))], xs, 0.1 * len(xs), late=late, placed=False)
    return me, out


def weight_grads(me, done, xts, blocks, width, begun=None, final=True):
    depth = xts[0].shape[0]
    flat = [p for _, pieces in blocks for p in pieces]
    parts, high, block = flat[0][0].shape[-3:]
    unique = []
    for g, _ in flat:
        if not any(g is u for u in unique):
            unique.append(g)
    spot = {id(u): n for n, u in enumerate(unique)}
    tokens = high * len(blocks[0][1])
    wide = block * len(blocks)
    cuts, spare = 4, 4
    tall = depth // cuts
    n_in = len(xts) + len(unique) + (begun is not None) + (done is not None)

    def body(me_ref, *refs):
        x_refs, g_refs = refs[: len(xts)], refs[len(xts) : n_in]
        out_ref, xt, gs, *rest = refs[n_in:]
        at = 0
        for x in x_refs:
            xt[:, at : at + x.shape[1]] = x[...]
            at += x.shape[1]
        row = me_ref[0]
        start = pl.multiple_of((row ^ blocks[0][0]) // CORES * wide, wide)
        copies = []
        for c in range(parts):
            for i, pieces in blocks:
                lanes = pl.ds(pl.multiple_of((row ^ i) % CORES * block, LANES), block)
                for k, (g, index) in enumerate(pieces):
                    g_ref = g_refs[spot[id(g)]]
                    shard = g_ref if index is None else g_ref.at[index]
                    gs[c % 2, k * high : (k + 1) * high, lanes] = shard[c]
            for m in range(cuts):
                rows = pl.ds(m * tall, tall)
                part = jnp.dot(xt[rows, :], gs[c % 2], preferred_element_type=jnp.float32)
                if begun is not None:
                    part = part + g_refs[len(unique)][c, rows, :]
                if not final:
                    out_ref[c, rows, :] = part
                    continue
                held, sems = rest
                slot = len(copies) % spare
                if len(copies) >= spare:
                    copies[-spare].wait()
                held[slot] = part
                copies.append(
                    pltpu.make_async_copy(
                        held.at[slot], out_ref.at[c, rows, pl.ds(start, wide)], sems.at[slot]
                    )
                )
                copies[-1].start()
        for copy in copies[-spare:]:
            copy.wait()

    ins = [*xts, *unique] + ([] if begun is None else [begun])
    specs = [VMEM] * len(ins)
    aliases = {}
    if done is not None:
        aliases = {len(ins): 0}
        ins.append(done)
        specs.append(ANY)
    scratch = [
        pltpu.VMEM((depth, tokens), jnp.bfloat16),
        pltpu.VMEM((2, tokens, wide), jnp.bfloat16),
    ]
    out = pltpu.VMEM((parts, depth, wide), jnp.float32)
    if final:
        out = jax.ShapeDtypeStruct((parts, depth, width), jnp.float32)
        scratch += [
            pltpu.VMEM((spare, tall, wide), jnp.float32),
            pltpu.SemaphoreType.DMA((spare,)),
        ]
    me, (out,) = local(
        me,
        body,
        [out],
        ins,
        6.0 if final else 4.0,
        specs,
        scratch=scratch,
        out_specs=[ANY if final else VMEM],
        aliases=aliases,
    )
    return me, out


def total(me, terms, late=()):
    def body(*refs):
        acc = refs[0][...].astype(jnp.float32)
        for ref in refs[1:-1]:
            acc = acc + ref[...].astype(jnp.float32)
        refs[-1][...] = acc.astype(jnp.bfloat16)

    me, (out,) = local(me, body, [bf16(*terms[0].shape)], terms, 0.05, late=late, placed=False)
    return me, out


def by_channels(inputs, weights, feature_taps, inner_taps, grad_out):
    x_own = inputs[0]
    block = weights.shape[2] // lax.axis_size("row")
    width = weights.shape[2]
    me = (jnp.stack([lax.axis_index("row"), lax.axis_index("col")]).astype(jnp.int32),)

    def send(name, value, axis, step):
        with jax.named_scope(name):
            return along(value, step) if axis == "col" else swap(value, axis, step)

    x1 = send("x1", x_own, "col", 1)
    x2 = send("x2", x1, "col", 1)
    x3 = send("x3", x2, "col", 1)
    with jax.named_scope("begin"):
        me, (w, x_own, there, here, across, *away, place) = begin(
            me, x_own, grad_out[0], jnp.transpose(weights, (1, 0, 2)), block
        )
    me = (place, *me[1:])
    def spread(me, name, x, away, turn=(), late=()):
        got = [send(name + "_core%d" % j, away[j], "row", 1) for j in range(2)]
        with jax.named_scope(name + "_keep"):
            me, keep = project(me, [x], w, block, 0)
        with jax.named_scope(name + "_join"):
            me, both = total(me, [keep[1], got[1]], [got[0]])
        groups.append((keep[0], got[0], send(name + "_y", both, "row", CORES)))
        if turn:
            with jax.named_scope(name + "_turned"):
                me, xt = turned(me, turn, late)
            xts.append(xt)
            others.append(send(name + "_xt_x", xt, "dp", 1))
        return me

    groups, xts, others = [], [], []
    me = spread(me, "proj0", x_own, away)
    with jax.named_scope("proj1_away"):
        me, away = project(me, [x1], w, block, 1)
    me = spread(me, "proj1", x1, away, [x_own, x1], [groups[0][2]])
    with jax.named_scope("proj2_away"):
        me, away = project(me, [x2], w, block, 1)
    me = spread(me, "proj2", x2, away, [x2], [groups[1][2]])
    with jax.named_scope("relay_up"):
        me, (there,) = relay(me, there)
    near = send("up_core", there, "row", 1)
    far = send("up_y", jnp.stack([across, near[1]]), "row", CORES)
    ups = [here, near[0], far[0], far[1]]
    with jax.named_scope("proj3_away"):
        me, away = project(me, [x3], w, block, 1)
    me = spread(me, "proj3", x3, away, [x3], [groups[2][2], others[0]])
    with jax.named_scope("laid_out"):
        me, (seq, cot) = laid_out(me, groups, ups)
    high = x_own.shape[0]
    with jax.named_scope("gate1"):
        me, (g1,) = gate(me, seq, cot, feature_taps, inner_taps, high, (1,), late=others[1:2])
    y1 = send("g1_y", g1, "row", CORES)
    c1 = send("g1_core", g1, "row", 1)
    with jax.named_scope("gate230"):
        me, (g, g30, g2) = gate(me, seq, cot, feature_taps, inner_taps, high, (2, 3, 0), g1)
    c2, c30 = send("g2_core", g2, "row", 1), send("g30_core", g30, "row", 1)
    with jax.named_scope("relay_g2"):
        me, (g2,) = relay(me, g2, late=[y1])
    y2 = send("g2_y", g2, "row", CORES)
    x = send("g_x", g, "dp", 1)
    cy1, cy2 = send("gy1_core", y1, "row", 1), send("gy2_core", y2, "row", 1)
    with jax.named_scope("input_grads1"):
        pieces = [(g, [0]), (c1, [None]), (y1, [None]), (cy1, [None])]
        me, (share1,) = input_grads(me, pieces, w)
    passed = send("share1", share1, "col", 1)
    with jax.named_scope("relay_g30"):
        me, (g30,) = relay(me, g30)
    y30 = send("g30_y", g30, "row", CORES)

    def whole(a):
        return [(a, 3), (a, 0), (a, 1), (a, 2)]

    def cut(last, one, two):
        return [(last, 1), (one, None), (two, None), (last, 0)]

    def halves(low, high):
        return [(high, 1), (low, 0), (low, 1), (high, 0)]

    with jax.named_scope("weight_grads_near_own"):
        blocks = [(0, whole(g)), (1, cut(c30, c1, c2))]
        me, begun = weight_grads(me, None, xts, blocks, width, final=False)
    with jax.named_scope("input_grads2"):
        pieces = [(g, [1]), (c2, [None]), (y2, [None]), (cy2, [None])]
        me, (share2,) = input_grads(me, pieces, w)
    with jax.named_scope("relay_x"):
        me, (x,) = relay(me, x, late=others[2:])
    xy12, cx = send("gx12_y", x[:2], "row", CORES), send("gx_core", x, "row", 1)
    with jax.named_scope("total2"):
        me, share2 = total(me, [share2, passed])
    passed = send("share2", share2, "col", 1)
    with jax.named_scope("relay_y30"):
        me, (y30,) = relay(me, y30)
    xy30, cy30 = send("gy30_x", y30, "dp", 1), send("gy30_core", y30, "row", 1)
    with jax.named_scope("input_grads30"):
        pieces = [(g, [2, 3]), (c30, [0, 1]), (y30, [0, 1]), (cy30, [0, 1])]
        me, (share3, share0) = input_grads(me, pieces, w)
    with jax.named_scope("weight_grads_near"):
        blocks = [(0, whole(x)), (1, whole(cx))]
        me, grad_w = weight_grads(me, None, others, blocks, width, begun)
    with jax.named_scope("total3"):
        me, share3 = total(me, [share3, passed])
    passed = send("share3", share3, "col", 1)
    with jax.named_scope("relay_xy"):
        me, (xy12, xy30) = relay(me, xy12, xy30)
    cxy12, cxy30 = send("gxy12_core", xy12, "row", 1), send("gxy30_core", xy30, "row", 1)
    with jax.named_scope("weight_grads_far"):
        blocks = [
            (2, cut(y30, y1, y2) + halves(xy12, xy30)),
            (3, cut(cy30, cy1, cy2) + halves(cxy12, cxy30)),
        ]
        me, grad_w = weight_grads(me, grad_w, xts + others, blocks, width)
    with jax.named_scope("total0"):
        me, grad_in = total(me, [share0, passed])
    return (grad_in[None], jnp.transpose(grad_w, (1, 0, 2)))


def solution(mesh):
    placed = (
        P("dp", "col", "row"),
        P("row", None, "col"),
        P(None, None, "col"),
        P(None, "col"),
        P("dp", "row", "col"),
    )

    def on_device(inputs, weights, feature_taps, inner_taps, grad_out):
        n_row = mesh.shape["row"]
        fits = weights.shape[2] % (n_row * LANES) == 0 and inputs.shape[1] % LANES == 0
        small = n_row == 2 * CORES and mesh.shape["dp"] == 2 and mesh.shape["col"] == 4
        plan = by_channels if fits and small else by_tokens
        return plan(inputs, weights, feature_taps, inner_taps, grad_out)

    return jax.shard_map(
        on_device,
        mesh=mesh,
        in_specs=placed,
        out_specs=(P("dp", "col", "row"), P("row", None, "col")),
        check_vma=False,
    )
```

```python
import math

import jax
import jax.numpy as jnp
from jax import lax
from jax.experimental import pallas as pl
from jax.experimental.pallas import tpu as pltpu
from jax.sharding import PartitionSpec as P

LANES = 128
PAD = 8
CORES = 2


def shifted(shard, axis, by):
    length = lax.axis_size(axis)
    pairs = [(i, i + by) for i in range(length) if 0 <= i + by < length]
    return lax.ppermute(shard, axis, pairs)


def with_halo(cells, axis, width):
    head = shifted(cells[:width], axis, -1)
    tail = shifted(cells[-width:], axis, 1)
    return jnp.concatenate([tail, cells, head], axis=0)


def causal(seq, taps):
    total = taps[0] * seq
    for lag in range(1, taps.shape[0]):
        pad = jnp.zeros((lag,) + seq.shape[1:], jnp.float32)
        total = total + taps[lag] * jnp.concatenate([pad, seq[:-lag]], axis=0)
    return total


def anticausal(seq, taps):
    total = taps[0] * seq
    for lag in range(1, taps.shape[0]):
        pad = jnp.zeros((lag,) + seq.shape[1:], jnp.float32)
        total = total + taps[lag] * jnp.concatenate([seq[lag:], pad], axis=0)
    return total


def rounded(value):
    return lax.optimization_barrier(value.astype(jnp.bfloat16)).astype(jnp.float32)


def by_tokens(inputs, weights, feature_taps, inner_taps, grad_out):
    tile = inputs[0]
    upstream_tile = grad_out[0]
    rows_dev = upstream_tile.shape[0]
    width_row = weights.shape[0]
    width_col = weights.shape[2]
    margin = feature_taps.shape[0] - 1 + (inner_taps.shape[0] - 1)
    flat_w = weights.reshape(width_row, 3 * width_col)
    columns = lax.all_gather(tile, "col", axis=0, tiled=True)
    proj = lax.psum_scatter(
        jnp.dot(columns, flat_w, preferred_element_type=jnp.float32).astype(jnp.bfloat16),
        "row",
        scatter_dimension=0,
        tiled=True,
    )
    length = rows_dev + 2 * margin
    window = with_halo(proj, "row", margin).astype(jnp.float32).reshape(length, 3, width_col)
    after = shifted(upstream_tile[:margin], "row", -1)
    upstream = jnp.concatenate(
        [
            jnp.zeros((margin, width_col), jnp.float32),
            upstream_tile.astype(jnp.float32),
            after.astype(jnp.float32),
        ],
        axis=0,
    )
    mixed = causal(window, feature_taps)
    query = mixed[:, 0]
    key = mixed[:, 1]
    value = mixed[:, 2]
    product = rounded(key * value)
    inner = causal(product, inner_taps)
    grad_query = upstream * inner
    grad_product = anticausal(upstream * query, inner_taps)
    grad_mixed = jnp.stack([grad_query, grad_product * value, grad_product * key], axis=1)
    grad_proj = anticausal(grad_mixed, feature_taps)[margin : margin + rows_dev].astype(
        jnp.bfloat16
    )
    gathered = lax.all_gather(grad_proj.reshape(rows_dev, 3 * width_col), "row", axis=0, tiled=True)
    grad_x = lax.psum_scatter(
        lax.dot_general(
            gathered, flat_w, (((1,), (1,)), ((), ())), preferred_element_type=jnp.float32
        ).astype(jnp.bfloat16),
        "col",
        scatter_dimension=0,
        tiled=True,
    )
    local = lax.dot_general(
        columns, gathered, (((0,), (0,)), ((), ())), preferred_element_type=jnp.float32
    )
    grad_w = lax.psum(local.astype(jnp.bfloat16), "dp").astype(jnp.float32)
    return (grad_x[None], grad_w.reshape(width_row, 3, width_col))


def swap(value, axis, step):
    size = lax.axis_size(axis)
    return lax.ppermute(value, axis, [(i, i ^ step) for i in range(size)])


LINE = (0, 2, 3, 1)


def along(value, steps):
    size = len(LINE)
    pairs = [(LINE[i], LINE[(i + steps) % size]) for i in range(size)]
    return lax.ppermute(value, "col", pairs)


def behind(z, steps):
    for _ in range(steps):
        z = jnp.where(z < 2, 2 * z + 1, 2 * z - 4)
    return z


VMEM = pl.BlockSpec(memory_space=pltpu.VMEM)
SMEM = pl.BlockSpec(memory_space=pltpu.SMEM)
HBM = pl.BlockSpec(memory_space=pltpu.HBM)
ANY = pl.BlockSpec(memory_space=pl.ANY)


PER_MICRO = 1.1e9


def hbm(value):
    return pltpu.with_memory_space_constraint(value, pltpu.HBM)


def bf16(*shape):
    return jax.ShapeDtypeStruct(shape, jnp.bfloat16)


def local(
    me, body, outs, ins, micros, in_specs=None, scratch=(), out_specs=None, aliases=None, late=(), placed=True
):
    place, *turn = me
    first = [place] if placed else []
    late = [*turn, *late]
    n_in = len(first) + len(ins)

    def ordered(*refs):
        body(*refs[:n_in], *refs[n_in + len(late) + 1 :])

    turns = {n_in: 0} if turn else {}
    moved = {len(first) + i: 1 + o for i, o in (aliases or {}).items()}
    turn, *results = pl.pallas_call(
        ordered,
        out_shape=[jax.ShapeDtypeStruct((8, LANES), jnp.float32), *outs],
        in_specs=[SMEM] * len(first) + [*(in_specs or [VMEM] * len(ins)), *[ANY] * len(late)],
        out_specs=[ANY, *(out_specs or [VMEM] * len(outs))],
        scratch_shapes=list(scratch),
        input_output_aliases={**turns, **moved},
        compiler_params=pltpu.CompilerParams(vmem_limit_bytes=16 * 2**20),
        cost_estimate=pl.CostEstimate(
            flops=int(micros * PER_MICRO), bytes_accessed=1, transcendentals=0
        ),
    )(*first, *ins, *late)
    return (place, turn), results


def multiply(x, w_ref, c, block_at, out_ref):
    block = out_ref.shape[-1]
    at = pl.multiple_of(block_at * block, LANES)
    out_ref[c] = jnp.dot(
        x, w_ref[c, :, pl.ds(at, block)], preferred_element_type=jnp.float32
    ).astype(jnp.bfloat16)


def begin(me, x, up, w, block):
    parts, depth, width = w.shape
    high = up.shape[0]

    def body(me_ref, x_hbm, up_hbm, w_hbm, *refs):
        w_ref, x_ref, there_ref, here_ref, across_ref, *away_refs, place_ref, up_ref, sems = refs
        row = me_ref[0]
        place_ref[0] = row
        place_ref[1] = me_ref[1]
        loads = [pltpu.make_async_copy(up_hbm, up_ref, sems.at[0])]
        loads += [pltpu.make_async_copy(x_hbm, x_ref, sems.at[1])]
        loads += [
            pltpu.make_async_copy(w_hbm.at[c], w_ref.at[c], sems.at[2 + c]) for c in range(parts)
        ]
        for load in loads:
            load.start()
        loads[0].wait()
        for j in range(2):
            at = pl.multiple_of((row ^ (2 * j + 1)) * block, LANES)
            there_ref[j] = up_ref[:, pl.ds(at, block)]
        here_ref[...] = up_ref[:, pl.ds(pl.multiple_of(row * block, LANES), block)]
        across_ref[...] = up_ref[:, pl.ds(pl.multiple_of((row ^ 2) * block, LANES), block)]
        loads[1].wait()
        for c in range(parts):
            loads[2 + c].wait()
            for j in range(2):
                multiply(x_ref[...], w_ref, c, row ^ (2 * j + 1), away_refs[j])

    return local(
        me,
        body,
        [
            pltpu.VMEM(w.shape, w.dtype),
            pltpu.VMEM(x.shape, x.dtype),
            bf16(2, high, block),
            bf16(high, block),
            bf16(high, block),
            bf16(parts, high, block),
            bf16(parts, high, block),
            pltpu.SMEM((2,), jnp.int32),
        ],
        [hbm(x), hbm(up), hbm(w)],
        3.5,
        [HBM, HBM, HBM],
        out_specs=[VMEM] * 7 + [SMEM],
        scratch=[
            pltpu.VMEM(up.shape, up.dtype),
            pltpu.SemaphoreType.DMA((2 + parts,)),
        ],
    )


def project(me, xs, w, block, other, late=()):
    parts = w.shape[0]
    tall = xs[0].shape[0] * len(xs)

    def body(me_ref, *refs):
        w_ref, out_refs = refs[len(xs)], refs[len(xs) + 1 :]
        x = jnp.concatenate([x[...] for x in refs[: len(xs)]], axis=0)
        for j in (1, 0):
            for c in range(parts):
                multiply(x, w_ref, c, me_ref[0] ^ (2 * j + other), out_refs[j])

    outs = [bf16(parts, tall, block)] * 2
    return local(me, body, outs, [*xs, w], 2.0 * len(xs), late=late)


def laid_out(me, groups, ups, late=()):
    parts, _, block = groups[0][2].shape
    tokens = sum(far.shape[1] for _, _, far in groups)
    high = ups[0].shape[0]
    n_in = 3 * len(groups)

    def body(me_ref, *refs):
        ins, up_refs, (seq, cot) = refs[:n_in], refs[n_in:-2], refs[-2:]
        row, z = me_ref[0], me_ref[1]
        for at in (0, PAD + tokens):
            seq[:, at : at + PAD, :] = jnp.zeros((parts, PAD, block), jnp.float32)
            cot[at : at + PAD, :] = jnp.zeros((PAD, block), jnp.float32)
        for s in range(len(groups)):
            keep, near, far = ins[3 * s : 3 * s + 3]
            to = pl.multiple_of(behind(z, s) * high + PAD, PAD)
            for c in range(parts):
                total = keep[c].astype(jnp.float32) + near[c].astype(jnp.float32)
                total = total + far[c].astype(jnp.float32)
                seq[c, pl.ds(to, high), :] = total.astype(jnp.bfloat16).astype(jnp.float32)
        for i, up in enumerate(up_refs):
            to = pl.multiple_of((row ^ i) * high + PAD, PAD)
            cot[pl.ds(to, high), :] = up[...].astype(jnp.float32)

    operands = [a for group in groups for a in group] + list(ups)
    outs = [
        pltpu.VMEM((parts, tokens + 2 * PAD, block), jnp.float32),
        pltpu.VMEM((tokens + 2 * PAD, block), jnp.float32),
    ]
    return local(me, body, outs, operands, 0.6, late=late)


def gate(me, seq, cot, feature_taps, inner_taps, high, shards, one=None, late=()):
    lags, parts, _ = feature_taps.shape
    long_lags = inner_taps.shape[0]
    block = cot.shape[1]
    window = high + 2 * PAD
    ins = [seq, cot, feature_taps, inner_taps] + ([] if one is None else [one])

    def back(value, lag):
        return pltpu.roll(value, lag, 0) if lag else value

    def ahead(value, lag):
        return pltpu.roll(value, window - lag, 0) if lag else value

    def body(me_ref, seq_ref, cot_ref, taps_ref, long_ref, *refs):
        row, z = me_ref[0], me_ref[1]
        if one is not None:
            one_ref, all_ref, last_ref, two_ref = refs
            all_ref[0] = one_ref[...]

        @pl.loop(0, block // LANES)
        def _(half):
            lanes = pl.ds(pl.multiple_of(half * LANES, LANES), LANES)
            wide = pl.ds(pl.multiple_of(row * block + half * LANES, LANES), LANES)
            taps = [[taps_ref[s, c : c + 1, wide] for c in range(parts)] for s in range(lags)]
            long_taps = [long_ref[s : s + 1, wide] for s in range(long_lags)]
            for s in shards:
                rows = pl.ds(pl.multiple_of(behind(z, s) * high, PAD), window)
                mixed = []
                for c in range(parts):
                    proj = seq_ref[c, rows, lanes]
                    total = taps[0][c] * proj
                    for lag in range(1, lags):
                        total = total + taps[lag][c] * back(proj, lag)
                    mixed.append(total)
                query, key, value = mixed
                upstream = cot_ref[rows, lanes]
                product = (key * value).astype(jnp.bfloat16).astype(jnp.float32)
                inner = long_taps[0] * product
                for lag in range(1, long_lags):
                    inner = inner + long_taps[lag] * back(product, lag)
                grad_inner = upstream * query
                grad_product = long_taps[0] * grad_inner
                for lag in range(1, long_lags):
                    grad_product = grad_product + long_taps[lag] * ahead(grad_inner, lag)
                grads = (upstream * inner, grad_product * value, grad_product * key)
                for c, grad in enumerate(grads):
                    total = taps[0][c] * grad
                    for lag in range(1, lags):
                        total = total + taps[lag][c] * ahead(grad, lag)
                    done = total[PAD : PAD + high].astype(jnp.bfloat16)
                    if one is None:
                        refs[0][c, :, lanes] = done
                        continue
                    all_ref[(s - 1) % 4, c, :, lanes] = done
                    if s == 2:
                        two_ref[c, :, lanes] = done
                    else:
                        last_ref[(s - 3) % 4, c, :, lanes] = done

    single = (parts, high, block)
    outs = [bf16(*single)]
    if one is not None:
        outs = [bf16(4, *single), bf16(2, *single), *outs]
    return local(me, body, outs, ins, 0.8 * len(shards), late=late)


def relay(me, *values, late=()):
    return local(
        me,
        lambda *refs: None,
        [jax.ShapeDtypeStruct(value.shape, value.dtype) for value in values],
        values,
        0.01,
        [ANY] * len(values),
        out_specs=[ANY] * len(values),
        aliases={i: i for i in range(len(values))},
        late=late,
        placed=False,
    )


def input_grads(me, pieces, w, late=()):
    parts, depth, width = w.shape
    high, block = pieces[0][0].shape[-2:]
    shards = len(pieces[0][1])

    def body(me_ref, *refs):
        w_ref, outs, wide = refs[len(pieces)], refs[len(pieces) + 1 : -1], refs[-1]
        for i, (g, (_, which)) in enumerate(zip(refs, pieces)):
            at = pl.multiple_of((me_ref[0] ^ i) * block, LANES)
            for s, index in enumerate(which):
                shard = g if index is None else g.at[index]
                wide[:, s * high : (s + 1) * high, pl.ds(at, block)] = shard[...]
        total = None
        for c in range(parts):
            term = lax.dot_general(
                wide[c], w_ref[c], (((1,), (1,)), ((), ())), preferred_element_type=jnp.float32
            )
            total = term if total is None else total + term
        for s, out in enumerate(outs):
            out[...] = total[s * high : (s + 1) * high].astype(jnp.bfloat16)

    return local(
        me,
        body,
        [bf16(high, depth)] * shards,
        [*(g for g, _ in pieces), w],
        6.0 if shards > 1 else 0.8,
        scratch=[pltpu.VMEM((parts, shards * high, width), jnp.bfloat16)],
        late=late,
    )


def turned(me, xs, late=()):
    high, depth = xs[0].shape

    def body(*refs):
        for s, x in enumerate(refs[:-1]):
            refs[-1][:, s * high : (s + 1) * high] = x[...].T

    me, (out,) = local(me, body, [bf16(depth, high * len(xs))], xs, 0.1 * len(xs), late=late, placed=False)
    return me, out


def weight_grads(me, done, xts, blocks, width, begun=None, final=True):
    depth = xts[0].shape[0]
    flat = [p for _, pieces in blocks for p in pieces]
    parts, high, block = flat[0][0].shape[-3:]
    unique = []
    for g, _ in flat:
        if not any(g is u for u in unique):
            unique.append(g)
    spot = {id(u): n for n, u in enumerate(unique)}
    tokens = high * len(blocks[0][1])
    wide = block * len(blocks)
    cuts, spare = 4, 4
    tall = depth // cuts
    n_in = len(xts) + len(unique) + (begun is not None) + (done is not None)

    def body(me_ref, *refs):
        x_refs, g_refs = refs[: len(xts)], refs[len(xts) : n_in]
        out_ref, xt, gs, *rest = refs[n_in:]
        at = 0
        for x in x_refs:
            xt[:, at : at + x.shape[1]] = x[...]
            at += x.shape[1]
        row = me_ref[0]
        start = pl.multiple_of((row ^ blocks[0][0]) // CORES * wide, wide)
        copies = []
        for c in range(parts):
            for i, pieces in blocks:
                lanes = pl.ds(pl.multiple_of((row ^ i) % CORES * block, LANES), block)
                for k, (g, index) in enumerate(pieces):
                    g_ref = g_refs[spot[id(g)]]
                    shard = g_ref if index is None else g_ref.at[index]
                    gs[c % 2, k * high : (k + 1) * high, lanes] = shard[c]
            for m in range(cuts):
                rows = pl.ds(m * tall, tall)
                part = jnp.dot(xt[rows, :], gs[c % 2], preferred_element_type=jnp.float32)
                if begun is not None:
                    part = part + g_refs[len(unique)][c, rows, :]
                if not final:
                    out_ref[c, rows, :] = part
                    continue
                held, sems = rest
                slot = len(copies) % spare
                if len(copies) >= spare:
                    copies[-spare].wait()
                held[slot] = part
                copies.append(
                    pltpu.make_async_copy(
                        held.at[slot], out_ref.at[c, rows, pl.ds(start, wide)], sems.at[slot]
                    )
                )
                copies[-1].start()
        for copy in copies[-spare:]:
            copy.wait()

    ins = [*xts, *unique] + ([] if begun is None else [begun])
    specs = [VMEM] * len(ins)
    aliases = {}
    if done is not None:
        aliases = {len(ins): 0}
        ins.append(done)
        specs.append(ANY)
    scratch = [
        pltpu.VMEM((depth, tokens), jnp.bfloat16),
        pltpu.VMEM((2, tokens, wide), jnp.bfloat16),
    ]
    out = pltpu.VMEM((parts, depth, wide), jnp.float32)
    if final:
        out = jax.ShapeDtypeStruct((parts, depth, width), jnp.float32)
        scratch += [
            pltpu.VMEM((spare, tall, wide), jnp.float32),
            pltpu.SemaphoreType.DMA((spare,)),
        ]
    me, (out,) = local(
        me,
        body,
        [out],
        ins,
        6.0 if final else 4.0,
        specs,
        scratch=scratch,
        out_specs=[ANY if final else VMEM],
        aliases=aliases,
    )
    return me, out


def total(me, terms, late=()):
    def body(*refs):
        acc = refs[0][...].astype(jnp.float32)
        for ref in refs[1:-1]:
            acc = acc + ref[...].astype(jnp.float32)
        refs[-1][...] = acc.astype(jnp.bfloat16)

    me, (out,) = local(me, body, [bf16(*terms[0].shape)], terms, 0.05, late=late, placed=False)
    return me, out


def by_channels(inputs, weights, feature_taps, inner_taps, grad_out):
    x_own = inputs[0]
    block = weights.shape[2] // lax.axis_size("row")
    width = weights.shape[2]
    me = (jnp.stack([lax.axis_index("row"), lax.axis_index("col")]).astype(jnp.int32),)

    def send(name, value, axis, step):
        with jax.named_scope(name):
            return along(value, step) if axis == "col" else swap(value, axis, step)

    x1 = send("x1", x_own, "col", 1)
    x2 = send("x2", x1, "col", 1)
    x3 = send("x3", x2, "col", 1)
    with jax.named_scope("begin"):
        me, (w, x_own, there, here, across, *away, place) = begin(
            me, x_own, grad_out[0], jnp.transpose(weights, (1, 0, 2)), block
        )
    me = (place, *me[1:])
    def spread(me, name, x, away, turn=(), late=()):
        got = [send(name + "_core%d" % j, away[j], "row", 1) for j in range(2)]
        with jax.named_scope(name + "_keep"):
            me, keep = project(me, [x], w, block, 0)
        with jax.named_scope(name + "_join"):
            me, both = total(me, [keep[1], got[1]], [got[0]])
        groups.append((keep[0], got[0], send(name + "_y", both, "row", CORES)))
        if turn:
            with jax.named_scope(name + "_turned"):
                me, xt = turned(me, turn, late)
            xts.append(xt)
            others.append(send(name + "_xt_x", xt, "dp", 1))
        return me

    groups, xts, others = [], [], []
    me = spread(me, "proj0", x_own, away)
    with jax.named_scope("proj1_away"):
        me, away = project(me, [x1], w, block, 1)
    me = spread(me, "proj1", x1, away, [x_own, x1], [groups[0][2]])
    with jax.named_scope("proj2_away"):
        me, away = project(me, [x2], w, block, 1)
    me = spread(me, "proj2", x2, away, [x2], [groups[1][2]])
    with jax.named_scope("relay_up"):
        me, (there,) = relay(me, there)
    near = send("up_core", there, "row", 1)
    far = send("up_y", jnp.stack([across, near[1]]), "row", CORES)
    ups = [here, near[0], far[0], far[1]]
    with jax.named_scope("proj3_away"):
        me, away = project(me, [x3], w, block, 1)
    me = spread(me, "proj3", x3, away, [x3], [groups[2][2], others[0]])
    with jax.named_scope("laid_out"):
        me, (seq, cot) = laid_out(me, groups, ups)
    high = x_own.shape[0]
    with jax.named_scope("gate1"):
        me, (g1,) = gate(me, seq, cot, feature_taps, inner_taps, high, (1,), late=others[1:2])
    y1 = send("g1_y", g1, "row", CORES)
    c1 = send("g1_core", g1, "row", 1)
    with jax.named_scope("gate230"):
        me, (g, g30, g2) = gate(me, seq, cot, feature_taps, inner_taps, high, (2, 3, 0), g1)
    c2, c30 = send("g2_core", g2, "row", 1), send("g30_core", g30, "row", 1)
    with jax.named_scope("relay_g2"):
        me, (g2,) = relay(me, g2, late=[y1, *others[2:]])
    y2 = send("g2_y", g2, "row", CORES)
    x = send("g_x", g, "dp", 1)
    cy1, cy2 = send("gy1_core", y1, "row", 1), send("gy2_core", y2, "row", 1)
    with jax.named_scope("input_grads1"):
        pieces = [(g, [0]), (c1, [None]), (y1, [None]), (cy1, [None])]
        me, (share1,) = input_grads(me, pieces, w)
    passed = send("share1", share1, "col", 1)
    with jax.named_scope("relay_g30"):
        me, (g30,) = relay(me, g30)
    y30 = send("g30_y", g30, "row", CORES)

    def whole(a):
        return [(a, 3), (a, 0), (a, 1), (a, 2)]

    def cut(last, one, two):
        return [(last, 1), (one, None), (two, None), (last, 0)]

    def halves(low, high):
        return [(high, 1), (low, 0), (low, 1), (high, 0)]

    with jax.named_scope("weight_grads_near_own"):
        blocks = [(0, whole(g)), (1, cut(c30, c1, c2))]
        me, begun = weight_grads(me, None, xts, blocks, width, final=False)
    with jax.named_scope("input_grads2"):
        pieces = [(g, [1]), (c2, [None]), (y2, [None]), (cy2, [None])]
        me, (share2,) = input_grads(me, pieces, w)
    with jax.named_scope("total2"):
        me, share2 = total(me, [share2, passed])
    passed = send("share2", share2, "col", 1)
    with jax.named_scope("relay_x"):
        me, (x,) = relay(me, x)
    xy12, cx = send("gx12_y", x[:2], "row", CORES), send("gx_core", x, "row", 1)
    with jax.named_scope("relay_y30"):
        me, (y30,) = relay(me, y30)
    xy30, cy30 = send("gy30_x", y30, "dp", 1), send("gy30_core", y30, "row", 1)
    with jax.named_scope("input_grads30"):
        pieces = [(g, [2, 3]), (c30, [0, 1]), (y30, [0, 1]), (cy30, [0, 1])]
        me, (share3, share0) = input_grads(me, pieces, w)
    with jax.named_scope("weight_grads_near"):
        blocks = [(0, whole(x)), (1, whole(cx))]
        me, grad_w = weight_grads(me, None, others, blocks, width, begun)
    with jax.named_scope("total3"):
        me, share3 = total(me, [share3, passed])
    passed = send("share3", share3, "col", 1)
    with jax.named_scope("relay_xy"):
        me, (xy12, xy30) = relay(me, xy12, xy30)
    cxy12, cxy30 = send("gxy12_core", xy12, "row", 1), send("gxy30_core", xy30, "row", 1)
    with jax.named_scope("weight_grads_far"):
        blocks = [
            (2, cut(y30, y1, y2) + halves(xy12, xy30)),
            (3, cut(cy30, cy1, cy2) + halves(cxy12, cxy30)),
        ]
        me, grad_w = weight_grads(me, grad_w, xts + others, blocks, width)
    with jax.named_scope("total0"):
        me, grad_in = total(me, [share0, passed])
    return (grad_in[None], jnp.transpose(grad_w, (1, 0, 2)))


def solution(mesh):
    placed = (
        P("dp", "col", "row"),
        P("row", None, "col"),
        P(None, None, "col"),
        P(None, "col"),
        P("dp", "row", "col"),
    )

    def on_device(inputs, weights, feature_taps, inner_taps, grad_out):
        n_row = mesh.shape["row"]
        fits = weights.shape[2] % (n_row * LANES) == 0 and inputs.shape[1] % LANES == 0
        small = n_row == 2 * CORES and mesh.shape["dp"] == 2 and mesh.shape["col"] == 4
        plan = by_channels if fits and small else by_tokens
        return plan(inputs, weights, feature_taps, inner_taps, grad_out)

    return jax.shard_map(
        on_device,
        mesh=mesh,
        in_specs=placed,
        out_specs=(P("dp", "col", "row"), P("row", None, "col")),
        check_vma=False,
    )
```

```python
import math

import jax
import jax.numpy as jnp
from jax import lax
from jax.experimental import pallas as pl
from jax.experimental.pallas import tpu as pltpu
from jax.sharding import PartitionSpec as P

LANES = 128
PAD = 8
CORES = 2


def shifted(shard, axis, by):
    length = lax.axis_size(axis)
    pairs = [(i, i + by) for i in range(length) if 0 <= i + by < length]
    return lax.ppermute(shard, axis, pairs)


def with_halo(cells, axis, width):
    head = shifted(cells[:width], axis, -1)
    tail = shifted(cells[-width:], axis, 1)
    return jnp.concatenate([tail, cells, head], axis=0)


def causal(seq, taps):
    total = taps[0] * seq
    for lag in range(1, taps.shape[0]):
        pad = jnp.zeros((lag,) + seq.shape[1:], jnp.float32)
        total = total + taps[lag] * jnp.concatenate([pad, seq[:-lag]], axis=0)
    return total


def anticausal(seq, taps):
    total = taps[0] * seq
    for lag in range(1, taps.shape[0]):
        pad = jnp.zeros((lag,) + seq.shape[1:], jnp.float32)
        total = total + taps[lag] * jnp.concatenate([seq[lag:], pad], axis=0)
    return total


def rounded(value):
    return lax.optimization_barrier(value.astype(jnp.bfloat16)).astype(jnp.float32)


def by_tokens(inputs, weights, feature_taps, inner_taps, grad_out):
    tile = inputs[0]
    upstream_tile = grad_out[0]
    rows_dev = upstream_tile.shape[0]
    width_row = weights.shape[0]
    width_col = weights.shape[2]
    margin = feature_taps.shape[0] - 1 + (inner_taps.shape[0] - 1)
    flat_w = weights.reshape(width_row, 3 * width_col)
    columns = lax.all_gather(tile, "col", axis=0, tiled=True)
    proj = lax.psum_scatter(
        jnp.dot(columns, flat_w, preferred_element_type=jnp.float32).astype(jnp.bfloat16),
        "row",
        scatter_dimension=0,
        tiled=True,
    )
    length = rows_dev + 2 * margin
    window = with_halo(proj, "row", margin).astype(jnp.float32).reshape(length, 3, width_col)
    after = shifted(upstream_tile[:margin], "row", -1)
    upstream = jnp.concatenate(
        [
            jnp.zeros((margin, width_col), jnp.float32),
            upstream_tile.astype(jnp.float32),
            after.astype(jnp.float32),
        ],
        axis=0,
    )
    mixed = causal(window, feature_taps)
    query = mixed[:, 0]
    key = mixed[:, 1]
    value = mixed[:, 2]
    product = rounded(key * value)
    inner = causal(product, inner_taps)
    grad_query = upstream * inner
    grad_product = anticausal(upstream * query, inner_taps)
    grad_mixed = jnp.stack([grad_query, grad_product * value, grad_product * key], axis=1)
    grad_proj = anticausal(grad_mixed, feature_taps)[margin : margin + rows_dev].astype(
        jnp.bfloat16
    )
    gathered = lax.all_gather(grad_proj.reshape(rows_dev, 3 * width_col), "row", axis=0, tiled=True)
    grad_x = lax.psum_scatter(
        lax.dot_general(
            gathered, flat_w, (((1,), (1,)), ((), ())), preferred_element_type=jnp.float32
        ).astype(jnp.bfloat16),
        "col",
        scatter_dimension=0,
        tiled=True,
    )
    local = lax.dot_general(
        columns, gathered, (((0,), (0,)), ((), ())), preferred_element_type=jnp.float32
    )
    grad_w = lax.psum(local.astype(jnp.bfloat16), "dp").astype(jnp.float32)
    return (grad_x[None], grad_w.reshape(width_row, 3, width_col))


def swap(value, axis, step):
    size = lax.axis_size(axis)
    return lax.ppermute(value, axis, [(i, i ^ step) for i in range(size)])


LINE = (0, 2, 3, 1)


def along(value, steps):
    size = len(LINE)
    pairs = [(LINE[i], LINE[(i + steps) % size]) for i in range(size)]
    return lax.ppermute(value, "col", pairs)


def behind(z, steps):
    for _ in range(steps):
        z = jnp.where(z < 2, 2 * z + 1, 2 * z - 4)
    return z


VMEM = pl.BlockSpec(memory_space=pltpu.VMEM)
SMEM = pl.BlockSpec(memory_space=pltpu.SMEM)
HBM = pl.BlockSpec(memory_space=pltpu.HBM)
ANY = pl.BlockSpec(memory_space=pl.ANY)


PER_MICRO = 1.1e9


def hbm(value):
    return pltpu.with_memory_space_constraint(value, pltpu.HBM)


def bf16(*shape):
    return jax.ShapeDtypeStruct(shape, jnp.bfloat16)


def local(
    me, body, outs, ins, micros, in_specs=None, scratch=(), out_specs=None, aliases=None, late=(), placed=True
):
    place, *turn = me
    first = [place] if placed else []
    late = [*turn, *late]
    n_in = len(first) + len(ins)

    def ordered(*refs):
        body(*refs[:n_in], *refs[n_in + len(late) + 1 :])

    turns = {n_in: 0} if turn else {}
    moved = {len(first) + i: 1 + o for i, o in (aliases or {}).items()}
    turn, *results = pl.pallas_call(
        ordered,
        out_shape=[jax.ShapeDtypeStruct((8, LANES), jnp.float32), *outs],
        in_specs=[SMEM] * len(first) + [*(in_specs or [VMEM] * len(ins)), *[ANY] * len(late)],
        out_specs=[ANY, *(out_specs or [VMEM] * len(outs))],
        scratch_shapes=list(scratch),
        input_output_aliases={**turns, **moved},
        compiler_params=pltpu.CompilerParams(vmem_limit_bytes=16 * 2**20),
        cost_estimate=pl.CostEstimate(
            flops=int(micros * PER_MICRO), bytes_accessed=1, transcendentals=0
        ),
    )(*first, *ins, *late)
    return (place, turn), results


def multiply(x, w_ref, c, block_at, out_ref):
    block = out_ref.shape[-1]
    at = pl.multiple_of(block_at * block, LANES)
    out_ref[c] = jnp.dot(
        x, w_ref[c, :, pl.ds(at, block)], preferred_element_type=jnp.float32
    ).astype(jnp.bfloat16)


def begin(me, x, up, w, block):
    parts, depth, width = w.shape
    high = up.shape[0]

    def body(me_ref, x_hbm, up_hbm, w_hbm, *refs):
        w_ref, x_ref, there_ref, here_ref, across_ref, *away_refs, place_ref, up_ref, sems = refs
        row = me_ref[0]
        place_ref[0] = row
        place_ref[1] = me_ref[1]
        loads = [pltpu.make_async_copy(up_hbm, up_ref, sems.at[0])]
        loads += [pltpu.make_async_copy(x_hbm, x_ref, sems.at[1])]
        loads += [
            pltpu.make_async_copy(w_hbm.at[c], w_ref.at[c], sems.at[2 + c]) for c in range(parts)
        ]
        for load in loads:
            load.start()
        loads[0].wait()
        for j in range(2):
            at = pl.multiple_of((row ^ (2 * j + 1)) * block, LANES)
            there_ref[j] = up_ref[:, pl.ds(at, block)]
        here_ref[...] = up_ref[:, pl.ds(pl.multiple_of(row * block, LANES), block)]
        across_ref[...] = up_ref[:, pl.ds(pl.multiple_of((row ^ 2) * block, LANES), block)]
        loads[1].wait()
        for c in range(parts):
            loads[2 + c].wait()
            for j in range(2):
                multiply(x_ref[...], w_ref, c, row ^ (2 * j + 1), away_refs[j])

    return local(
        me,
        body,
        [
            pltpu.VMEM(w.shape, w.dtype),
            pltpu.VMEM(x.shape, x.dtype),
            bf16(2, high, block),
            bf16(high, block),
            bf16(high, block),
            bf16(parts, high, block),
            bf16(parts, high, block),
            pltpu.SMEM((2,), jnp.int32),
        ],
        [hbm(x), hbm(up), hbm(w)],
        3.5,
        [HBM, HBM, HBM],
        out_specs=[VMEM] * 7 + [SMEM],
        scratch=[
            pltpu.VMEM(up.shape, up.dtype),
            pltpu.SemaphoreType.DMA((2 + parts,)),
        ],
    )


def project(me, xs, w, block, other, late=()):
    parts = w.shape[0]
    tall = xs[0].shape[0] * len(xs)

    def body(me_ref, *refs):
        w_ref, out_refs = refs[len(xs)], refs[len(xs) + 1 :]
        x = jnp.concatenate([x[...] for x in refs[: len(xs)]], axis=0)
        for j in (1, 0):
            for c in range(parts):
                multiply(x, w_ref, c, me_ref[0] ^ (2 * j + other), out_refs[j])

    outs = [bf16(parts, tall, block)] * 2
    return local(me, body, outs, [*xs, w], 2.0 * len(xs), late=late)


def laid_out(me, groups, ups, late=()):
    parts, _, block = groups[0][2].shape
    tokens = sum(far.shape[1] for _, _, far in groups)
    high = ups[0].shape[0]
    n_in = 3 * len(groups)

    def body(me_ref, *refs):
        ins, up_refs, (seq, cot) = refs[:n_in], refs[n_in:-2], refs[-2:]
        row, z = me_ref[0], me_ref[1]
        for at in (0, PAD + tokens):
            seq[:, at : at + PAD, :] = jnp.zeros((parts, PAD, block), jnp.float32)
            cot[at : at + PAD, :] = jnp.zeros((PAD, block), jnp.float32)
        for s in range(len(groups)):
            keep, near, far = ins[3 * s : 3 * s + 3]
            to = pl.multiple_of(behind(z, s) * high + PAD, PAD)
            for c in range(parts):
                total = keep[c].astype(jnp.float32) + near[c].astype(jnp.float32)
                total = total + far[c].astype(jnp.float32)
                seq[c, pl.ds(to, high), :] = total.astype(jnp.bfloat16).astype(jnp.float32)
        for i, up in enumerate(up_refs):
            to = pl.multiple_of((row ^ i) * high + PAD, PAD)
            cot[pl.ds(to, high), :] = up[...].astype(jnp.float32)

    operands = [a for group in groups for a in group] + list(ups)
    outs = [
        pltpu.VMEM((parts, tokens + 2 * PAD, block), jnp.float32),
        pltpu.VMEM((tokens + 2 * PAD, block), jnp.float32),
    ]
    return local(me, body, outs, operands, 0.6, late=late)


def gate(me, seq, cot, feature_taps, inner_taps, high, shards, one=None, late=()):
    lags, parts, _ = feature_taps.shape
    long_lags = inner_taps.shape[0]
    block = cot.shape[1]
    window = high + 2 * PAD
    ins = [seq, cot, feature_taps, inner_taps] + ([] if one is None else [one])

    def back(value, lag):
        return pltpu.roll(value, lag, 0) if lag else value

    def ahead(value, lag):
        return pltpu.roll(value, window - lag, 0) if lag else value

    def body(me_ref, seq_ref, cot_ref, taps_ref, long_ref, *refs):
        row, z = me_ref[0], me_ref[1]
        if one is not None:
            one_ref, all_ref, last_ref, two_ref = refs
            all_ref[0] = one_ref[...]

        @pl.loop(0, block // LANES)
        def _(half):
            lanes = pl.ds(pl.multiple_of(half * LANES, LANES), LANES)
            wide = pl.ds(pl.multiple_of(row * block + half * LANES, LANES), LANES)
            taps = [[taps_ref[s, c : c + 1, wide] for c in range(parts)] for s in range(lags)]
            long_taps = [long_ref[s : s + 1, wide] for s in range(long_lags)]
            for s in shards:
                rows = pl.ds(pl.multiple_of(behind(z, s) * high, PAD), window)
                mixed = []
                for c in range(parts):
                    proj = seq_ref[c, rows, lanes]
                    total = taps[0][c] * proj
                    for lag in range(1, lags):
                        total = total + taps[lag][c] * back(proj, lag)
                    mixed.append(total)
                query, key, value = mixed
                upstream = cot_ref[rows, lanes]
                product = (key * value).astype(jnp.bfloat16).astype(jnp.float32)
                inner = long_taps[0] * product
                for lag in range(1, long_lags):
                    inner = inner + long_taps[lag] * back(product, lag)
                grad_inner = upstream * query
                grad_product = long_taps[0] * grad_inner
                for lag in range(1, long_lags):
                    grad_product = grad_product + long_taps[lag] * ahead(grad_inner, lag)
                grads = (upstream * inner, grad_product * value, grad_product * key)
                for c, grad in enumerate(grads):
                    total = taps[0][c] * grad
                    for lag in range(1, lags):
                        total = total + taps[lag][c] * ahead(grad, lag)
                    done = total[PAD : PAD + high].astype(jnp.bfloat16)
                    if one is None:
                        refs[0][c, :, lanes] = done
                        continue
                    all_ref[(s - 1) % 4, c, :, lanes] = done
                    if s == 2:
                        two_ref[c, :, lanes] = done
                    else:
                        last_ref[(s - 3) % 4, c, :, lanes] = done

    single = (parts, high, block)
    outs = [bf16(*single)]
    if one is not None:
        outs = [bf16(4, *single), bf16(2, *single), *outs]
    return local(me, body, outs, ins, 0.8 * len(shards), late=late)


def relay(me, *values, late=()):
    return local(
        me,
        lambda *refs: None,
        [jax.ShapeDtypeStruct(value.shape, value.dtype) for value in values],
        values,
        0.01,
        [ANY] * len(values),
        out_specs=[ANY] * len(values),
        aliases={i: i for i in range(len(values))},
        late=late,
        placed=False,
    )


def input_grads(me, pieces, w, late=()):
    parts, depth, width = w.shape
    high, block = pieces[0][0].shape[-2:]
    shards = len(pieces[0][1])

    def body(me_ref, *refs):
        w_ref, outs, wide = refs[len(pieces)], refs[len(pieces) + 1 : -1], refs[-1]
        for i, (g, (_, which)) in enumerate(zip(refs, pieces)):
            at = pl.multiple_of((me_ref[0] ^ i) * block, LANES)
            for s, index in enumerate(which):
                shard = g if index is None else g.at[index]
                wide[:, s * high : (s + 1) * high, pl.ds(at, block)] = shard[...]
        total = None
        for c in range(parts):
            term = lax.dot_general(
                wide[c], w_ref[c], (((1,), (1,)), ((), ())), preferred_element_type=jnp.float32
            )
            total = term if total is None else total + term
        for s, out in enumerate(outs):
            out[...] = total[s * high : (s + 1) * high].astype(jnp.bfloat16)

    return local(
        me,
        body,
        [bf16(high, depth)] * shards,
        [*(g for g, _ in pieces), w],
        0.3 if shards > 1 else 0.8,
        scratch=[pltpu.VMEM((parts, shards * high, width), jnp.bfloat16)],
        late=late,
    )


def turned(me, xs, late=()):
    high, depth = xs[0].shape

    def body(*refs):
        for s, x in enumerate(refs[:-1]):
            refs[-1][:, s * high : (s + 1) * high] = x[...].T

    me, (out,) = local(me, body, [bf16(depth, high * len(xs))], xs, 0.1 * len(xs), late=late, placed=False)
    return me, out


def weight_grads(me, done, xts, blocks, width, begun=None, final=True):
    depth = xts[0].shape[0]
    flat = [p for _, pieces in blocks for p in pieces]
    parts, high, block = flat[0][0].shape[-3:]
    unique = []
    for g, _ in flat:
        if not any(g is u for u in unique):
            unique.append(g)
    spot = {id(u): n for n, u in enumerate(unique)}
    tokens = high * len(blocks[0][1])
    wide = block * len(blocks)
    cuts, spare = 4, 4
    tall = depth // cuts
    n_in = len(xts) + len(unique) + (begun is not None) + (done is not None)

    def body(me_ref, *refs):
        x_refs, g_refs = refs[: len(xts)], refs[len(xts) : n_in]
        out_ref, xt, gs, *rest = refs[n_in:]
        at = 0
        for x in x_refs:
            xt[:, at : at + x.shape[1]] = x[...]
            at += x.shape[1]
        row = me_ref[0]
        start = pl.multiple_of((row ^ blocks[0][0]) // CORES * wide, wide)
        copies = []
        for c in range(parts):
            for i, pieces in blocks:
                lanes = pl.ds(pl.multiple_of((row ^ i) % CORES * block, LANES), block)
                for k, (g, index) in enumerate(pieces):
                    g_ref = g_refs[spot[id(g)]]
                    shard = g_ref if index is None else g_ref.at[index]
                    gs[c % 2, k * high : (k + 1) * high, lanes] = shard[c]
            for m in range(cuts):
                rows = pl.ds(m * tall, tall)
                part = jnp.dot(xt[rows, :], gs[c % 2], preferred_element_type=jnp.float32)
                if begun is not None:
                    part = part + g_refs[len(unique)][c, rows, :]
                if not final:
                    out_ref[c, rows, :] = part
                    continue
                held, sems = rest
                slot = len(copies) % spare
                if len(copies) >= spare:
                    copies[-spare].wait()
                held[slot] = part
                copies.append(
                    pltpu.make_async_copy(
                        held.at[slot], out_ref.at[c, rows, pl.ds(start, wide)], sems.at[slot]
                    )
                )
                copies[-1].start()
        for copy in copies[-spare:]:
            copy.wait()

    ins = [*xts, *unique] + ([] if begun is None else [begun])
    specs = [VMEM] * len(ins)
    aliases = {}
    if done is not None:
        aliases = {len(ins): 0}
        ins.append(done)
        specs.append(ANY)
    scratch = [
        pltpu.VMEM((depth, tokens), jnp.bfloat16),
        pltpu.VMEM((2, tokens, wide), jnp.bfloat16),
    ]
    out = pltpu.VMEM((parts, depth, wide), jnp.float32)
    if final:
        out = jax.ShapeDtypeStruct((parts, depth, width), jnp.float32)
        scratch += [
            pltpu.VMEM((spare, tall, wide), jnp.float32),
            pltpu.SemaphoreType.DMA((spare,)),
        ]
    me, (out,) = local(
        me,
        body,
        [out],
        ins,
        (6.0 if done is not None else 0.3) if final else 4.0,
        specs,
        scratch=scratch,
        out_specs=[ANY if final else VMEM],
        aliases=aliases,
    )
    return me, out


def first_half(me, value):
    shape = (value.shape[0] // 2, *value.shape[1:])

    def body(value_ref, out_ref):
        out_ref[...] = value_ref[: shape[0]]

    me, (out,) = local(me, body, [bf16(*shape)], [value], 0.05, placed=False)
    return me, out


def total(me, terms, late=()):
    def body(*refs):
        acc = refs[0][...].astype(jnp.float32)
        for ref in refs[1:-1]:
            acc = acc + ref[...].astype(jnp.float32)
        refs[-1][...] = acc.astype(jnp.bfloat16)

    me, (out,) = local(me, body, [bf16(*terms[0].shape)], terms, 0.05, late=late, placed=False)
    return me, out


def by_channels(inputs, weights, feature_taps, inner_taps, grad_out):
    x_own = inputs[0]
    block = weights.shape[2] // lax.axis_size("row")
    width = weights.shape[2]
    me = (jnp.stack([lax.axis_index("row"), lax.axis_index("col")]).astype(jnp.int32),)

    def send(name, value, axis, step):
        with jax.named_scope(name):
            return along(value, step) if axis == "col" else swap(value, axis, step)

    x1 = send("x1", x_own, "col", 1)
    x2 = send("x2", x1, "col", 1)
    x3 = send("x3", x2, "col", 1)
    with jax.named_scope("begin"):
        me, (w, x_own, there, here, across, *away, place) = begin(
            me, x_own, grad_out[0], jnp.transpose(weights, (1, 0, 2)), block
        )
    me = (place, *me[1:])
    def spread(me, name, x, away, turn=(), late=()):
        got = [send(name + "_core%d" % j, away[j], "row", 1) for j in range(2)]
        with jax.named_scope(name + "_keep"):
            me, keep = project(me, [x], w, block, 0)
        with jax.named_scope(name + "_join"):
            me, both = total(me, [keep[1], got[1]], [got[0]])
        groups.append((keep[0], got[0], send(name + "_y", both, "row", CORES)))
        if turn:
            with jax.named_scope(name + "_turned"):
                me, xt = turned(me, turn, late)
            xts.append(xt)
            others.append(send(name + "_xt_x", xt, "dp", 1))
        return me

    groups, xts, others = [], [], []
    me = spread(me, "proj0", x_own, away)
    with jax.named_scope("proj1_away"):
        me, away = project(me, [x1], w, block, 1)
    me = spread(me, "proj1", x1, away, [x_own, x1], [groups[0][2]])
    with jax.named_scope("proj2_away"):
        me, away = project(me, [x2], w, block, 1)
    me = spread(me, "proj2", x2, away, [x2], [groups[1][2]])
    with jax.named_scope("relay_up"):
        me, (there,) = relay(me, there)
    near = send("up_core", there, "row", 1)
    far = send("up_y", jnp.stack([across, near[1]]), "row", CORES)
    ups = [here, near[0], far[0], far[1]]
    with jax.named_scope("proj3_away"):
        me, away = project(me, [x3], w, block, 1)
    me = spread(me, "proj3", x3, away, [x3], [groups[2][2], others[0]])
    with jax.named_scope("laid_out"):
        me, (seq, cot) = laid_out(me, groups, ups)
    high = x_own.shape[0]
    with jax.named_scope("gate1"):
        me, (g1,) = gate(me, seq, cot, feature_taps, inner_taps, high, (1,), late=others[1:2])
    y1 = send("g1_y", g1, "row", CORES)
    c1 = send("g1_core", g1, "row", 1)
    with jax.named_scope("gate230"):
        me, (g, g30, g2) = gate(me, seq, cot, feature_taps, inner_taps, high, (2, 3, 0), g1)
    c2, c30 = send("g2_core", g2, "row", 1), send("g30_core", g30, "row", 1)
    with jax.named_scope("relay_g2"):
        me, (g2,) = relay(me, g2, late=[y1, *others[2:]])
    y2 = send("g2_y", g2, "row", CORES)
    x = send("g_x", g, "dp", 1)
    cy1, cy2 = send("gy1_core", y1, "row", 1), send("gy2_core", y2, "row", 1)
    with jax.named_scope("input_grads1"):
        pieces = [(g, [0]), (c1, [None]), (y1, [None]), (cy1, [None])]
        me, (share1,) = input_grads(me, pieces, w)
    passed = send("share1", share1, "col", 1)
    with jax.named_scope("relay_g30"):
        me, (g30,) = relay(me, g30)
    y30 = send("g30_y", g30, "row", CORES)

    def whole(a):
        return [(a, 3), (a, 0), (a, 1), (a, 2)]

    def cut(last, one, two):
        return [(last, 1), (one, None), (two, None), (last, 0)]

    def halves(low, high):
        return [(high, 1), (low, 0), (low, 1), (high, 0)]

    with jax.named_scope("weight_grads_near_own"):
        blocks = [(0, whole(g)), (1, cut(c30, c1, c2))]
        me, begun = weight_grads(me, None, xts, blocks, width, final=False)
    with jax.named_scope("input_grads2"):
        pieces = [(g, [1]), (c2, [None]), (y2, [None]), (cy2, [None])]
        me, (share2,) = input_grads(me, pieces, w)
    with jax.named_scope("total2"):
        me, share2 = total(me, [share2, passed])
    passed = send("share2", share2, "col", 1)
    with jax.named_scope("relay_x"):
        me, (x,) = relay(me, x)
    with jax.named_scope("first_half"):
        me, x12 = first_half(me, x)
    xy12, cx = send("gx12_y", x12, "row", CORES), send("gx_core", x, "row", 1)
    with jax.named_scope("relay_y30"):
        me, (y30,) = relay(me, y30)
    xy30, cy30 = send("gy30_x", y30, "dp", 1), send("gy30_core", y30, "row", 1)
    with jax.named_scope("input_grads30"):
        pieces = [(g, [2, 3]), (c30, [0, 1]), (y30, [0, 1]), (cy30, [0, 1])]
        me, (share3, share0) = input_grads(me, pieces, w)
    with jax.named_scope("weight_grads_near"):
        blocks = [(0, whole(x)), (1, whole(cx))]
        me, grad_w = weight_grads(me, None, others, blocks, width, begun)
    with jax.named_scope("total3"):
        me, share3 = total(me, [share3, passed], [xy12])
    passed = send("share3", share3, "col", 1)
    with jax.named_scope("relay_xy"):
        me, (xy12, xy30) = relay(me, xy12, xy30)
    cxy12, cxy30 = send("gxy12_core", xy12, "row", 1), send("gxy30_core", xy30, "row", 1)
    with jax.named_scope("weight_grads_far"):
        blocks = [
            (2, cut(y30, y1, y2) + halves(xy12, xy30)),
            (3, cut(cy30, cy1, cy2) + halves(cxy12, cxy30)),
        ]
        me, grad_w = weight_grads(me, grad_w, xts + others, blocks, width)
    with jax.named_scope("total0"):
        me, grad_in = total(me, [share0, passed])
    return (grad_in[None], jnp.transpose(grad_w, (1, 0, 2)))


def solution(mesh):
    placed = (
        P("dp", "col", "row"),
        P("row", None, "col"),
        P(None, None, "col"),
        P(None, "col"),
        P("dp", "row", "col"),
    )

    def on_device(inputs, weights, feature_taps, inner_taps, grad_out):
        n_row = mesh.shape["row"]
        fits = weights.shape[2] % (n_row * LANES) == 0 and inputs.shape[1] % LANES == 0
        small = n_row == 2 * CORES and mesh.shape["dp"] == 2 and mesh.shape["col"] == 4
        plan = by_channels if fits and small else by_tokens
        return plan(inputs, weights, feature_taps, inner_taps, grad_out)

    return jax.shard_map(
        on_device,
        mesh=mesh,
        in_specs=placed,
        out_specs=(P("dp", "col", "row"), P("row", None, "col")),
        check_vma=False,
    )
```

```python
import math

import jax
import jax.numpy as jnp
from jax import lax
from jax.experimental import pallas as pl
from jax.experimental.pallas import tpu as pltpu
from jax.sharding import PartitionSpec as P

LANES = 128
PAD = 8
CORES = 2


def shifted(shard, axis, by):
    length = lax.axis_size(axis)
    pairs = [(i, i + by) for i in range(length) if 0 <= i + by < length]
    return lax.ppermute(shard, axis, pairs)


def with_halo(cells, axis, width):
    head = shifted(cells[:width], axis, -1)
    tail = shifted(cells[-width:], axis, 1)
    return jnp.concatenate([tail, cells, head], axis=0)


def causal(seq, taps):
    total = taps[0] * seq
    for lag in range(1, taps.shape[0]):
        pad = jnp.zeros((lag,) + seq.shape[1:], jnp.float32)
        total = total + taps[lag] * jnp.concatenate([pad, seq[:-lag]], axis=0)
    return total


def anticausal(seq, taps):
    total = taps[0] * seq
    for lag in range(1, taps.shape[0]):
        pad = jnp.zeros((lag,) + seq.shape[1:], jnp.float32)
        total = total + taps[lag] * jnp.concatenate([seq[lag:], pad], axis=0)
    return total


def rounded(value):
    return lax.optimization_barrier(value.astype(jnp.bfloat16)).astype(jnp.float32)


def by_tokens(inputs, weights, feature_taps, inner_taps, grad_out):
    tile = inputs[0]
    upstream_tile = grad_out[0]
    rows_dev = upstream_tile.shape[0]
    width_row = weights.shape[0]
    width_col = weights.shape[2]
    margin = feature_taps.shape[0] - 1 + (inner_taps.shape[0] - 1)
    flat_w = weights.reshape(width_row, 3 * width_col)
    columns = lax.all_gather(tile, "col", axis=0, tiled=True)
    proj = lax.psum_scatter(
        jnp.dot(columns, flat_w, preferred_element_type=jnp.float32).astype(jnp.bfloat16),
        "row",
        scatter_dimension=0,
        tiled=True,
    )
    length = rows_dev + 2 * margin
    window = with_halo(proj, "row", margin).astype(jnp.float32).reshape(length, 3, width_col)
    after = shifted(upstream_tile[:margin], "row", -1)
    upstream = jnp.concatenate(
        [
            jnp.zeros((margin, width_col), jnp.float32),
            upstream_tile.astype(jnp.float32),
            after.astype(jnp.float32),
        ],
        axis=0,
    )
    mixed = causal(window, feature_taps)
    query = mixed[:, 0]
    key = mixed[:, 1]
    value = mixed[:, 2]
    product = rounded(key * value)
    inner = causal(product, inner_taps)
    grad_query = upstream * inner
    grad_product = anticausal(upstream * query, inner_taps)
    grad_mixed = jnp.stack([grad_query, grad_product * value, grad_product * key], axis=1)
    grad_proj = anticausal(grad_mixed, feature_taps)[margin : margin + rows_dev].astype(
        jnp.bfloat16
    )
    gathered = lax.all_gather(grad_proj.reshape(rows_dev, 3 * width_col), "row", axis=0, tiled=True)
    grad_x = lax.psum_scatter(
        lax.dot_general(
            gathered, flat_w, (((1,), (1,)), ((), ())), preferred_element_type=jnp.float32
        ).astype(jnp.bfloat16),
        "col",
        scatter_dimension=0,
        tiled=True,
    )
    local = lax.dot_general(
        columns, gathered, (((0,), (0,)), ((), ())), preferred_element_type=jnp.float32
    )
    grad_w = lax.psum(local.astype(jnp.bfloat16), "dp").astype(jnp.float32)
    return (grad_x[None], grad_w.reshape(width_row, 3, width_col))


def swap(value, axis, step):
    size = lax.axis_size(axis)
    return lax.ppermute(value, axis, [(i, i ^ step) for i in range(size)])


LINE = (0, 2, 3, 1)


def along(value, steps):
    size = len(LINE)
    pairs = [(LINE[i], LINE[(i + steps) % size]) for i in range(size)]
    return lax.ppermute(value, "col", pairs)


def behind(z, steps):
    for _ in range(steps):
        z = jnp.where(z < 2, 2 * z + 1, 2 * z - 4)
    return z


VMEM = pl.BlockSpec(memory_space=pltpu.VMEM)
SMEM = pl.BlockSpec(memory_space=pltpu.SMEM)
HBM = pl.BlockSpec(memory_space=pltpu.HBM)
ANY = pl.BlockSpec(memory_space=pl.ANY)


PER_MICRO = 1.1e9


def hbm(value):
    return pltpu.with_memory_space_constraint(value, pltpu.HBM)


def bf16(*shape):
    return jax.ShapeDtypeStruct(shape, jnp.bfloat16)


def local(
    me, body, outs, ins, micros, in_specs=None, scratch=(), out_specs=None, aliases=None, late=(), placed=True
):
    place, *turn = me
    first = [place] if placed else []
    late = [*turn, *late]
    n_in = len(first) + len(ins)

    def ordered(*refs):
        body(*refs[:n_in], *refs[n_in + len(late) + 1 :])

    turns = {n_in: 0} if turn else {}
    moved = {len(first) + i: 1 + o for i, o in (aliases or {}).items()}
    turn, *results = pl.pallas_call(
        ordered,
        out_shape=[jax.ShapeDtypeStruct((8, LANES), jnp.float32), *outs],
        in_specs=[SMEM] * len(first) + [*(in_specs or [VMEM] * len(ins)), *[ANY] * len(late)],
        out_specs=[ANY, *(out_specs or [VMEM] * len(outs))],
        scratch_shapes=list(scratch),
        input_output_aliases={**turns, **moved},
        compiler_params=pltpu.CompilerParams(vmem_limit_bytes=16 * 2**20),
        cost_estimate=pl.CostEstimate(
            flops=int(micros * PER_MICRO), bytes_accessed=1, transcendentals=0
        ),
    )(*first, *ins, *late)
    return (place, turn), results


def multiply(x, w_ref, c, block_at, out_ref):
    block = out_ref.shape[-1]
    at = pl.multiple_of(block_at * block, LANES)
    out_ref[c] = jnp.dot(
        x, w_ref[c, :, pl.ds(at, block)], preferred_element_type=jnp.float32
    ).astype(jnp.bfloat16)


def begin(me, x, up, w, block):
    parts, depth, width = w.shape
    high = up.shape[0]

    def body(me_ref, x_hbm, up_hbm, w_hbm, *refs):
        w_ref, x_ref, there_ref, here_ref, across_ref, *away_refs, place_ref, up_ref, sems = refs
        row = me_ref[0]
        place_ref[0] = row
        place_ref[1] = me_ref[1]
        loads = [pltpu.make_async_copy(up_hbm, up_ref, sems.at[0])]
        loads += [pltpu.make_async_copy(x_hbm, x_ref, sems.at[1])]
        loads += [
            pltpu.make_async_copy(w_hbm.at[c], w_ref.at[c], sems.at[2 + c]) for c in range(parts)
        ]
        for load in loads:
            load.start()
        loads[0].wait()
        for j in range(2):
            at = pl.multiple_of((row ^ (2 * j + 1)) * block, LANES)
            there_ref[j] = up_ref[:, pl.ds(at, block)]
        here_ref[...] = up_ref[:, pl.ds(pl.multiple_of(row * block, LANES), block)]
        across_ref[...] = up_ref[:, pl.ds(pl.multiple_of((row ^ 2) * block, LANES), block)]
        loads[1].wait()
        for c in range(parts):
            loads[2 + c].wait()
            for j in range(2):
                multiply(x_ref[...], w_ref, c, row ^ (2 * j + 1), away_refs[j])

    return local(
        me,
        body,
        [
            pltpu.VMEM(w.shape, w.dtype),
            pltpu.VMEM(x.shape, x.dtype),
            bf16(2, high, block),
            bf16(high, block),
            bf16(high, block),
            bf16(parts, high, block),
            bf16(parts, high, block),
            pltpu.SMEM((2,), jnp.int32),
        ],
        [hbm(x), hbm(up), hbm(w)],
        3.5,
        [HBM, HBM, HBM],
        out_specs=[VMEM] * 7 + [SMEM],
        scratch=[
            pltpu.VMEM(up.shape, up.dtype),
            pltpu.SemaphoreType.DMA((2 + parts,)),
        ],
    )


def project(me, xs, w, block, other, late=()):
    parts = w.shape[0]
    tall = xs[0].shape[0] * len(xs)

    def body(me_ref, *refs):
        w_ref, out_refs = refs[len(xs)], refs[len(xs) + 1 :]
        x = jnp.concatenate([x[...] for x in refs[: len(xs)]], axis=0)
        for j in (1, 0):
            for c in range(parts):
                multiply(x, w_ref, c, me_ref[0] ^ (2 * j + other), out_refs[j])

    outs = [bf16(parts, tall, block)] * 2
    return local(me, body, outs, [*xs, w], 2.0 * len(xs), late=late)


def laid_out(me, groups, ups, late=()):
    parts, _, block = groups[0][2].shape
    tokens = sum(far.shape[1] for _, _, far in groups)
    high = ups[0].shape[0]
    n_in = 3 * len(groups)

    def body(me_ref, *refs):
        ins, up_refs, (seq, cot) = refs[:n_in], refs[n_in:-2], refs[-2:]
        row, z = me_ref[0], me_ref[1]
        for at in (0, PAD + tokens):
            seq[:, at : at + PAD, :] = jnp.zeros((parts, PAD, block), jnp.float32)
            cot[at : at + PAD, :] = jnp.zeros((PAD, block), jnp.float32)
        for s in range(len(groups)):
            keep, near, far = ins[3 * s : 3 * s + 3]
            to = pl.multiple_of(behind(z, s) * high + PAD, PAD)
            for c in range(parts):
                total = keep[c].astype(jnp.float32) + near[c].astype(jnp.float32)
                total = total + far[c].astype(jnp.float32)
                seq[c, pl.ds(to, high), :] = total.astype(jnp.bfloat16).astype(jnp.float32)
        for i, up in enumerate(up_refs):
            to = pl.multiple_of((row ^ i) * high + PAD, PAD)
            cot[pl.ds(to, high), :] = up[...].astype(jnp.float32)

    operands = [a for group in groups for a in group] + list(ups)
    outs = [
        pltpu.VMEM((parts, tokens + 2 * PAD, block), jnp.float32),
        pltpu.VMEM((tokens + 2 * PAD, block), jnp.float32),
    ]
    return local(me, body, outs, operands, 0.6, late=late)


def gate(me, seq, cot, feature_taps, inner_taps, high, shards, one=None, late=()):
    lags, parts, _ = feature_taps.shape
    long_lags = inner_taps.shape[0]
    block = cot.shape[1]
    window = high + 2 * PAD
    ins = [seq, cot, feature_taps, inner_taps] + ([] if one is None else [one])

    def back(value, lag):
        return pltpu.roll(value, lag, 0) if lag else value

    def ahead(value, lag):
        return pltpu.roll(value, window - lag, 0) if lag else value

    def body(me_ref, seq_ref, cot_ref, taps_ref, long_ref, *refs):
        row, z = me_ref[0], me_ref[1]
        if one is not None:
            one_ref, all_ref, last_ref, two_ref = refs
            all_ref[0] = one_ref[...]

        @pl.loop(0, block // LANES)
        def _(half):
            lanes = pl.ds(pl.multiple_of(half * LANES, LANES), LANES)
            wide = pl.ds(pl.multiple_of(row * block + half * LANES, LANES), LANES)
            taps = [[taps_ref[s, c : c + 1, wide] for c in range(parts)] for s in range(lags)]
            long_taps = [long_ref[s : s + 1, wide] for s in range(long_lags)]
            for s in shards:
                rows = pl.ds(pl.multiple_of(behind(z, s) * high, PAD), window)
                mixed = []
                for c in range(parts):
                    proj = seq_ref[c, rows, lanes]
                    total = taps[0][c] * proj
                    for lag in range(1, lags):
                        total = total + taps[lag][c] * back(proj, lag)
                    mixed.append(total)
                query, key, value = mixed
                upstream = cot_ref[rows, lanes]
                product = (key * value).astype(jnp.bfloat16).astype(jnp.float32)
                inner = long_taps[0] * product
                for lag in range(1, long_lags):
                    inner = inner + long_taps[lag] * back(product, lag)
                grad_inner = upstream * query
                grad_product = long_taps[0] * grad_inner
                for lag in range(1, long_lags):
                    grad_product = grad_product + long_taps[lag] * ahead(grad_inner, lag)
                grads = (upstream * inner, grad_product * value, grad_product * key)
                for c, grad in enumerate(grads):
                    total = taps[0][c] * grad
                    for lag in range(1, lags):
                        total = total + taps[lag][c] * ahead(grad, lag)
                    done = total[PAD : PAD + high].astype(jnp.bfloat16)
                    if one is None:
                        refs[0][c, :, lanes] = done
                        continue
                    all_ref[(s - 1) % 4, c, :, lanes] = done
                    if s == 2:
                        two_ref[c, :, lanes] = done
                    else:
                        last_ref[(s - 3) % 4, c, :, lanes] = done

    single = (parts, high, block)
    outs = [bf16(*single)]
    if one is not None:
        outs = [bf16(4, *single), bf16(2, *single), *outs]
    return local(me, body, outs, ins, 0.8 * len(shards), late=late)


def relay(me, *values, late=()):
    return local(
        me,
        lambda *refs: None,
        [jax.ShapeDtypeStruct(value.shape, value.dtype) for value in values],
        values,
        0.01,
        [ANY] * len(values),
        out_specs=[ANY] * len(values),
        aliases={i: i for i in range(len(values))},
        late=late,
        placed=False,
    )


def input_grads(me, pieces, w, late=()):
    parts, depth, width = w.shape
    high, block = pieces[0][0].shape[-2:]
    shards = len(pieces[0][1])

    def body(me_ref, *refs):
        w_ref, outs, wide = refs[len(pieces)], refs[len(pieces) + 1 : -1], refs[-1]
        for i, (g, (_, which)) in enumerate(zip(refs, pieces)):
            at = pl.multiple_of((me_ref[0] ^ i) * block, LANES)
            for s, index in enumerate(which):
                shard = g if index is None else g.at[index]
                wide[:, s * high : (s + 1) * high, pl.ds(at, block)] = shard[...]
        total = None
        for c in range(parts):
            term = lax.dot_general(
                wide[c], w_ref[c], (((1,), (1,)), ((), ())), preferred_element_type=jnp.float32
            )
            total = term if total is None else total + term
        for s, out in enumerate(outs):
            out[...] = total[s * high : (s + 1) * high].astype(jnp.bfloat16)

    return local(
        me,
        body,
        [bf16(high, depth)] * shards,
        [*(g for g, _ in pieces), w],
        0.3 if shards > 1 else 0.8,
        scratch=[pltpu.VMEM((parts, shards * high, width), jnp.bfloat16)],
        late=late,
    )


def turned(me, xs, late=()):
    high, depth = xs[0].shape

    def body(*refs):
        for s, x in enumerate(refs[:-1]):
            refs[-1][:, s * high : (s + 1) * high] = x[...].T

    me, (out,) = local(me, body, [bf16(depth, high * len(xs))], xs, 0.1 * len(xs), late=late, placed=False)
    return me, out


def weight_grads(me, done, xts, blocks, width, begun=None, final=True, micros=4.0):
    cols = [x[1] if isinstance(x, tuple) else (0, x.shape[1]) for x in xts]
    xts = [x[0] if isinstance(x, tuple) else x for x in xts]
    depth = xts[0].shape[0]
    flat = [p for _, pieces in blocks for p in pieces]
    parts, high, block = flat[0][0].shape[-3:]
    unique = []
    for g, _ in flat:
        if not any(g is u for u in unique):
            unique.append(g)
    spot = {id(u): n for n, u in enumerate(unique)}
    tokens = high * len(blocks[0][1])
    wide = block * len(blocks)
    cuts, spare = 4, 4
    tall = depth // cuts
    n_in = len(xts) + len(unique) + (begun is not None) + (done is not None)

    def body(me_ref, *refs):
        x_refs, g_refs = refs[: len(xts)], refs[len(xts) : n_in]
        out_ref, xt, gs, *rest = refs[n_in:]
        at = 0
        for x, (low, end) in zip(x_refs, cols):
            xt[:, at : at + end - low] = x[:, low:end]
            at += end - low
        row = me_ref[0]
        start = pl.multiple_of((row ^ blocks[0][0]) // CORES * wide, wide)
        copies = []
        for c in range(parts):
            for i, pieces in blocks:
                lanes = pl.ds(pl.multiple_of((row ^ i) % CORES * block, LANES), block)
                for k, (g, index) in enumerate(pieces):
                    g_ref = g_refs[spot[id(g)]]
                    shard = g_ref if index is None else g_ref.at[index]
                    gs[c % 2, k * high : (k + 1) * high, lanes] = shard[c]
            for m in range(cuts):
                rows = pl.ds(m * tall, tall)
                part = jnp.dot(xt[rows, :], gs[c % 2], preferred_element_type=jnp.float32)
                if begun is not None:
                    part = part + g_refs[len(unique)][c, rows, :]
                if not final:
                    out_ref[c, rows, :] = part
                    continue
                held, sems = rest
                slot = len(copies) % spare
                if len(copies) >= spare:
                    copies[-spare].wait()
                held[slot] = part
                copies.append(
                    pltpu.make_async_copy(
                        held.at[slot], out_ref.at[c, rows, pl.ds(start, wide)], sems.at[slot]
                    )
                )
                copies[-1].start()
        for copy in copies[-spare:]:
            copy.wait()

    ins = [*xts, *unique] + ([] if begun is None else [begun])
    specs = [VMEM] * len(ins)
    aliases = {}
    if done is not None:
        aliases = {len(ins): 0}
        ins.append(done)
        specs.append(ANY)
    scratch = [
        pltpu.VMEM((depth, tokens), jnp.bfloat16),
        pltpu.VMEM((2, tokens, wide), jnp.bfloat16),
    ]
    out = pltpu.VMEM((parts, depth, wide), jnp.float32)
    if final:
        out = jax.ShapeDtypeStruct((parts, depth, width), jnp.float32)
        scratch += [
            pltpu.VMEM((spare, tall, wide), jnp.float32),
            pltpu.SemaphoreType.DMA((spare,)),
        ]
    me, (out,) = local(
        me,
        body,
        [out],
        ins,
        (6.0 if done is not None else 0.3) if final else micros,
        specs,
        scratch=scratch,
        out_specs=[ANY if final else VMEM],
        aliases=aliases,
    )
    return me, out


def first_half(me, value):
    shape = (value.shape[0] // 2, *value.shape[1:])

    def body(value_ref, out_ref):
        out_ref[...] = value_ref[: shape[0]]

    me, (out,) = local(me, body, [bf16(*shape)], [value], 0.05, placed=False)
    return me, out


def total(me, terms, late=()):
    def body(*refs):
        acc = refs[0][...].astype(jnp.float32)
        for ref in refs[1:-1]:
            acc = acc + ref[...].astype(jnp.float32)
        refs[-1][...] = acc.astype(jnp.bfloat16)

    me, (out,) = local(me, body, [bf16(*terms[0].shape)], terms, 0.05, late=late, placed=False)
    return me, out


def by_channels(inputs, weights, feature_taps, inner_taps, grad_out):
    x_own = inputs[0]
    block = weights.shape[2] // lax.axis_size("row")
    width = weights.shape[2]
    me = (jnp.stack([lax.axis_index("row"), lax.axis_index("col")]).astype(jnp.int32),)

    def send(name, value, axis, step):
        with jax.named_scope(name):
            return along(value, step) if axis == "col" else swap(value, axis, step)

    x1 = send("x1", x_own, "col", 1)
    x2 = send("x2", x1, "col", 1)
    x3 = send("x3", x2, "col", 1)
    with jax.named_scope("begin"):
        me, (w, x_own, there, here, across, *away, place) = begin(
            me, x_own, grad_out[0], jnp.transpose(weights, (1, 0, 2)), block
        )
    me = (place, *me[1:])
    def spread(me, name, x, away, turn=(), late=()):
        got = [send(name + "_core%d" % j, away[j], "row", 1) for j in range(2)]
        with jax.named_scope(name + "_keep"):
            me, keep = project(me, [x], w, block, 0)
        with jax.named_scope(name + "_join"):
            me, both = total(me, [keep[1], got[1]], [got[0]])
        groups.append((keep[0], got[0], send(name + "_y", both, "row", CORES)))
        if turn:
            with jax.named_scope(name + "_turned"):
                me, xt = turned(me, turn, late)
            xts.append(xt)
            others.append(send(name + "_xt_x", xt, "dp", 1))
        return me

    groups, xts, others = [], [], []
    me = spread(me, "proj0", x_own, away)
    with jax.named_scope("proj1_away"):
        me, away = project(me, [x1], w, block, 1)
    me = spread(me, "proj1", x1, away, [x_own, x1], [groups[0][2]])
    with jax.named_scope("proj2_away"):
        me, away = project(me, [x2], w, block, 1)
    me = spread(me, "proj2", x2, away, [x2], [groups[1][2]])
    with jax.named_scope("relay_up"):
        me, (there,) = relay(me, there)
    near = send("up_core", there, "row", 1)
    far = send("up_y", jnp.stack([across, near[1]]), "row", CORES)
    ups = [here, near[0], far[0], far[1]]
    with jax.named_scope("proj3_away"):
        me, away = project(me, [x3], w, block, 1)
    me = spread(me, "proj3", x3, away, [x3], [groups[2][2], others[0]])
    with jax.named_scope("laid_out"):
        me, (seq, cot) = laid_out(me, groups, ups)
    high = x_own.shape[0]
    with jax.named_scope("gate1"):
        me, (g1,) = gate(me, seq, cot, feature_taps, inner_taps, high, (1,), late=others[1:2])
    y1 = send("g1_y", g1, "row", CORES)
    c1 = send("g1_core", g1, "row", 1)
    with jax.named_scope("gate230"):
        me, (g, g30, g2) = gate(me, seq, cot, feature_taps, inner_taps, high, (2, 3, 0), g1)
    c2, c30 = send("g2_core", g2, "row", 1), send("g30_core", g30, "row", 1)
    with jax.named_scope("relay_g2"):
        me, (g2,) = relay(me, g2, late=[y1, *others[2:]])
    y2 = send("g2_y", g2, "row", CORES)
    x = send("g_x", g, "dp", 1)
    cy1, cy2 = send("gy1_core", y1, "row", 1), send("gy2_core", y2, "row", 1)
    with jax.named_scope("input_grads1"):
        pieces = [(g, [0]), (c1, [None]), (y1, [None]), (cy1, [None])]
        me, (share1,) = input_grads(me, pieces, w)
    passed = send("share1", share1, "col", 1)
    with jax.named_scope("relay_g30"):
        me, (g30,) = relay(me, g30)
    y30 = send("g30_y", g30, "row", CORES)

    def whole(a):
        return [(a, 3), (a, 0), (a, 1), (a, 2)]

    def cut(last, one, two):
        return [(last, 1), (one, None), (two, None), (last, 0)]

    def halves(low, high):
        return [(high, 1), (low, 0), (low, 1), (high, 0)]

    with jax.named_scope("weight_grads_near_own"):
        blocks = [(0, whole(g)), (1, cut(c30, c1, c2))]
        me, begun = weight_grads(me, None, xts, blocks, width, final=False)
    with jax.named_scope("input_grads2"):
        pieces = [(g, [1]), (c2, [None]), (y2, [None]), (cy2, [None])]
        me, (share2,) = input_grads(me, pieces, w)
    with jax.named_scope("total2"):
        me, share2 = total(me, [share2, passed])
    passed = send("share2", share2, "col", 1)
    far_own = [(2, [(y1, None), (y2, None)]), (3, [(cy1, None), (cy2, None)])]
    with jax.named_scope("weight_grads_far_own"):
        some = [(xts[0], (high, 2 * high)), xts[1]]
        me, far_begun = weight_grads(me, None, some, far_own, width, final=False, micros=0.05)
    with jax.named_scope("relay_x"):
        me, (x,) = relay(me, x)
    with jax.named_scope("first_half"):
        me, x12 = first_half(me, x)
    xy12, cx = send("gx12_y", x12, "row", CORES), send("gx_core", x, "row", 1)
    with jax.named_scope("relay_y30"):
        me, (y30,) = relay(me, y30)
    xy30, cy30 = send("gy30_x", y30, "dp", 1), send("gy30_core", y30, "row", 1)
    with jax.named_scope("input_grads30"):
        pieces = [(g, [2, 3]), (c30, [0, 1]), (y30, [0, 1]), (cy30, [0, 1])]
        me, (share3, share0) = input_grads(me, pieces, w)
    with jax.named_scope("weight_grads_near"):
        blocks = [(0, whole(x)), (1, whole(cx))]
        me, grad_w = weight_grads(me, None, others, blocks, width, begun)
    with jax.named_scope("total3"):
        me, share3 = total(me, [share3, passed], [xy12])
    passed = send("share3", share3, "col", 1)
    with jax.named_scope("relay_xy"):
        me, (xy12, xy30) = relay(me, xy12, xy30)
    cxy12, cxy30 = send("gxy12_core", xy12, "row", 1), send("gxy30_core", xy30, "row", 1)
    with jax.named_scope("weight_grads_far"):
        blocks = [
            (2, [(y30, 1), (y30, 0)] + halves(xy12, xy30)),
            (3, [(cy30, 1), (cy30, 0)] + halves(cxy12, cxy30)),
        ]
        me, grad_w = weight_grads(
            me, grad_w, [(xts[0], (0, high)), xts[2], *others], blocks, width, far_begun
        )
    with jax.named_scope("total0"):
        me, grad_in = total(me, [share0, passed])
    return (grad_in[None], jnp.transpose(grad_w, (1, 0, 2)))


def solution(mesh):
    placed = (
        P("dp", "col", "row"),
        P("row", None, "col"),
        P(None, None, "col"),
        P(None, "col"),
        P("dp", "row", "col"),
    )

    def on_device(inputs, weights, feature_taps, inner_taps, grad_out):
        n_row = mesh.shape["row"]
        fits = weights.shape[2] % (n_row * LANES) == 0 and inputs.shape[1] % LANES == 0
        small = n_row == 2 * CORES and mesh.shape["dp"] == 2 and mesh.shape["col"] == 4
        plan = by_channels if fits and small else by_tokens
        return plan(inputs, weights, feature_taps, inner_taps, grad_out)

    return jax.shard_map(
        on_device,
        mesh=mesh,
        in_specs=placed,
        out_specs=(P("dp", "col", "row"), P("row", None, "col")),
        check_vma=False,
    )
```
